32 devices in a mesh: dp: 16 (over z, y, core), tensor: 2 (over x).
Axes of the slice: x: 2, y: 2, z: 4, core: 2. Of those that a mesh axis runs over, the one named last changes fastest.
Arguments:
- inputs: bfloat16 [73728, 512], P(('dp', 'tensor')), may hold values from -3 to 3
- pack_long: int32 [192], P('dp'), may hold values from 0 to 1
- item_table: int32 [768], P('dp'), may hold values from 0 to 63
- tau_table: float32 [64], replicated, may hold values from 0.5 to 2
- delta_table: float32 [64, 384], replicated, may hold values from -6 to 6
- project_weight: bfloat16 [3, 512, 512], P(None, None, 'tensor'), may hold values from -0.25 to 0.25
- project_bias: float32 [2, 512], P(None, 'tensor'), may hold values from -1.5 to 1.5
- merge_weight: bfloat16 [512, 512], P('tensor'), may hold values from -1 to 1
- merge_bias: float32 [512], replicated, may hold values from -1.5 to 1.5
- first_gain: float32 [512], replicated, may hold values from 0.5 to 1.5
- first_shift: float32 [512], replicated, may hold values from -1 to 1
- expand_weight: bfloat16 [512, 2048], P(None, 'tensor'), may hold values from -0.25 to 0.25
- expand_bias: float32 [2048], P('tensor'), may hold values from -1.5 to 1.5
- reduce_weight: bfloat16 [2048, 512], P('tensor'), may hold values from -0.25 to 0.25
- reduce_bias: float32 [512], replicated, may hold values from -1.5 to 1.5
- second_gain: float32 [512], replicated, may hold values from 0.5 to 1.5
- second_shift: float32 [512], replicated, may hold values from -1 to 1
- grad_output: bfloat16 [73728, 512], P(('dp', 'tensor')), may hold values from -3 to 3
Outputs:
- block_output: float32 [73728, 512], P(('dp', 'tensor'))
- input_grad: float32 [73728, 512], P(('dp', 'tensor'))
- project_weight_grad: float32 [3, 512, 512], P(None, None, 'tensor')
- project_bias_grad: float32 [2, 512], P(None, 'tensor')
- merge_weight_grad: float32 [512, 512], P('tensor')
- merge_bias_grad: float32 [512], replicated
- first_gain_grad: float32 [512], replicated
- first_shift_grad: float32 [512], replicated
- expand_weight_grad: float32 [512, 2048], P(None, 'tensor')
- expand_bias_grad: float32 [2048], P('tensor')
- reduce_weight_grad: float32 [2048, 512], P('tensor')
- reduce_bias_grad: float32 [512], replicated
- second_gain_grad: float32 [512], replicated
- second_shift_grad: float32 [512], replicated
The draws below stay inside these ranges and needn't reach their ends.
All inputs are finite; a program needn't handle non-finite values.
Results may differ from the reference program's by a relative error of at most 0.02.
The reference program's roundings to bfloat16 on the way count: a program that leaves them out, or rounds other values in their place, can miss the bound.
Values may be sent and summed in bfloat16 or wider, within the bound.
No kernel may reach another device: no remote copies, remote signals or barrier semaphores. Data moves between devices by JAX's collectives and lax.ppermute only.
A program may use at most 192 MiB of HBM per device.

```python
import math
import jax
import jax.numpy as jnp
from jax import lax

D = 512
HEADS = 8
HEAD = 64
FF = 2048
SHORT = 96
LONG = 384
TABLE = 64
PACKS = 12
SLOTS_DEV = 48
TOKENS = 73728
N_DP = 16


def place_ends(values, key, low, largest):
    place = [jax.random.randint(jax.random.fold_in(key, axis), (), 0, length) for axis, length in enumerate(values.shape)]
    widest = values.shape.index(max(values.shape))
    beside = place[:widest] + [(place[widest] + 1) % values.shape[widest]] + place[widest + 1:]
    return values.at[tuple(place)].set(low).at[tuple(beside)].set(largest)


def levels(rng, shape, split, low, high):
    factor_of, own = 1.0, jax.random.fold_in(rng, 6)
    for dim, blocks in split:
        steps = jnp.exp(jax.random.uniform(jax.random.fold_in(own, dim), (blocks,), jnp.float32, low / len(split), high / len(split)))
        factor_of = factor_of * jnp.repeat(steps, shape[dim] // blocks).reshape([-1 if axis == dim else 1 for axis in range(len(shape))])
    return factor_of


def gaussian(own_key, shape, scale, reach, pieces=(), held_as=jnp.bfloat16):
    loudness = levels(own_key, shape, pieces, -0.22, 0.18) if pieces else 1.0
    drawn = jax.random.normal(own_key, shape, jnp.float32) * scale * loudness
    return jnp.minimum(jnp.maximum(drawn, -reach), reach).astype(held_as)


def setup_inputs(seed: int = 0) -> dict:
    key_of = jax.random.split(jax.random.key(seed), 19)
    return {
        "inputs": gaussian(key_of[0], (TOKENS, D), 1.0, 3.0, ((0, 32),)),
        "pack_long": place_ends(jax.random.randint(key_of[1], (N_DP * PACKS,), 0, 2), jax.random.fold_in(key_of[1], 1), 0, 1).astype(jnp.int32),
        "item_table": place_ends(jax.random.randint(key_of[2], (N_DP * SLOTS_DEV,), 0, TABLE), jax.random.fold_in(key_of[2], 1), 0, TABLE - 1).astype(jnp.int32),
        "tau_table": jnp.clip(jnp.exp(jax.random.uniform(key_of[3], (TABLE,), jnp.float32, math.log(0.5), math.log(2.0))), 0.5, 2.0),
        "delta_table": gaussian(key_of[4], (TABLE, LONG), 2.0, 6.0, (), jnp.float32),
        "project_weight": gaussian(key_of[5], (3, D, D), D ** -0.5, 0.25, ((2, 2),)),
        "project_bias": gaussian(key_of[6], (2, D), 0.3, 1.5, ((1, 2),), jnp.float32),
        "merge_weight": gaussian(key_of[7], (D, D), (D // 16) ** -0.5, 1.0, ((0, 2),)),
        "merge_bias": gaussian(key_of[8], (D,), 0.3, 1.5, (), jnp.float32),
        "first_gain": jnp.clip(1.0 + 0.1 * jax.random.normal(key_of[9], (D,), jnp.float32), 0.5, 1.5),
        "first_shift": gaussian(key_of[10], (D,), 0.2, 1.0, (), jnp.float32),
        "expand_weight": gaussian(key_of[11], (D, FF), D ** -0.5, 0.25, ((1, 2),)),
        "expand_bias": gaussian(key_of[12], (FF,), 0.3, 1.5, ((0, 2),), jnp.float32),
        "reduce_weight": gaussian(key_of[13], (FF, D), (FF // 4) ** -0.5, 0.25, ((0, 2),)),
        "reduce_bias": gaussian(key_of[14], (D,), 0.3, 1.5, (), jnp.float32),
        "second_gain": jnp.clip(1.0 + 0.1 * jax.random.normal(key_of[15], (D,), jnp.float32), 0.5, 1.5),
        "second_shift": gaussian(key_of[16], (D,), 0.2, 1.0, (), jnp.float32),
        "grad_output": gaussian(key_of[17], (TOKENS, D), 1.0, 3.0, ((0, 32),)),
    }


@jax.custom_vjp
def low(v):
    return lax.optimization_barrier(v.astype(jnp.bfloat16)).astype(jnp.float32)

@jax.custom_vjp
def low_back(v):
    return v

def low_keep(v):
    return (low(v), None)

def low_pass(kept, grad):
    return (grad,)

def back_keep(v):
    return (v, None)

def back_low(kept, grad):
    return (low(grad),)
low.defvjp(low_keep, low_pass)
low_back.defvjp(back_keep, back_low)

def product(left, right):
    return jnp.dot(left, right, precision=lax.Precision.HIGHEST, preferred_element_type=jnp.float32)

def layer_norm(values, gain, shift):
    mean = lax.optimization_barrier(jnp.mean(values, axis=-1, keepdims=True))
    centred = values - mean
    spread = lax.optimization_barrier(jnp.mean(centred * centred, axis=-1, keepdims=True))
    return centred * lax.rsqrt(spread + 1e-05) * gain + shift

def attend(query, keys, values, tau_row, delta_row, segment):
    width = 2 * LONG
    blocks = query.shape[0] // width
    scale = HEAD ** (-0.5)

    def one_block(parts):
        block_q, block_k, block_v, block_tau, block_delta, block_seg = parts
        heads_q = block_q.reshape(width, HEADS, HEAD)
        heads_k = block_k.reshape(width, HEADS, HEAD)
        heads_v = block_v.reshape(width, HEADS, HEAD)
        raw = low_back(jnp.einsum('qhd,khd->hqk', heads_q, heads_k, precision=lax.Precision.HIGHEST))
        scores = (block_tau[None, :, None] * raw + block_delta[None, None, :]) * scale
        same = block_seg[:, None] == block_seg[None, :]
        scores = jnp.where(same[None], scores, -1e+30)
        weights = low(jax.nn.softmax(scores, axis=-1))
        mixed = jnp.einsum('hqk,khd->qhd', weights, heads_v, precision=lax.Precision.HIGHEST)
        return mixed.reshape(width, HEADS * HEAD)
    parts = (query.reshape(blocks, width, -1), keys.reshape(blocks, width, -1), values.reshape(blocks, width, -1), tau_row.reshape(blocks, width), delta_row.reshape(blocks, width), segment.reshape(blocks, width))
    return lax.map(jax.checkpoint(one_block), parts).reshape(query.shape[0], HEADS * HEAD)

def reference(inputs, pack_long, item_table, tau_table, delta_table, project_weight, project_bias, merge_weight, merge_bias, first_gain, first_shift, expand_weight, expand_bias, reduce_weight, reduce_bias, second_gain, second_shift, grad_output):
    total = inputs.shape[0]
    per = LONG // SHORT
    places = jnp.arange(total, dtype=jnp.int32)
    pack = (places // LONG).astype(jnp.int32)
    lead = (pack * per).astype(jnp.int32)
    slot = (places // SHORT).astype(jnp.int32)
    longer = pack_long[pack] == 1
    table_row = jnp.where(longer, item_table[lead], item_table[slot]).astype(jnp.int32)
    position = jnp.where(longer, places % LONG, places % SHORT).astype(jnp.int32)
    segment = jnp.where(longer, lead, slot).astype(jnp.int32)
    tau_row = tau_table[table_row].astype(jnp.float32)
    delta_row = delta_table[table_row, position].astype(jnp.float32)

    def forward(source, weight_qkv, bias_qv, weight_merge, bias_merge, gain_a, shift_a, weight_expand, bias_expand, weight_reduce, bias_reduce, gain_b, shift_b):
        query = low_back(low(product(source, weight_qkv[0]) + bias_qv[0]))
        keys = low_back(low(product(source, weight_qkv[1])))
        values = low_back(low(product(source, weight_qkv[2]) + bias_qv[1]))
        attended = low_back(low(attend(query, keys, values, tau_row, delta_row, segment)))
        mixed = low_back(product(attended, weight_merge)) + bias_merge
        normed = layer_norm(source + mixed, gain_a, shift_a)
        preact = low_back(product(low(normed), weight_expand) + bias_expand)
        active = low(jax.nn.gelu(preact, approximate=False))
        fed = low_back(product(active, weight_reduce)) + bias_reduce
        return layer_norm(normed + fed, gain_b, shift_b)
    params = tuple((p.astype(jnp.float32) for p in (project_weight, project_bias, merge_weight, merge_bias, first_gain, first_shift, expand_weight, expand_bias, reduce_weight, reduce_bias, second_gain, second_shift)))
    output, pullback = jax.vjp(forward, inputs.astype(jnp.float32), *params)
    grads = pullback(grad_output.astype(jnp.float32))
    return (output, grads[0], grads[1], grads[2], grads[3], grads[4], grads[5], grads[6], grads[7], grads[8], grads[9], grads[10], grads[11], grads[12])
```

```python
import functools
import jax
import jax.numpy as jnp
from jax import lax
from jax.experimental import pallas as pl
from jax.experimental.pallas import tpu as pltpu
from jax.sharding import PartitionSpec as P

HEAD = 64
SHORT = 96
LONG = 384
TABLE = 64
PAIR = 2 * HEAD
LOG2E = 1.4426950408889634
F32 = jnp.float32
BF16 = jnp.bfloat16


def layer_norm(values, gain, shift):
    mean = jnp.mean(values, axis=-1, keepdims=True)
    centred = values - mean
    spread = jnp.mean(centred * centred, axis=-1, keepdims=True)
    return centred * lax.rsqrt(spread + 1e-05) * gain + shift


def exact_gelu(values):
    return jax.nn.gelu(values, approximate=False)


def describe(pack_long, item_table, tau_table, delta_table):
    packs = pack_long.shape[0]
    per = LONG // SHORT
    count = packs * LONG
    longer = jnp.broadcast_to(pack_long[:, None] == 1, (packs, LONG)).reshape(count)
    lead_row = jnp.broadcast_to(item_table.reshape(packs, per)[:, :1], (packs, LONG)).reshape(count)
    each_row = jnp.broadcast_to(item_table[:, None], (packs * per, SHORT)).reshape(count)
    table_row = jnp.where(longer, lead_row, each_row)
    places = jnp.arange(count, dtype=jnp.int32)
    position = jnp.where(longer, places % LONG, places % SHORT)
    segment = jnp.where(longer, places // LONG * per, places // SHORT)
    picker = (table_row[:, None] == jnp.arange(TABLE, dtype=jnp.int32)[None, :]).astype(jnp.float32)
    tau_row = jnp.sum(picker * tau_table[None, :], axis=1)
    picked = jnp.dot(
        picker, delta_table, precision=lax.Precision.HIGHEST, preferred_element_type=jnp.float32
    )
    placed = position[:, None] == jnp.arange(LONG, dtype=jnp.int32)[None, :]
    delta_row = jnp.sum(jnp.where(placed, picked, 0.0), axis=1)
    return (tau_row, delta_row, segment)


def project(rows_all, project_weight, project_bias):
    query = (
        jnp.dot(rows_all, project_weight[0], preferred_element_type=jnp.float32) + project_bias[0]
    ).astype(jnp.bfloat16)
    keys = jnp.dot(rows_all, project_weight[1], preferred_element_type=jnp.float32).astype(
        jnp.bfloat16
    )
    values = (
        jnp.dot(rows_all, project_weight[2], preferred_element_type=jnp.float32) + project_bias[1]
    ).astype(jnp.bfloat16)
    return (query, keys, values)


def split_blocks(arrays):
    width = 2 * LONG
    return tuple((a.reshape((a.shape[0] // width, width) + a.shape[1:]) for a in arrays))


def block_scores(block_q, block_k, block_tau, block_delta, block_seg):
    raw = jnp.einsum("qhd,khd->hqk", block_q, block_k, preferred_element_type=jnp.float32)
    scores = (block_tau[None, :, None] * raw + block_delta[None, None, :]) * HEAD ** (-0.5)
    same = block_seg[:, None] == block_seg[None, :]
    return jnp.where(same[None], scores, -1e30)


def attend_forward(query, keys, values, tau_row, delta_row, segment):
    heads = query.shape[1] // HEAD
    shaped = tuple((a.reshape(a.shape[0], heads, HEAD) for a in (query, keys, values)))

    def one_block(parts):
        block_q, block_k, block_v, block_tau, block_delta, block_seg = parts
        scores = block_scores(block_q, block_k, block_tau, block_delta, block_seg)
        top = jnp.max(scores, axis=-1, keepdims=True)
        expo = jnp.exp(scores - top)
        totals = jnp.sum(expo, axis=-1, keepdims=True)
        weights = (expo / totals).astype(jnp.bfloat16)
        mixed = jnp.einsum("hqk,khd->qhd", weights, block_v, preferred_element_type=jnp.float32)
        return (
            mixed.reshape(mixed.shape[0], heads * HEAD).astype(jnp.bfloat16),
            top + jnp.log(totals),
        )

    attended, logsum = lax.map(one_block, split_blocks(shaped + (tau_row, delta_row, segment)))
    return (attended.reshape(query.shape), logsum)


def attend_backward(query, keys, values, grad_att, logsum, tau_row, delta_row, segment):
    heads = query.shape[1] // HEAD
    shaped = tuple((a.reshape(a.shape[0], heads, HEAD) for a in (query, keys, values, grad_att)))
    blocked = split_blocks(shaped + (tau_row, delta_row, segment))

    def one_block(parts):
        block_q, block_k, block_v, block_g, block_lse, block_tau, block_delta, block_seg = parts
        scores = block_scores(block_q, block_k, block_tau, block_delta, block_seg)
        probs = jnp.exp(scores - block_lse)
        dprob = jnp.einsum("qhd,khd->hqk", block_g, block_v, preferred_element_type=jnp.float32)
        dscore = probs * (dprob - jnp.sum(dprob * probs, axis=-1, keepdims=True))
        lowered = (dscore * HEAD ** (-0.5) * block_tau[None, :, None]).astype(jnp.bfloat16)
        grad_q = jnp.einsum("hqk,khd->qhd", lowered, block_k, preferred_element_type=jnp.float32)
        grad_k = jnp.einsum("hqk,qhd->khd", lowered, block_q, preferred_element_type=jnp.float32)
        grad_v = jnp.einsum(
            "hqk,qhd->khd", probs.astype(jnp.bfloat16), block_g, preferred_element_type=jnp.float32
        )
        width = block_q.shape[0]
        return tuple(
            (g.reshape(width, heads * HEAD).astype(jnp.bfloat16) for g in (grad_q, grad_k, grad_v))
        )

    grads = lax.map(one_block, blocked[:4] + (logsum,) + blocked[4:])
    return tuple((g.reshape(query.shape) for g in grads))


def row_term(left, right, form):
    return jnp.einsum(form, left, right, preferred_element_type=jnp.float32)


def feed_backward(feed_rows, preact_rows, active_rows, grad_fed, reduce_matrix):
    grad_reduce_weight = jnp.einsum(
        "tf,td->fd", active_rows, grad_fed, preferred_element_type=jnp.float32
    )
    grad_active = jnp.einsum(
        "td,fd->tf", grad_fed, reduce_matrix, preferred_element_type=jnp.float32
    )
    grad_preact = jax.vjp(exact_gelu, preact_rows)[1](grad_active)[0].astype(jnp.bfloat16)
    grad_expand_bias = jnp.sum(grad_preact.astype(jnp.float32), axis=0)
    grad_expand_weight = jnp.einsum(
        "td,tf->df", feed_rows, grad_preact, preferred_element_type=jnp.float32
    )
    return (grad_reduce_weight, grad_preact, grad_expand_bias, grad_expand_weight)


def split_layer(
    inputs,
    pack_long,
    item_table,
    tau_table,
    delta_table,
    project_weight,
    project_bias,
    merge_weight,
    merge_bias,
    first_gain,
    first_shift,
    expand_weight,
    expand_bias,
    reduce_weight,
    reduce_bias,
    second_gain,
    second_shift,
    grad_output,
):
    tau_row, delta_row, segment = describe(pack_long, item_table, tau_table, delta_table)
    rows_all = lax.all_gather(inputs, "tensor", axis=0, tiled=True)
    query, keys, values = project(rows_all, project_weight, project_bias)
    attended, logsum = attend_forward(query, keys, values, tau_row, delta_row, segment)
    mixed_part = lax.psum_scatter(
        row_term(attended, merge_weight, "tc,cd->td"), "tensor", scatter_dimension=0, tiled=True
    )
    first_sum = inputs.astype(jnp.float32) + (mixed_part + merge_bias)
    normed, first_back = jax.vjp(layer_norm, first_sum, first_gain, first_shift)
    normed_low = normed.astype(jnp.bfloat16)
    feed_all = lax.all_gather(normed_low, "tensor", axis=0, tiled=True)
    preact = jnp.dot(feed_all, expand_weight, preferred_element_type=jnp.float32) + expand_bias
    active = exact_gelu(preact).astype(jnp.bfloat16)
    fed_part = lax.psum_scatter(
        row_term(active, reduce_weight, "tf,fd->td"), "tensor", scatter_dimension=0, tiled=True
    )
    second_sum = normed + (fed_part + reduce_bias)
    block_output, second_back = jax.vjp(layer_norm, second_sum, second_gain, second_shift)
    grad_second, grad_gain_b, grad_shift_b = second_back(grad_output.astype(jnp.float32))
    grad_reduce_bias = jnp.sum(grad_second, axis=0)
    grad_fed = lax.all_gather(grad_second.astype(jnp.bfloat16), "tensor", axis=0, tiled=True)
    feed_again = lax.all_gather(normed_low, "tensor", axis=0, tiled=True)
    preact_again = (
        jnp.dot(feed_again, expand_weight, preferred_element_type=jnp.float32) + expand_bias
    )
    active_again = exact_gelu(preact_again).astype(jnp.bfloat16)
    grad_reduce_weight, grad_preact, grad_expand_bias, grad_expand_weight = feed_backward(
        feed_again, preact_again, active_again, grad_fed, reduce_weight
    )
    grad_normed = grad_second + lax.psum_scatter(
        row_term(grad_preact, expand_weight, "tf,df->td"), "tensor", scatter_dimension=0, tiled=True
    )
    grad_first, grad_gain_a, grad_shift_a = first_back(grad_normed)
    grad_merge_bias = jnp.sum(grad_first, axis=0)
    grad_att = lax.all_gather(grad_first.astype(jnp.bfloat16), "tensor", axis=0, tiled=True)
    grad_merge_weight = jnp.einsum(
        "tc,td->cd", attended, grad_att, preferred_element_type=jnp.float32
    )
    grad_attended = jnp.einsum(
        "td,cd->tc", grad_att, merge_weight, preferred_element_type=jnp.float32
    ).astype(jnp.bfloat16)
    rows_again = lax.all_gather(inputs, "tensor", axis=0, tiled=True)
    query_again, keys_again, values_again = project(rows_again, project_weight, project_bias)
    grad_q, grad_k, grad_v = attend_backward(
        query_again, keys_again, values_again, grad_attended, logsum, tau_row, delta_row, segment
    )
    grad_stack = jnp.stack((grad_q, grad_k, grad_v), axis=1)
    grad_project_weight = jnp.einsum(
        "td,tjc->jdc", rows_again, grad_stack, preferred_element_type=jnp.float32
    )
    grad_project_bias = jnp.stack(
        (jnp.sum(grad_q.astype(jnp.float32), axis=0), jnp.sum(grad_v.astype(jnp.float32), axis=0))
    )
    input_grad = grad_first + lax.psum_scatter(
        row_term(grad_stack, project_weight, "tjc,jdc->td").astype(jnp.bfloat16),
        "tensor",
        scatter_dimension=0,
        tiled=True,
    ).astype(jnp.float32)
    summed_all = (
        lax.psum(grad_project_weight.astype(jnp.bfloat16), "dp").astype(jnp.float32),
        lax.psum(grad_project_bias.astype(jnp.bfloat16), "dp").astype(jnp.float32),
        lax.psum(grad_merge_weight.astype(jnp.bfloat16), "dp").astype(jnp.float32),
        lax.psum(grad_expand_weight.astype(jnp.bfloat16), "dp").astype(jnp.float32),
        lax.psum(grad_expand_bias.astype(jnp.bfloat16), "dp").astype(jnp.float32),
        lax.psum(grad_reduce_weight.astype(jnp.bfloat16), "dp").astype(jnp.float32),
    )
    summed_attention = summed_all[:3]
    summed_feed = summed_all[3:]
    small = lax.psum(
        (grad_merge_bias, grad_gain_a, grad_shift_a, grad_reduce_bias, grad_gain_b, grad_shift_b),
        ("dp", "tensor"),
    )
    return (
        block_output,
        input_grad,
        summed_attention[0],
        summed_attention[1],
        summed_attention[2],
        small[0],
        small[1],
        small[2],
        summed_feed[0],
        summed_feed[1],
        summed_feed[2],
        small[3],
        small[4],
        small[5],
    )


def mm(a, b):
    return lax.dot_general(a, b, (((1,), (0,)), ((), ())), preferred_element_type=F32)


def mm_nt(a, b):
    return lax.dot_general(a, b, (((1,), (1,)), ((), ())), preferred_element_type=F32)


def mm_tn(a, b):
    return lax.dot_general(a, b, (((0,), (0,)), ((), ())), preferred_element_type=F32)


def col_sum(v):
    return jnp.sum(v, axis=0, keepdims=True)


def row_mean(v):
    return jnp.mean(v, axis=1, keepdims=True)


def pack_rows(pack, long_ref, item_ref):
    per = LONG // SHORT
    longer = long_ref[pack] == 1
    rows = [jnp.where(longer, item_ref[pack * per], item_ref[pack * per + k]) for k in range(per)]
    return longer, rows


def pack_tau(rows, tau_ref):
    slot = lax.broadcasted_iota(jnp.int32, (LONG, 1), 0) // SHORT
    tau = jnp.full((LONG, 1), tau_ref[rows[0]], F32)
    for k in range(1, LONG // SHORT):
        tau = jnp.where(slot == k, tau_ref[rows[k]], tau)
    return tau


def pack_bias(longer, rows, delta_ref):
    slot_r = lax.broadcasted_iota(jnp.int32, (LONG, 1), 0) // SHORT
    slot_c = lax.broadcasted_iota(jnp.int32, (1, LONG), 1) // SHORT
    shift = delta_ref[pl.ds(rows[0], 1), :]
    for k in range(1, LONG // SHORT):
        piece = jnp.broadcast_to(delta_ref[pl.ds(rows[k], 1), :], (8, LONG))
        piece = pltpu.roll(piece, SHORT * k, 1)[0:1]
        shift = jnp.where(jnp.logical_and(jnp.logical_not(longer), slot_c == k), piece, shift)
    mask = jnp.logical_or(longer, slot_r == slot_c)
    return jnp.where(mask, shift * (HEAD**-0.5 * LOG2E), -1e30)


def forward_kernel(
    place, long_ref, item_ref, tau_ref, delta_ref, x_ref, wa_ref, wb_ref, b_ref,
    q_ref, k_ref, v_ref, o_ref, r_ref, p_ref, w_ref, bias_ref,
):
    step = pl.program_id(0)

    @pl.when(step == 0)
    def _():
        w_ref[:, :, :PAIR] = wa_ref[...]
        w_ref[:, :, PAIR:] = wb_ref[...]

    longer, rows = pack_rows(step + place[1], long_ref, item_ref)
    bias_ref[...] = pack_bias(longer, rows, delta_ref)
    tau = pack_tau(rows, tau_ref) * (HEAD**-0.5 * LOG2E)
    x = x_ref[...]
    q = (mm(x, w_ref[0]) + b_ref[0:1]).astype(BF16)
    k = mm(x, w_ref[1]).astype(BF16)
    v = (mm(x, w_ref[2]) + b_ref[1:2]).astype(BF16)
    q_ref[...] = q
    k_ref[...] = k
    v_ref[...] = v
    scaled = (q.astype(F32) * tau).astype(BF16)
    vf = v.astype(F32)
    first = lax.broadcasted_iota(jnp.int32, (1, PAIR), 1) < HEAD
    heads = q.shape[1] // HEAD

    def score(h):
        at = slice(h * HEAD, (h + 1) * HEAD)
        return mm_nt(scaled[:, at], k[:, at])

    def soften(s):
        s = s + bias_ref[...]
        return jnp.exp2(s - jnp.max(s, axis=1, keepdims=True)).astype(BF16)

    mixed = []

    def mix(h, w):
        p_ref[0, h] = w
        at = slice(h // 2 * PAIR, (h // 2 + 1) * PAIR)
        own = first if h % 2 == 0 else jnp.logical_not(first)
        mixed.append(mm(w, jnp.where(own, vf[:, at], 1.0).astype(BF16)))
        if h % 2 == 1:
            a, b = mixed[-2:]
            r = 1.0 / pltpu.roll(jnp.where(first, b, a), HEAD, 1)
            r_ref[:, at] = r
            o_ref[:, at] = (jnp.where(first, a, b) * r).astype(BF16)

    s = score(0)
    held = None
    for h in range(heads):
        later = score(h + 1) if h + 1 < heads else None
        w = soften(s)
        if held is not None:
            mix(h - 1, held)
        held, s = w, later
    mix(heads - 1, held)


def whole(shape):
    return pl.BlockSpec(shape, lambda *_: (0,) * len(shape), pipeline_mode=pl.Buffered(1))


def smem():
    return pl.BlockSpec(memory_space=pltpu.SMEM)


def kernel_params():
    return pltpu.CompilerParams(vmem_limit_bytes=60 * 2**20)


def cost(us):
    return pl.CostEstimate(flops=int(us * 1.0e9), bytes_accessed=0, transcendentals=0)


def attend(place, long_, item, tau, delta, x, wa, wb, bias, own):
    n, d = x.shape
    packs = n // LONG
    cols = 2 * PAIR
    row = lambda c: pl.BlockSpec((LONG, c), lambda i, *_: (i, 0))
    pick = (lambda h: lambda i, place, *_: (0, 0, place[0] ^ h)) if own else (lambda h: lambda *_: (0, 0, 0))
    out = jax.ShapeDtypeStruct((n, cols), BF16)
    heads = cols // HEAD
    return pl.pallas_call(
        forward_kernel,
        grid_spec=pltpu.PrefetchScalarGridSpec(
            num_scalar_prefetch=3,
            grid=(packs,),
            in_specs=[smem(), whole(delta.shape), row(d)]
            + [
                pl.BlockSpec((3, d, PAIR), pick(h), pipeline_mode=pl.Buffered(1)) for h in (0, 1)
            ]
            + [whole(bias.shape)],
            out_specs=[row(cols)] * 5
            + [pl.BlockSpec((1, heads, LONG, LONG), lambda i, *_: (i, 0, 0, 0))],
            scratch_shapes=[pltpu.VMEM((3, d, cols), BF16), pltpu.VMEM((LONG, LONG), F32)],
        ),
        out_shape=[out] * 4
        + [
            jax.ShapeDtypeStruct((n, cols), F32),
            jax.ShapeDtypeStruct((packs, heads, LONG, LONG), BF16),
        ],
        compiler_params=kernel_params(),
        cost_estimate=cost(11),
        name="attend_own" if own else "attend_other",
    )(place, long_, item, tau, delta, x, wa, wb, bias)


def gelu_parts(u):
    z = jnp.abs(u)
    t = 1.0 / (1.0 + (0.3275911 * 0.7071067811865476) * z)
    e = jnp.exp2(u * u * (-0.5 * LOG2E))
    poly = 0.5 * -1.453152027 + t * (0.5 * 1.061405429)
    poly = 0.5 * -0.284496736 + t * (0.5 * 1.421413741 + t * poly)
    tail = t * (0.5 * 0.254829592 + t * poly) * e
    return jnp.where(u >= 0, 1.0 - tail, tail), e


def feed_kernel(
    place, o0_ref, o1_ref, x_ref, gy_ref, mk_ref, ms_ref, ek_ref, es_ref, rk_ref, rs_ref,
    near_ref, far_ref, be_ref, vec_ref,
    out_ref, dh1_ref, do_ref, grad_ref, sum_ref, sbe_ref,
    wm_ref, act_ref, du_ref, gp_ref, n1_ref, dh2_ref, dh1b_ref, o_ref, *, tiles, tile,
):
    step = pl.program_id(0)
    d = x_ref.shape[1]
    hid = ek_ref.shape[1]
    mrows = mk_ref.shape[0]
    half = 2 * mrows
    expand = (ek_ref, es_ref, near_ref.at[0:d], far_ref.at[0:d])
    reduce_ = (rk_ref, rs_ref, near_ref.at[d:d + hid], far_ref.at[d:d + hid])

    @pl.when(step == 0)
    def _():
        wm_ref[0:mrows] = mk_ref[...]
        wm_ref[mrows:half] = ms_ref[...]
        wm_ref[half:half + mrows] = near_ref[d + hid:]
        wm_ref[half + mrows:] = far_ref[d + hid:]

    @pl.when(step < tiles)
    def _():
        here = pl.ds(pl.multiple_of(step * tile, tile), tile)
        bm, g1, b1, br, g2, b2 = [vec_ref[k:k + 1] for k in range(6)]
        o0, o1 = o0_ref[...], o1_ref[...]
        o_ref[here, :half] = o0
        o_ref[here, half:] = o1
        h1 = x_ref[...].astype(F32) + (mm(o0, wm_ref[:half]) + mm(o1, wm_ref[half:]) + bm)
        c = h1 - row_mean(h1)
        rs = lax.rsqrt(row_mean(c * c) + 1e-05)
        xh = c * rs
        n1 = xh * g1 + b1
        low = n1.astype(BF16)
        n1_ref[here] = low
        u = mm(low, expand[0][...])
        fed = n1 + br
        for k in range(4):
            later = mm(low, expand[k + 1][...]) if k < 3 else None
            at = slice(k * hid, (k + 1) * hid)
            u = u + be_ref[0:1, at]
            phi, e = gelu_parts(u)
            act = (u * phi).astype(BF16)
            act_ref[here, at] = act
            gp_ref[:, at] = (phi + u * (e * 0.3989422804014327)).astype(BF16)
            fed = fed + mm(act, reduce_[k][...])
            u = later
        c2 = fed - row_mean(fed)
        rs2 = lax.rsqrt(row_mean(c2 * c2) + 1e-05)
        xh2 = c2 * rs2
        out_ref[...] = xh2 * g2 + b2
        gy = gy_ref[...].astype(F32)
        gg = gy * g2
        dh2 = rs2 * ((gg - row_mean(gg)) - xh2 * row_mean(gg * xh2))
        dh2b = dh2.astype(BF16)
        dh2_ref[here] = dh2b
        dn = dh2
        sbe = []
        da = mm_nt(dh2b, reduce_[0][...])
        for k in range(4):
            later = mm_nt(dh2b, reduce_[k + 1][...]) if k < 3 else None
            at = slice(k * hid, (k + 1) * hid)
            du = (da * gp_ref[:, at].astype(F32)).astype(BF16)
            du_ref[here, at] = du
            sbe.append(col_sum(du.astype(F32)))
            dn = dn + mm_nt(du, expand[k][...])
            da = later
        gg1 = dn * g1
        dh1 = rs * ((gg1 - row_mean(gg1)) - xh * row_mean(gg1 * xh))
        dh1_ref[...] = dh1
        dh1b = dh1.astype(BF16)
        dh1b_ref[here] = dh1b
        do_ref[...] = mm_nt(dh1b, wm_ref[...]).astype(BF16)
        sums = [col_sum(dh1), col_sum(dn * xh), col_sum(dn), col_sum(dh2), col_sum(gy * xh2), col_sum(gy)]
        sums = jnp.concatenate(sums + [jnp.zeros((2, d), F32)], axis=0)
        sbe = jnp.broadcast_to(jnp.concatenate(sbe, axis=1), sbe_ref.shape)

        @pl.when(step == 0)
        def _():
            sum_ref[...] = sums
            sbe_ref[...] = sbe

        @pl.when(step > 0)
        def _():
            sum_ref[...] += sums
            sbe_ref[...] += sbe

    for quarter in range(4):

        @pl.when(step == tiles + quarter)
        def _(quarter=quarter):
            at = slice(quarter * hid, (quarter + 1) * hid)
            om = slice(quarter * mrows, (quarter + 1) * mrows)
            grad_ref[0, 0:hid] = mm_tn(act_ref[:, at], dh2_ref[...]).astype(BF16)
            grad_ref[0, hid:hid + d] = mm_tn(n1_ref[...], du_ref[:, at]).astype(BF16)
            grad_ref[0, hid + d:] = mm_tn(o_ref[:, om], dh1b_ref[...]).astype(BF16)


def feed(place, o0, o1, x, gy, merge, expand, reduce_, near, far, be, vec):
    n, d = x.shape
    tile = LONG
    tiles = n // tile
    mrows, hid = merge.shape[0] // 2, expand.shape[1] // 2
    full_hid = 4 * hid
    at = lambda i: jnp.minimum(i, tiles - 1)
    row = lambda c: pl.BlockSpec((tile, c), lambda i, *_: (at(i), 0))
    once = pl.Buffered(1)
    by_row = lambda shape, h: pl.BlockSpec(shape, lambda i, place: (place[0] ^ h, 0), pipeline_mode=once)
    by_col = lambda shape, h: pl.BlockSpec(shape, lambda i, place: (0, place[0] ^ h), pipeline_mode=once)
    S = jax.ShapeDtypeStruct
    grows = hid + d + mrows
    return pl.pallas_call(
        functools.partial(feed_kernel, tiles=tiles, tile=tile),
        grid_spec=pltpu.PrefetchScalarGridSpec(
            num_scalar_prefetch=1,
            grid=(tiles + 4,),
            in_specs=[row(o0.shape[1]), row(o1.shape[1]), row(d), row(d)]
            + [by_row((mrows, d), h) for h in (0, 1)]
            + [by_col((d, hid), h) for h in (0, 1)]
            + [by_row((hid, d), h) for h in (0, 1)]
            + [whole(near.shape), whole(far.shape), whole(be.shape), whole(vec.shape)],
            out_specs=[row(d), row(d), row(d)]
            + [
                pl.BlockSpec((1, grows, d), lambda i, *_: (jnp.maximum(i - tiles, 0), 0, 0)),
                pl.BlockSpec((8, d), lambda i, *_: (0, 0)),
                pl.BlockSpec((8, full_hid), lambda i, *_: (0, 0)),
            ],
            scratch_shapes=[
                pltpu.VMEM((4 * mrows, d), BF16),
                pltpu.VMEM((n, full_hid), BF16),
                pltpu.VMEM((n, full_hid), BF16),
                pltpu.VMEM((tile, full_hid), BF16),
                pltpu.VMEM((n, d), BF16),
                pltpu.VMEM((n, d), BF16),
                pltpu.VMEM((n, d), BF16),
                pltpu.VMEM((n, 4 * mrows), BF16),
            ],
        ),
        out_shape=[S((n, d), F32), S((n, d), F32), S((n, d), BF16), S((4, grows, d), BF16)]
        + [S((8, d), F32), S((8, full_hid), F32)],
        compiler_params=kernel_params(),
        cost_estimate=cost(60),
        name="feed",
    )(place, o0, o1, x, gy, merge, merge, expand, expand, reduce_, reduce_, near, far, be, vec)


def backward_kernel(
    place, long_ref, item_ref, tau_ref, q_ref, k_ref, v_ref, g_ref, o_ref, r_ref, p_ref,
    dq_ref, dk_ref, dv_ref,
):
    _, rows = pack_rows(pl.program_id(0) + place[1], long_ref, item_ref)
    tau = pack_tau(rows, tau_ref) * HEAD**-0.5
    heads = q_ref.shape[1] // HEAD
    lane = lax.broadcasted_iota(jnp.int32, (1, PAIR), 1)
    first = lane < HEAD
    ready = []
    for i in range(heads // 2):
        at = slice(i * PAIR, (i + 1) * PAIR)
        g = g_ref[:, at].astype(F32) * r_ref[:, at]
        low = g.astype(BF16)
        scaled = (g * tau).astype(BF16).astype(F32)
        d = scaled * o_ref[:, at].astype(F32)
        v = v_ref[:, at].astype(F32)
        for j in range(2):
            own = first if j == 0 else jnp.logical_not(first)
            spare = HEAD if j == 0 else 0
            dd = jnp.sum(jnp.where(own, d, 0.0), axis=1, keepdims=True)
            high = dd.astype(BF16).astype(F32)
            left = jnp.where(lane == spare, -high, jnp.where(lane == spare + 1, high - dd, 0.0))
            left = jnp.where(own, scaled, left).astype(BF16)
            ones = jnp.where(jnp.logical_or(lane == spare, lane == spare + 1), 1.0, 0.0)
            right = jnp.where(own, v, ones).astype(BF16)
            ready.append((left, right, low[:, j * HEAD:(j + 1) * HEAD]))

    def score(h):
        return mm_nt(ready[h][0], ready[h][1])

    res = []
    t = score(0)
    for h in range(heads):
        later = score(h + 1) if h + 1 < heads else None
        at = slice(h * HEAD, (h + 1) * HEAD)
        w = p_ref[0, h]
        r = (w.astype(F32) * t).astype(BF16)
        res.append((mm(r, k_ref[:, at]), mm_tn(q_ref[:, at], r), mm_tn(ready[h][2], w)))
        t = later
    for i in range(heads // 2):
        at = slice(i * PAIR, (i + 1) * PAIR)
        a, b = res[2 * i], res[2 * i + 1]
        dq_ref[:, at] = jnp.concatenate([a[0], b[0]], axis=1).astype(BF16)
        dk_ref[:, at] = jnp.concatenate([a[1], b[1]], axis=0).T.astype(BF16)
        dv_ref[:, at] = jnp.concatenate([a[2], b[2]], axis=0).T.astype(BF16)


def attend_back(place, long_, item, tau, q, k, v, g, o, r, p, slot):
    n, cols = q.shape
    packs = n // LONG
    row = lambda c: pl.BlockSpec((LONG, c), lambda i, *_: (i, 0))
    out = jax.ShapeDtypeStruct((n, cols), BF16)
    return pl.pallas_call(
        backward_kernel,
        grid_spec=pltpu.PrefetchScalarGridSpec(
            num_scalar_prefetch=3,
            grid=(packs,),
            in_specs=[smem()]
            + [row(cols)] * 3
            + [pl.BlockSpec((LONG, cols), lambda i, *_: (i, slot))]
            + [row(cols)] * 2
            + [pl.BlockSpec((1,) + p.shape[1:], lambda i, *_: (i, 0, 0, 0))],
            out_specs=[row(cols)] * 3,
        ),
        out_shape=[out] * 3,
        compiler_params=kernel_params(),
        cost_estimate=cost(11),
        name="attend_back%d" % slot,
    )(place, long_, item, tau, q, k, v, g, o, r, p)


def project_grad_kernel(x_ref, *refs):
    d_refs, (grad_ref, sum_ref) = refs[:-2], refs[-2:]
    depth = x_ref.shape[1]
    for k, d_ref in enumerate(d_refs):
        slot, j = divmod(k, 3)

        @pl.when(pl.program_id(0) == k)
        def _(slot=slot, j=j, d_ref=d_ref):
            d = d_ref[...]
            res = mm_tn(x_ref[...], d).astype(BF16)
            grad_ref[slot, 0, j * depth:(j + 1) * depth] = res[:, :PAIR]
            grad_ref[slot, 1, j * depth:(j + 1) * depth] = res[:, PAIR:]
            if j != 1:
                row = slot * 2 + j // 2
                sum_ref[row:row + 1] = col_sum(d.astype(F32))


def project_grad(x, grads):
    n, d = x.shape
    cols = grads[0].shape[1]
    S = jax.ShapeDtypeStruct
    return pl.pallas_call(
        project_grad_kernel,
        grid=(6,),
        in_specs=[whole(x.shape)] + [whole(g.shape) for g in grads],
        out_specs=[
            pl.BlockSpec((2, 2, 3 * d, PAIR), lambda i: (0, 0, 0, 0)),
            pl.BlockSpec((8, cols), lambda i: (0, 0)),
        ],
        out_shape=[S((2, 2, 3 * d, PAIR), BF16), S((8, cols), F32)],
        compiler_params=kernel_params(),
        cost_estimate=cost(7),
        name="project_grad",
    )(x, *grads)


def input_grad_kernel(place, dh1_ref, ka_ref, sa_ref, near_ref, far_ref, *refs):
    d_refs, (out_ref, w_ref) = refs[:-2], refs[-2:]

    @pl.when(pl.program_id(0) == 0)
    def _():
        for j in range(3):
            for k, ref in enumerate((ka_ref, sa_ref, near_ref, far_ref)):
                slot, h = divmod(k, 2)
                lo = (slot * 3 + j) * 2 * PAIR + h * PAIR
                w_ref[:, lo:lo + PAIR] = ref[j]

    d = jnp.concatenate([ref[...] for ref in d_refs], axis=1)
    out_ref[...] = dh1_ref[...] + mm_nt(d, w_ref[...])


def input_grad(place, dh1, weight, near, far, grads):
    n, d = dh1.shape
    tile = 2 * LONG if n % (2 * LONG) == 0 else LONG
    cols = grads[0].shape[1]
    row = lambda c: pl.BlockSpec((tile, c), lambda i, *_: (i, 0))
    pick = lambda h: pl.BlockSpec((3, d, PAIR), lambda i, place: (0, 0, place[0] ^ h), pipeline_mode=pl.Buffered(1))
    return pl.pallas_call(
        input_grad_kernel,
        grid_spec=pltpu.PrefetchScalarGridSpec(
            num_scalar_prefetch=1,
            grid=(n // tile,),
            in_specs=[row(d), pick(0), pick(1), whole(near.shape), whole(far.shape)] + [row(cols)] * 6,
            out_specs=row(d),
            scratch_shapes=[pltpu.VMEM((d, 6 * cols), BF16)],
        ),
        out_shape=jax.ShapeDtypeStruct((n, d), F32),
        compiler_params=kernel_params(),
        cost_estimate=cost(6),
        name="input_grad",
    )(place, dh1, weight, weight, near, far, *grads)


def flip(v, axis, mask):
    size = lax.axis_size(axis)
    return lax.ppermute(v, axis, [(i, i ^ mask) for i in range(size)])


def add_low(*parts):
    return functools.reduce(lambda a, b: a + b, [p.astype(F32) for p in parts]).astype(BF16)


def sum_quarters(grad, dp_size):
    core = lax.axis_index("dp") % 2
    got = flip(grad[:, 1], "dp", 1)
    far = flip(add_low(grad[1, 0], got[1]), "tensor", 1)
    mine = add_low(grad[0, 0], got[0], far)
    rows = mine.shape[0] // 2
    bit = lax.axis_index("dp") // 2 % 2
    send = lax.dynamic_slice_in_dim(mine, (1 - bit) * rows, rows, 0)
    keep = lax.dynamic_slice_in_dim(mine, bit * rows, rows, 0)
    total = add_low(keep, flip(send, "dp", 2))
    mask = 4
    while mask < dp_size:
        total = add_low(total, flip(total, "dp", mask))
        mask *= 2
    other = flip(total, "dp", 2)
    total = jnp.where(bit == 0, jnp.concatenate([total, other]), jnp.concatenate([other, total]))
    other = flip(total, "dp", 1)
    return jnp.where(core == 0, jnp.stack([total, other]), jnp.stack([other, total]))


def ordered(v, core):
    cols = v.shape[-1] // 2
    return jnp.where(core == 0, v, jnp.concatenate([v[..., cols:], v[..., :cols]], axis=-1))


def row_layer(
    inputs,
    pack_long,
    item_table,
    tau_table,
    delta_table,
    project_weight,
    project_bias,
    merge_weight,
    merge_bias,
    first_gain,
    first_shift,
    expand_weight,
    expand_bias,
    reduce_weight,
    reduce_bias,
    second_gain,
    second_shift,
    grad_output,
    dp_size,
):
    n, d = inputs.shape
    hid = expand_weight.shape[1] // 2
    mrows = merge_weight.shape[0] // 2
    core = lax.axis_index("dp") % 2
    place = jnp.stack([core, lax.axis_index("tensor") * (n // LONG)]).astype(jnp.int32)

    project_near = flip(lax.dynamic_slice_in_dim(project_weight, core * PAIR, PAIR, 2), "tensor", 1)
    biases = flip(jnp.concatenate([project_bias.reshape(-1), expand_bias]), "tensor", 1)
    rest = jnp.concatenate(
        [
            lax.dynamic_slice_in_dim(expand_weight, core * hid, hid, 1),
            lax.dynamic_slice_in_dim(reduce_weight, core * hid, hid, 0),
            lax.dynamic_slice_in_dim(merge_weight, core * mrows, mrows, 0),
        ],
        axis=0,
    )
    rest_near = flip(rest, "tensor", 1)
    project_far = flip(project_near, "dp", 1)
    rest_far = flip(rest_near, "dp", 1)

    table = (place, pack_long, item_table, tau_table)
    bias_own = ordered(project_bias, core)
    bias_other = ordered(biases[: project_bias.size].reshape(project_bias.shape), core)
    expand_all = jnp.concatenate([ordered(expand_bias, core), ordered(biases[project_bias.size :], core)])
    vectors = jnp.stack(
        [merge_bias, first_gain, first_shift, reduce_bias, second_gain, second_shift, merge_bias, merge_bias]
    )
    q0, k0, v0, o0, r0, p0 = attend(
        *table, delta_table, inputs, project_weight, project_weight, bias_own, True
    )
    q1, k1, v1, o1, r1, p1 = attend(
        *table, delta_table, inputs, project_near, project_far, bias_other, False
    )
    block_output, dh1, grad_att, grad_feed, sums, sum_hidden = feed(
        place, o0, o1, inputs, grad_output, merge_weight, expand_weight, reduce_weight,
        rest_near, rest_far, expand_all[None], vectors,
    )
    back0 = attend_back(*table, q0, k0, v0, grad_att, o0, r0, p0, 0)
    back1 = attend_back(*table, q1, k1, v1, grad_att, o1, r1, p1, 1)
    grads = tuple(back0) + tuple(back1)
    grad_project, sum_project = project_grad(inputs, grads)
    dx = input_grad(place, dh1, project_weight, project_near, project_far, grads)

    feed_sum = sum_quarters(grad_feed.reshape(2, 2, *grad_feed.shape[1:]), dp_size)
    project_sum = sum_quarters(grad_project, dp_size)

    wide = sum_project.shape[1]
    per_slot = [
        jnp.concatenate(
            [
                sums[:6].reshape(-1),
                ordered(sum_hidden[0, s * 2 * hid : (s + 1) * 2 * hid], core),
                ordered(sum_project[2 * s : 2 * s + 2], core).reshape(-1),
            ]
        )
        for s in (0, 1)
    ]
    small = per_slot[0] + flip(per_slot[1], "tensor", 1)
    mask = 1
    while mask < dp_size:
        small = small + flip(small, "dp", mask)
        mask *= 2
    vec = small[: 6 * d].reshape(6, d)
    hidden = small[6 * d : 6 * d + 2 * hid]
    biases = small[6 * d + 2 * hid :].reshape(2, wide)

    feed_sum = feed_sum.astype(F32)
    project_sum = project_sum.astype(F32).reshape(2, 3, d, PAIR)
    return (
        block_output,
        dx,
        jnp.concatenate([project_sum[0], project_sum[1]], axis=-1),
        biases,
        feed_sum[:, hid + d :].reshape(2 * mrows, d),
        vec[0],
        vec[1],
        vec[2],
        jnp.concatenate([feed_sum[0, hid : hid + d], feed_sum[1, hid : hid + d]], axis=1),
        hidden,
        feed_sum[:, :hid].reshape(2 * hid, d),
        vec[3],
        vec[4],
        vec[5],
    )


def on_device(*args, dp_size, tensor_size):
    inputs, project_weight = args[0], args[5]
    fits = tensor_size == 2 and dp_size >= 4 and dp_size & (dp_size - 1) == 0
    fits = fits and inputs.shape[0] % LONG == 0 and project_weight.shape[2] == 2 * PAIR
    if fits:
        return row_layer(*args, dp_size=dp_size)
    return split_layer(*args)


def solution(mesh):
    placed = (
        P(("dp", "tensor"), None),
        P("dp"),
        P("dp"),
        P(),
        P(),
        P(None, None, "tensor"),
        P(None, "tensor"),
        P("tensor", None),
        P(),
        P(),
        P(),
        P(None, "tensor"),
        P("tensor"),
        P("tensor", None),
        P(),
        P(),
        P(),
        P(("dp", "tensor"), None),
    )
    return jax.shard_map(
        functools.partial(
            on_device, dp_size=mesh.shape["dp"], tensor_size=mesh.shape["tensor"]
        ),
        mesh=mesh,
        in_specs=placed,
        out_specs=(
            P(("dp", "tensor"), None),
            P(("dp", "tensor"), None),
            P(None, None, "tensor"),
            P(None, "tensor"),
            P("tensor", None),
            P(),
            P(),
            P(),
            P(None, "tensor"),
            P("tensor"),
            P("tensor", None),
            P(),
            P(),
            P(),
        ),
        check_vma=False,
    )
```

```python
import functools
import jax
import jax.numpy as jnp
from jax import lax
from jax.experimental import pallas as pl
from jax.experimental.pallas import tpu as pltpu
from jax.sharding import Mesh, PartitionSpec as P

HEAD = 64
SHORT = 96
LONG = 384
TABLE = 64
PAIR = 2 * HEAD
SMALL = 128
SMALL_PAIR = 32
LOG2E = 1.4426950408889634
F32 = jnp.float32
BF16 = jnp.bfloat16


def layer_norm(values, gain, shift):
    mean = jnp.mean(values, axis=-1, keepdims=True)
    centred = values - mean
    spread = jnp.mean(centred * centred, axis=-1, keepdims=True)
    return centred * lax.rsqrt(spread + 1e-05) * gain + shift


def exact_gelu(values):
    return jax.nn.gelu(values, approximate=False)


def describe(pack_long, item_table, tau_table, delta_table):
    packs = pack_long.shape[0]
    per = LONG // SHORT
    count = packs * LONG
    longer = jnp.broadcast_to(pack_long[:, None] == 1, (packs, LONG)).reshape(count)
    lead_row = jnp.broadcast_to(item_table.reshape(packs, per)[:, :1], (packs, LONG)).reshape(count)
    each_row = jnp.broadcast_to(item_table[:, None], (packs * per, SHORT)).reshape(count)
    table_row = jnp.where(longer, lead_row, each_row)
    places = jnp.arange(count, dtype=jnp.int32)
    position = jnp.where(longer, places % LONG, places % SHORT)
    segment = jnp.where(longer, places // LONG * per, places // SHORT)
    picker = (table_row[:, None] == jnp.arange(TABLE, dtype=jnp.int32)[None, :]).astype(jnp.float32)
    tau_row = jnp.sum(picker * tau_table[None, :], axis=1)
    picked = jnp.dot(
        picker, delta_table, precision=lax.Precision.HIGHEST, preferred_element_type=jnp.float32
    )
    placed = position[:, None] == jnp.arange(LONG, dtype=jnp.int32)[None, :]
    delta_row = jnp.sum(jnp.where(placed, picked, 0.0), axis=1)
    return (tau_row, delta_row, segment)


def project(rows_all, project_weight, project_bias):
    query = (
        jnp.dot(rows_all, project_weight[0], preferred_element_type=jnp.float32) + project_bias[0]
    ).astype(jnp.bfloat16)
    keys = jnp.dot(rows_all, project_weight[1], preferred_element_type=jnp.float32).astype(
        jnp.bfloat16
    )
    values = (
        jnp.dot(rows_all, project_weight[2], preferred_element_type=jnp.float32) + project_bias[1]
    ).astype(jnp.bfloat16)
    return (query, keys, values)


def split_blocks(arrays):
    width = 2 * LONG
    return tuple((a.reshape((a.shape[0] // width, width) + a.shape[1:]) for a in arrays))


def block_scores(block_q, block_k, block_tau, block_delta, block_seg):
    raw = jnp.einsum("qhd,khd->hqk", block_q, block_k, preferred_element_type=jnp.float32)
    scores = (block_tau[None, :, None] * raw + block_delta[None, None, :]) * HEAD ** (-0.5)
    same = block_seg[:, None] == block_seg[None, :]
    return jnp.where(same[None], scores, -1e30)


def attend_forward(query, keys, values, tau_row, delta_row, segment):
    heads = query.shape[1] // HEAD
    shaped = tuple((a.reshape(a.shape[0], heads, HEAD) for a in (query, keys, values)))

    def one_block(parts):
        block_q, block_k, block_v, block_tau, block_delta, block_seg = parts
        scores = block_scores(block_q, block_k, block_tau, block_delta, block_seg)
        top = jnp.max(scores, axis=-1, keepdims=True)
        expo = jnp.exp(scores - top)
        totals = jnp.sum(expo, axis=-1, keepdims=True)
        weights = (expo / totals).astype(jnp.bfloat16)
        mixed = jnp.einsum("hqk,khd->qhd", weights, block_v, preferred_element_type=jnp.float32)
        return (
            mixed.reshape(mixed.shape[0], heads * HEAD).astype(jnp.bfloat16),
            top + jnp.log(totals),
        )

    attended, logsum = lax.map(one_block, split_blocks(shaped + (tau_row, delta_row, segment)))
    return (attended.reshape(query.shape), logsum)


def attend_backward(query, keys, values, grad_att, logsum, tau_row, delta_row, segment):
    heads = query.shape[1] // HEAD
    shaped = tuple((a.reshape(a.shape[0], heads, HEAD) for a in (query, keys, values, grad_att)))
    blocked = split_blocks(shaped + (tau_row, delta_row, segment))

    def one_block(parts):
        block_q, block_k, block_v, block_g, block_lse, block_tau, block_delta, block_seg = parts
        scores = block_scores(block_q, block_k, block_tau, block_delta, block_seg)
        probs = jnp.exp(scores - block_lse)
        dprob = jnp.einsum("qhd,khd->hqk", block_g, block_v, preferred_element_type=jnp.float32)
        dscore = probs * (dprob - jnp.sum(dprob * probs, axis=-1, keepdims=True))
        lowered = (dscore * HEAD ** (-0.5) * block_tau[None, :, None]).astype(jnp.bfloat16)
        grad_q = jnp.einsum("hqk,khd->qhd", lowered, block_k, preferred_element_type=jnp.float32)
        grad_k = jnp.einsum("hqk,qhd->khd", lowered, block_q, preferred_element_type=jnp.float32)
        grad_v = jnp.einsum(
            "hqk,qhd->khd", probs.astype(jnp.bfloat16), block_g, preferred_element_type=jnp.float32
        )
        width = block_q.shape[0]
        return tuple(
            (g.reshape(width, heads * HEAD).astype(jnp.bfloat16) for g in (grad_q, grad_k, grad_v))
        )

    grads = lax.map(one_block, blocked[:4] + (logsum,) + blocked[4:])
    return tuple((g.reshape(query.shape) for g in grads))


def row_term(left, right, form):
    return jnp.einsum(form, left, right, preferred_element_type=jnp.float32)


def feed_backward(feed_rows, preact_rows, active_rows, grad_fed, reduce_matrix):
    grad_reduce_weight = jnp.einsum(
        "tf,td->fd", active_rows, grad_fed, preferred_element_type=jnp.float32
    )
    grad_active = jnp.einsum(
        "td,fd->tf", grad_fed, reduce_matrix, preferred_element_type=jnp.float32
    )
    grad_preact = jax.vjp(exact_gelu, preact_rows)[1](grad_active)[0].astype(jnp.bfloat16)
    grad_expand_bias = jnp.sum(grad_preact.astype(jnp.float32), axis=0)
    grad_expand_weight = jnp.einsum(
        "td,tf->df", feed_rows, grad_preact, preferred_element_type=jnp.float32
    )
    return (grad_reduce_weight, grad_preact, grad_expand_bias, grad_expand_weight)


def split_layer(
    inputs,
    pack_long,
    item_table,
    tau_table,
    delta_table,
    project_weight,
    project_bias,
    merge_weight,
    merge_bias,
    first_gain,
    first_shift,
    expand_weight,
    expand_bias,
    reduce_weight,
    reduce_bias,
    second_gain,
    second_shift,
    grad_output,
):
    tau_row, delta_row, segment = describe(pack_long, item_table, tau_table, delta_table)
    rows_all = lax.all_gather(inputs, "tensor", axis=0, tiled=True)
    query, keys, values = project(rows_all, project_weight, project_bias)
    attended, logsum = attend_forward(query, keys, values, tau_row, delta_row, segment)
    mixed_part = lax.psum_scatter(
        row_term(attended, merge_weight, "tc,cd->td"), "tensor", scatter_dimension=0, tiled=True
    )
    first_sum = inputs.astype(jnp.float32) + (mixed_part + merge_bias)
    normed, first_back = jax.vjp(layer_norm, first_sum, first_gain, first_shift)
    normed_low = normed.astype(jnp.bfloat16)
    feed_all = lax.all_gather(normed_low, "tensor", axis=0, tiled=True)
    preact = jnp.dot(feed_all, expand_weight, preferred_element_type=jnp.float32) + expand_bias
    active = exact_gelu(preact).astype(jnp.bfloat16)
    fed_part = lax.psum_scatter(
        row_term(active, reduce_weight, "tf,fd->td"), "tensor", scatter_dimension=0, tiled=True
    )
    second_sum = normed + (fed_part + reduce_bias)
    block_output, second_back = jax.vjp(layer_norm, second_sum, second_gain, second_shift)
    grad_second, grad_gain_b, grad_shift_b = second_back(grad_output.astype(jnp.float32))
    grad_reduce_bias = jnp.sum(grad_second, axis=0)
    grad_fed = lax.all_gather(grad_second.astype(jnp.bfloat16), "tensor", axis=0, tiled=True)
    feed_again = lax.all_gather(normed_low, "tensor", axis=0, tiled=True)
    preact_again = (
        jnp.dot(feed_again, expand_weight, preferred_element_type=jnp.float32) + expand_bias
    )
    active_again = exact_gelu(preact_again).astype(jnp.bfloat16)
    grad_reduce_weight, grad_preact, grad_expand_bias, grad_expand_weight = feed_backward(
        feed_again, preact_again, active_again, grad_fed, reduce_weight
    )
    grad_normed = grad_second + lax.psum_scatter(
        row_term(grad_preact, expand_weight, "tf,df->td"), "tensor", scatter_dimension=0, tiled=True
    )
    grad_first, grad_gain_a, grad_shift_a = first_back(grad_normed)
    grad_merge_bias = jnp.sum(grad_first, axis=0)
    grad_att = lax.all_gather(grad_first.astype(jnp.bfloat16), "tensor", axis=0, tiled=True)
    grad_merge_weight = jnp.einsum(
        "tc,td->cd", attended, grad_att, preferred_element_type=jnp.float32
    )
    grad_attended = jnp.einsum(
        "td,cd->tc", grad_att, merge_weight, preferred_element_type=jnp.float32
    ).astype(jnp.bfloat16)
    rows_again = lax.all_gather(inputs, "tensor", axis=0, tiled=True)
    query_again, keys_again, values_again = project(rows_again, project_weight, project_bias)
    grad_q, grad_k, grad_v = attend_backward(
        query_again, keys_again, values_again, grad_attended, logsum, tau_row, delta_row, segment
    )
    grad_stack = jnp.stack((grad_q, grad_k, grad_v), axis=1)
    grad_project_weight = jnp.einsum(
        "td,tjc->jdc", rows_again, grad_stack, preferred_element_type=jnp.float32
    )
    grad_project_bias = jnp.stack(
        (jnp.sum(grad_q.astype(jnp.float32), axis=0), jnp.sum(grad_v.astype(jnp.float32), axis=0))
    )
    input_grad = grad_first + lax.psum_scatter(
        row_term(grad_stack, project_weight, "tjc,jdc->td").astype(jnp.bfloat16),
        "tensor",
        scatter_dimension=0,
        tiled=True,
    ).astype(jnp.float32)
    summed_all = (
        lax.psum(grad_project_weight.astype(jnp.bfloat16), "dp").astype(jnp.float32),
        lax.psum(grad_project_bias.astype(jnp.bfloat16), "dp").astype(jnp.float32),
        lax.psum(grad_merge_weight.astype(jnp.bfloat16), "dp").astype(jnp.float32),
        lax.psum(grad_expand_weight.astype(jnp.bfloat16), "dp").astype(jnp.float32),
        lax.psum(grad_expand_bias.astype(jnp.bfloat16), "dp").astype(jnp.float32),
        lax.psum(grad_reduce_weight.astype(jnp.bfloat16), "dp").astype(jnp.float32),
    )
    summed_attention = summed_all[:3]
    summed_feed = summed_all[3:]
    small = lax.psum(
        (grad_merge_bias, grad_gain_a, grad_shift_a, grad_reduce_bias, grad_gain_b, grad_shift_b),
        ("dp", "tensor"),
    )
    return (
        block_output,
        input_grad,
        summed_attention[0],
        summed_attention[1],
        summed_attention[2],
        small[0],
        small[1],
        small[2],
        summed_feed[0],
        summed_feed[1],
        summed_feed[2],
        small[3],
        small[4],
        small[5],
    )


def mm(a, b):
    return lax.dot_general(a, b, (((1,), (0,)), ((), ())), preferred_element_type=F32)


def mm_nt(a, b):
    return lax.dot_general(a, b, (((1,), (1,)), ((), ())), preferred_element_type=F32)


def mm_tn(a, b):
    return lax.dot_general(a, b, (((0,), (0,)), ((), ())), preferred_element_type=F32)


def col_sum(v):
    return jnp.sum(v, axis=0, keepdims=True)


def row_mean(v):
    return jnp.mean(v, axis=1, keepdims=True)


def pack_rows(pack, long_ref, item_ref):
    per = LONG // SHORT
    longer = long_ref[pack] == 1
    rows = [jnp.where(longer, item_ref[pack * per], item_ref[pack * per + k]) for k in range(per)]
    return longer, rows


def pack_tau(rows, tau_ref):
    slot = lax.broadcasted_iota(jnp.int32, (LONG, 1), 0) // SHORT
    tau = jnp.full((LONG, 1), tau_ref[rows[0]], F32)
    for k in range(1, LONG // SHORT):
        tau = jnp.where(slot == k, tau_ref[rows[k]], tau)
    return tau


def pack_bias(longer, rows, delta_ref):
    slot_r = lax.broadcasted_iota(jnp.int32, (LONG, 1), 0) // SHORT
    slot_c = lax.broadcasted_iota(jnp.int32, (1, LONG), 1) // SHORT
    shift = delta_ref[pl.ds(rows[0], 1), :]
    for k in range(1, LONG // SHORT):
        piece = jnp.broadcast_to(delta_ref[pl.ds(rows[k], 1), :], (8, LONG))
        piece = pltpu.roll(piece, SHORT * k, 1)[0:1]
        shift = jnp.where(jnp.logical_and(jnp.logical_not(longer), slot_c == k), piece, shift)
    mask = jnp.logical_or(longer, slot_r == slot_c)
    return jnp.where(mask, shift * (HEAD**-0.5 * LOG2E), -1e30)


def forward_kernel(
    place, long_ref, item_ref, tau_ref, delta_ref, x_ref, wa_ref, wb_ref, ba_ref, bb_ref,
    q_ref, k_ref, v_ref, o_ref, r_ref, p_ref, w_ref, bias_ref,
):
    step = pl.program_id(0)

    @pl.when(step == 0)
    def _():
        w_ref[:, :, :PAIR] = wa_ref[...]
        w_ref[:, :, PAIR:] = wb_ref[...]

    longer, rows = pack_rows(step + place[1], long_ref, item_ref)
    bias_ref[...] = pack_bias(longer, rows, delta_ref)
    tau = pack_tau(rows, tau_ref) * (HEAD**-0.5 * LOG2E)
    x = x_ref[...]
    b = jnp.concatenate([ba_ref[...], bb_ref[...]], axis=1)
    q = (mm(x, w_ref[0]) + b[0:1]).astype(BF16)
    k = mm(x, w_ref[1]).astype(BF16)
    v = (mm(x, w_ref[2]) + b[1:2]).astype(BF16)
    q_ref[...] = q
    k_ref[...] = k
    v_ref[...] = v
    scaled = (q.astype(F32) * tau).astype(BF16)
    vf = v.astype(F32)
    first = lax.broadcasted_iota(jnp.int32, (1, PAIR), 1) < HEAD
    heads = q.shape[1] // HEAD

    def score(h):
        at = slice(h * HEAD, (h + 1) * HEAD)
        return mm_nt(scaled[:, at], k[:, at])

    def soften(s):
        s = s + bias_ref[...]
        return jnp.exp2(s - jnp.max(s, axis=1, keepdims=True)).astype(BF16)

    mixed = []

    def mix(h, w):
        p_ref[0, h] = w
        at = slice(h // 2 * PAIR, (h // 2 + 1) * PAIR)
        own = first if h % 2 == 0 else jnp.logical_not(first)
        mixed.append(mm(w, jnp.where(own, vf[:, at], 1.0).astype(BF16)))
        if h % 2 == 1:
            a, b = mixed[-2:]
            r = 1.0 / pltpu.roll(jnp.where(first, b, a), HEAD, 1)
            r_ref[:, at] = r
            o_ref[:, at] = (jnp.where(first, a, b) * r).astype(BF16)

    s = score(0)
    held = None
    for h in range(heads):
        later = score(h + 1) if h + 1 < heads else None
        w = soften(s)
        if held is not None:
            mix(h - 1, held)
        held, s = w, later
    mix(heads - 1, held)


def whole(shape):
    return pl.BlockSpec(shape, lambda *_: (0,) * len(shape), pipeline_mode=pl.Buffered(1))


def smem():
    return pl.BlockSpec(memory_space=pltpu.SMEM)


def kernel_params(mib):
    return pltpu.CompilerParams(vmem_limit_bytes=mib * 2**20)


def cost(us):
    return pl.CostEstimate(flops=int(us * 1.0e6), bytes_accessed=0, transcendentals=0)


def attend(place, long_, item, tau, delta, x, wa, wb, bias, own):
    n, d = x.shape
    packs = n // LONG
    cols = 2 * PAIR
    row = lambda c: pl.BlockSpec((LONG, c), lambda i, *_: (i, 0))
    pick = (lambda h: lambda i, place, *_: (0, 0, place[0] ^ h)) if own else (lambda h: lambda *_: (0, 0, 0))
    out = jax.ShapeDtypeStruct((n, cols), BF16)
    heads = cols // HEAD
    return pl.pallas_call(
        forward_kernel,
        grid_spec=pltpu.PrefetchScalarGridSpec(
            num_scalar_prefetch=3,
            grid=(packs,),
            in_specs=[smem(), whole(delta.shape), row(d)]
            + [
                pl.BlockSpec((3, d, PAIR), pick(h), pipeline_mode=pl.Buffered(1)) for h in (0, 1)
            ]
            + [pl.BlockSpec((2, PAIR), lambda i, place, *_, h=h: (0, place[0] ^ h)) for h in (0, 1)],
            out_specs=[row(cols)] * 5
            + [pl.BlockSpec((1, heads, LONG, LONG), lambda i, *_: (i, 0, 0, 0))],
            scratch_shapes=[pltpu.VMEM((3, d, cols), BF16), pltpu.VMEM((LONG, LONG), F32)],
        ),
        out_shape=[out] * 4
        + [
            jax.ShapeDtypeStruct((n, cols), F32),
            jax.ShapeDtypeStruct((packs, heads, LONG, LONG), BF16),
        ],
        compiler_params=kernel_params(60),
        cost_estimate=cost(1 if own else 8000),
        name="attend_own" if own else "attend_other",
    )(place, long_, item, tau, delta, x, wa, wb, bias, bias)


def gelu_parts(u):
    phi = 0.5 + 0.5 * lax.erf(u * 0.7071067811865476)
    return phi, jnp.exp2(u * u * (-0.5 * LOG2E))


def feed_kernel(
    place, o0_ref, o1_ref, x_ref, gy_ref, mk_ref, ms_ref, ek_ref, es_ref, rk_ref, rs_ref,
    near_ref, far_ref, b0_ref, b1_ref, b2_ref, b3_ref, bm_ref, g1_ref, h1_ref, br_ref, g2_ref, h2_ref,
    out_ref, dh1_ref, do_ref, act_ref, du_ref, n1_ref, dh2_ref, dh1b_ref, sum_ref, sbe_ref, send_ref,
    wm_ref, act_all, du_all, gp_ref, n1_all, dh2_all, dh1b_all, o_all, *, tiles, tile,
):
    step = pl.program_id(0)
    d = x_ref.shape[1]
    hid = ek_ref.shape[1]
    mrows = mk_ref.shape[0]
    half = 2 * mrows
    expand = (ek_ref, es_ref, near_ref.at[0:d], far_ref.at[0:d])
    reduce_ = (rk_ref, rs_ref, near_ref.at[d:d + hid], far_ref.at[d:d + hid])

    @pl.when(step == 0)
    def _():
        wm_ref[0:mrows] = mk_ref[...]
        wm_ref[mrows:half] = ms_ref[...]
        wm_ref[half:half + mrows] = near_ref[d + hid:]
        wm_ref[half + mrows:] = far_ref[d + hid:]

    @pl.when(step < tiles)
    def _():
        here = pl.ds(pl.multiple_of(step * tile, tile), tile)
        bm, g1, b1, br, g2, b2 = [ref[...] for ref in (bm_ref, g1_ref, h1_ref, br_ref, g2_ref, h2_ref)]
        be = (b0_ref, b1_ref, b2_ref, b3_ref)
        o0, o1 = o0_ref[...], o1_ref[...]
        o_all[here, :mrows] = o0[:, mrows:]
        o_all[here, mrows:] = o1[:, mrows:]
        h1 = x_ref[...].astype(F32) + (mm(o0, wm_ref[:half]) + mm(o1, wm_ref[half:]) + bm)
        c = h1 - row_mean(h1)
        rs = lax.rsqrt(row_mean(c * c) + 1e-05)
        xh = c * rs
        n1 = xh * g1 + b1
        low = n1.astype(BF16)
        n1_ref[...] = low
        n1_all[here] = low
        u = mm(low, expand[0][...])
        fed = n1 + br
        for k in range(4):
            later = mm(low, expand[k + 1][...]) if k < 3 else None
            at = slice(k * hid, (k + 1) * hid)
            u = u + be[k][...]
            phi, e = gelu_parts(u)
            act = (u * phi).astype(BF16)
            mine = slice(k // 2 * hid, (k // 2 + 1) * hid)
            if k % 2 == 0:
                act_ref[:, mine] = act
            else:
                act_all[here, mine] = act
            gp_ref[:, at] = (phi + u * (e * 0.3989422804014327)).astype(BF16)
            fed = fed + mm(act, reduce_[k][...])
            u = later
        c2 = fed - row_mean(fed)
        rs2 = lax.rsqrt(row_mean(c2 * c2) + 1e-05)
        xh2 = c2 * rs2
        out_ref[...] = xh2 * g2 + b2
        gy = gy_ref[...].astype(F32)
        gg = gy * g2
        dh2 = rs2 * ((gg - row_mean(gg)) - xh2 * row_mean(gg * xh2))
        dh2b = dh2.astype(BF16)
        dh2_ref[...] = dh2b
        dh2_all[here] = dh2b
        dn = dh2
        sbe = []
        da = mm_nt(dh2b, reduce_[0][...])
        for k in range(4):
            later = mm_nt(dh2b, reduce_[k + 1][...]) if k < 3 else None
            at = slice(k * hid, (k + 1) * hid)
            du = (da * gp_ref[:, at].astype(F32)).astype(BF16)
            mine = slice(k // 2 * hid, (k // 2 + 1) * hid)
            if k % 2 == 0:
                du_ref[:, mine] = du
            else:
                du_all[here, mine] = du
            sbe.append(col_sum(du.astype(F32)))
            dn = dn + mm_nt(du, expand[k][...])
            da = later
        gg1 = dn * g1
        dh1 = rs * ((gg1 - row_mean(gg1)) - xh * row_mean(gg1 * xh))
        dh1_ref[...] = dh1
        dh1b = dh1.astype(BF16)
        dh1b_ref[...] = dh1b
        dh1b_all[here] = dh1b
        do_ref[...] = mm_nt(dh1b, wm_ref[...]).astype(BF16)
        sums = [col_sum(dh1), col_sum(dn * xh), col_sum(dn), col_sum(dh2), col_sum(gy * xh2), col_sum(gy)]
        sums = jnp.concatenate(sums + [jnp.zeros((2, d), F32)], axis=0)
        sbe = jnp.broadcast_to(jnp.concatenate(sbe, axis=1), sbe_ref.shape)

        @pl.when(step == 0)
        def _():
            sum_ref[...] = sums
            sbe_ref[...] = sbe

        @pl.when(step > 0)
        def _():
            sum_ref[...] += sums
            sbe_ref[...] += sbe

    for slot in range(2):

        @pl.when(step == tiles + slot)
        def _(slot=slot):
            at = slice(slot * hid, (slot + 1) * hid)
            om = slice(slot * mrows, (slot + 1) * mrows)
            send_ref[0, 0:hid] = mm_tn(act_all[:, at], dh2_all[...]).astype(BF16)
            send_ref[0, hid:hid + d] = mm_tn(n1_all[...], du_all[:, at]).astype(BF16)
            rows = hid + d + mrows
            send_ref[0, hid + d:rows] = mm_tn(o_all[:, om], dh1b_all[...]).astype(BF16)
            send_ref[0, rows:] = small_rows(place[0] ^ 1, sum_ref[...], sbe_ref[...], slot, 1, hid)


def small_rows(which, sums, sbe, slot, h, hid):
    lo = (2 * slot + h) * hid
    part = jnp.where(which == 0, sums[0:3], sums[3:6])
    fill = jnp.zeros((SMALL - 4, sums.shape[1]), F32)
    return jnp.concatenate([sbe[0:1, lo:lo + hid], part, fill], axis=0).astype(BF16)


def feed(place, o0, o1, x, gy, merge, expand, reduce_, near, far, be0, be1, vecs):
    n, d = x.shape
    tile = LONG
    tiles = n // tile
    mrows, hid = merge.shape[0] // 2, expand.shape[1] // 2
    full_hid = 4 * hid
    at = lambda i: jnp.minimum(i, tiles - 1)
    row = lambda c: pl.BlockSpec((tile, c), lambda i, *_: (at(i), 0))
    once = pl.Buffered(1)
    by_row = lambda shape, h: pl.BlockSpec(shape, lambda i, place: (place[0] ^ h, 0), pipeline_mode=once)
    by_col = lambda shape, h: pl.BlockSpec(shape, lambda i, place: (0, place[0] ^ h), pipeline_mode=once)
    S = jax.ShapeDtypeStruct
    grows = hid + d + mrows + SMALL
    bias = lambda h: pl.BlockSpec((1, hid), lambda i, place: (0, place[0] ^ h), pipeline_mode=once)
    return pl.pallas_call(
        functools.partial(feed_kernel, tiles=tiles, tile=tile),
        grid_spec=pltpu.PrefetchScalarGridSpec(
            num_scalar_prefetch=1,
            grid=(tiles + 2,),
            in_specs=[row(o0.shape[1]), row(o1.shape[1]), row(d), row(d)]
            + [by_row((mrows, d), h) for h in (0, 1)]
            + [by_col((d, hid), h) for h in (0, 1)]
            + [by_row((hid, d), h) for h in (0, 1)]
            + [whole(near.shape), whole(far.shape)]
            + [bias(0), bias(1), bias(0), bias(1)]
            + [whole((1, d))] * 6,
            out_specs=[row(d), row(d), row(d), row(2 * hid), row(2 * hid), row(d), row(d), row(d)]
            + [
                pl.BlockSpec((8, d), lambda i, *_: (0, 0)),
                pl.BlockSpec((8, full_hid), lambda i, *_: (0, 0)),
                pl.BlockSpec((1, grows, d), lambda i, *_: (jnp.maximum(i - tiles, 0), 0, 0)),
            ],
            scratch_shapes=[
                pltpu.VMEM((4 * mrows, d), BF16),
                pltpu.VMEM((n, 2 * hid), BF16),
                pltpu.VMEM((n, 2 * hid), BF16),
                pltpu.VMEM((tile, full_hid), BF16),
                pltpu.VMEM((n, d), BF16),
                pltpu.VMEM((n, d), BF16),
                pltpu.VMEM((n, d), BF16),
                pltpu.VMEM((n, 2 * mrows), BF16),
            ],
        ),
        out_shape=[S((n, d), F32), S((n, d), F32), S((n, d), BF16)]
        + [S((n, 2 * hid), BF16)] * 2
        + [S((n, d), BF16)] * 3
        + [S((8, d), F32), S((8, full_hid), F32), S((2, grows, d), BF16)],
        compiler_params=kernel_params(58),
        cost_estimate=cost(60),
        name="feed",
    )(place, o0, o1, x, gy, merge, merge, expand, expand, reduce_, reduce_, near, far, be0, be0, be1, be1, *vecs)


def feed_grad_kernel(
    place, act_hbm, du_hbm, n1_hbm, dh2_hbm, dh1b_hbm, o0_hbm, o1_hbm, sum_ref, sbe_ref, keep_hbm,
    act, du, n1, dh2, dh1b, o, keep, sems, out_sems,
):
    hid, d, mrows = act.shape[2], n1.shape[1], o.shape[2]

    def fetch(src, dst, k):
        copy = pltpu.make_async_copy(src, dst, sems.at[k])
        copy.start()
        return copy

    cols = lambda s: (slice(None), pl.ds(s * hid, hid))
    heads = lambda ref: ref.at[:, pl.ds(0, mrows)]
    order = (
        (act_hbm.at[cols(1)], act.at[1]), (dh2_hbm, dh2), (n1_hbm, n1), (du_hbm.at[cols(1)], du.at[1]),
        (heads(o1_hbm), o.at[1]), (dh1b_hbm, dh1b),
        (act_hbm.at[cols(0)], act.at[0]), (du_hbm.at[cols(0)], du.at[0]), (heads(o0_hbm), o.at[0]),
    )
    copies = [fetch(src, dst, k) for k, (src, dst) in enumerate(order)]
    flush = []
    rows = hid + d + mrows
    for slot, waits in ((1, (0, 2, 4, 6)), (0, (6, 7, 8, 9))):
        for k in range(waits[0], waits[1]):
            copies[k].wait()
        keep[slot, 0:hid] = mm_tn(act[slot], dh2[...]).astype(BF16)
        for k in range(waits[1], waits[2]):
            copies[k].wait()
        keep[slot, hid:hid + d] = mm_tn(n1[...], du[slot]).astype(BF16)
        for k in range(waits[2], waits[3]):
            copies[k].wait()
        keep[slot, hid + d:rows] = mm_tn(o[slot], dh1b[...]).astype(BF16)
        keep[slot, rows:] = small_rows(place[0], sum_ref[...], sbe_ref[...], slot, 0, hid)
        out = pltpu.make_async_copy(keep.at[slot], keep_hbm.at[slot], out_sems.at[slot])
        out.start()
        flush.append(out)
    for out in flush:
        out.wait()


def feed_grad(place, act, du, n1, dh2, dh1b, o0, o1, sums, sbe):
    n, d = n1.shape
    hid, mrows = act.shape[1] // 2, o0.shape[1] // 2
    grows = hid + d + mrows + SMALL
    hbm = pl.BlockSpec(memory_space=pl.ANY)
    return pl.pallas_call(
        feed_grad_kernel,
        in_specs=[smem()] + [hbm] * 7 + [whole(sums.shape), whole(sbe.shape)],
        out_specs=hbm,
        out_shape=jax.ShapeDtypeStruct((2, grows, d), BF16),
        scratch_shapes=[
            pltpu.VMEM((2, n, hid), BF16),
            pltpu.VMEM((2, n, hid), BF16),
            pltpu.VMEM((n, d), BF16),
            pltpu.VMEM((n, d), BF16),
            pltpu.VMEM((n, d), BF16),
            pltpu.VMEM((2, n, mrows), BF16),
            pltpu.VMEM((2, grows, d), BF16),
            pltpu.SemaphoreType.DMA((9,)),
            pltpu.SemaphoreType.DMA((2,)),
        ],
        compiler_params=kernel_params(58),
        cost_estimate=cost(9),
        name="feed_grad",
    )(place, act, du, n1, dh2, dh1b, o0, o1, sums, sbe)


def backward_kernel(place, long_ref, item_ref, tau_ref, *refs, sets, steps, group):
    step = pl.program_id(0)
    width = group * LONG
    per = [refs[7 * s:7 * s + 7] for s in range(sets)]
    x_ref = refs[7 * sets]
    outs = refs[7 * sets + 1:7 * sets + 1 + 2 * sets]
    x_all, d_all = refs[-2:]
    x_all[pl.ds(pl.multiple_of(step * width, width), width)] = x_ref[...]
    lane = lax.broadcasted_iota(jnp.int32, (1, PAIR), 1)
    first = lane < HEAD
    ready = []
    for m in range(group):
        _, rows = pack_rows(step * group + m + place[1], long_ref, item_ref)
        tau = pack_tau(rows, tau_ref) * HEAD**-0.5
        here = slice(m * LONG, (m + 1) * LONG)
        for s in range(sets):
            _, _, v_ref, g_ref, o_ref, r_ref, _ = per[s]
            g = g_ref[here].astype(F32) * r_ref[here]
            low = g.astype(BF16)
            scaled = (g * tau).astype(BF16).astype(F32)
            d = scaled * o_ref[here].astype(F32)
            v = v_ref[here].astype(F32)
            for j in range(2):
                own = first if j == 0 else jnp.logical_not(first)
                spare = HEAD if j == 0 else 0
                dd = jnp.sum(jnp.where(own, d, 0.0), axis=1, keepdims=True)
                high = dd.astype(BF16).astype(F32)
                left = jnp.where(lane == spare, -high, jnp.where(lane == spare + 1, high - dd, 0.0))
                left = jnp.where(own, scaled, left).astype(BF16)
                ones = jnp.where(jnp.logical_or(lane == spare, lane == spare + 1), 1.0, 0.0)
                right = jnp.where(own, v, ones).astype(BF16)
                ready.append((left, right, low[:, j * HEAD:(j + 1) * HEAD], m, s, j))
    res = []
    t = mm_nt(*ready[0][:2])
    for n, (_, _, low, m, s, j) in enumerate(ready):
        later = mm_nt(*ready[n + 1][:2]) if n + 1 < len(ready) else None
        q_ref, k_ref, _, _, _, _, p_ref = per[s]
        here = slice(m * LONG, (m + 1) * LONG)
        at = slice(j * HEAD, (j + 1) * HEAD)
        w = p_ref[m, j]
        r = (w.astype(F32) * t).astype(BF16)
        res.append((mm(r, k_ref[here, at]), mm_tn(q_ref[here, at], r), mm_tn(low, w)))
        t = later
        if j == 1:
            a, b = res[-2:]
            out = [jnp.concatenate([a[0], b[0]], axis=1).astype(BF16)]
            out += [jnp.concatenate([a[k], b[k]], axis=0).T.astype(BF16) for k in (1, 2)]
            spot = pl.ds(pl.multiple_of(step * width + m * LONG, LONG), LONG)
            for k in range(3):
                outs[2 * s][here, k * PAIR:(k + 1) * PAIR] = out[k]
                d_all[spot, (3 * s + k) * PAIR:(3 * s + k + 1) * PAIR] = out[k]

    @pl.when(step == steps - 1)
    def _():
        depth = x_ref.shape[1]
        res = mm_tn(x_all[...], d_all[...]).astype(BF16)
        for s in range(sets):
            grad_ref = outs[2 * s + 1]
            for k in range(3):
                grad_ref[k * depth:(k + 1) * depth] = res[:, (3 * s + k) * PAIR:(3 * s + k + 1) * PAIR]
            cols = [slice((3 * s + k) * PAIR, (3 * s + k + 1) * PAIR) for k in (0, 2)]
            dq, dv = [col_sum(d_all[:, at].astype(F32)) for at in cols]
            small = jnp.concatenate([dq, dv, jnp.zeros((SMALL_PAIR - 2, PAIR), F32)], axis=0)
            grad_ref[3 * depth:] = small.astype(BF16)


def attend_back(place, long_, item, tau, saved, x, quarters):
    n, d = x.shape
    sets = len(quarters)
    group = 2 // sets
    width = group * LONG
    steps = n // width
    col = lambda c: pl.BlockSpec((width, PAIR), lambda i, *_: (i, c))
    S = jax.ShapeDtypeStruct
    rows = 3 * d + SMALL_PAIR
    specs, operands = [], []
    for slot, h in quarters:
        p = saved[slot][-1]
        specs += [col(h)] * 3 + [col(2 * slot + h)] + [col(h)] * 2
        specs += [pl.BlockSpec((group, 2) + p.shape[2:], lambda i, *_, h=h: (i, h, 0, 0))]
        operands += list(saved[slot])
    return pl.pallas_call(
        functools.partial(backward_kernel, sets=sets, steps=steps, group=group),
        grid_spec=pltpu.PrefetchScalarGridSpec(
            num_scalar_prefetch=3,
            grid=(steps,),
            in_specs=[smem()] + specs + [pl.BlockSpec((width, d), lambda i, *_: (i, 0))],
            out_specs=[
                pl.BlockSpec((width, 3 * PAIR), lambda i, *_: (i, 0)),
                pl.BlockSpec((rows, PAIR), lambda i, *_: (0, 0)),
            ]
            * sets,
            scratch_shapes=[pltpu.VMEM((n, d), BF16), pltpu.VMEM((n, sets * 3 * PAIR), BF16)],
        ),
        out_shape=[S((n, 3 * PAIR), BF16), S((rows, PAIR), BF16)] * sets,
        compiler_params=kernel_params(60),
        cost_estimate=cost(8),
        name="attend_back_" + "_".join("%d%d" % q for q in quarters),
    )(place, long_, item, tau, *operands, x)


def input_grad_kernel(place, dh1_ref, ka_ref, sa_ref, near_ref, far_ref, *refs):
    d_refs, (out_ref, w_ref) = refs[:-2], refs[-2:]

    @pl.when(pl.program_id(0) == 0)
    def _():
        for j in range(3):
            for k, ref in enumerate((ka_ref, sa_ref, near_ref, far_ref)):
                lo = (k * 3 + j) * PAIR
                w_ref[:, lo:lo + PAIR] = ref[j]

    d = jnp.concatenate([ref[...] for ref in d_refs], axis=1)
    out_ref[...] = dh1_ref[...] + mm_nt(d, w_ref[...])


def input_grad(place, dh1, weight, near, far, grads):
    n, d = dh1.shape
    tile = 2 * LONG if n % (2 * LONG) == 0 else LONG
    cols = grads[0].shape[1]
    row = lambda c: pl.BlockSpec((tile, c), lambda i, *_: (i, 0))
    pick = lambda h: pl.BlockSpec((3, d, PAIR), lambda i, place: (0, 0, place[0] ^ h), pipeline_mode=pl.Buffered(1))
    return pl.pallas_call(
        input_grad_kernel,
        grid_spec=pltpu.PrefetchScalarGridSpec(
            num_scalar_prefetch=1,
            grid=(n // tile,),
            in_specs=[row(d), pick(0), pick(1), whole(near.shape), whole(far.shape)] + [row(cols)] * 4,
            out_specs=row(d),
            scratch_shapes=[pltpu.VMEM((d, 4 * cols), BF16)],
        ),
        out_shape=jax.ShapeDtypeStruct((n, d), F32),
        compiler_params=kernel_params(60),
        cost_estimate=cost(6),
        name="input_grad",
    )(place, dh1, weight, weight, near, far, *grads)


def flip(v, axis, mask=1):
    size = lax.axis_size(axis)
    return lax.ppermute(v, axis, [(i, i ^ mask) for i in range(size)])


def add_low(*parts):
    return functools.reduce(lambda a, b: a + b, [p.astype(F32) for p in parts]).astype(BF16)


def piece(v, which, rows):
    return lax.dynamic_slice_in_dim(v, which * rows, rows, v.ndim - 2)


def in_order(bit, own, other):
    return jnp.where(bit == 0, jnp.concatenate([own, other]), jnp.concatenate([other, own]))


def row_layer(
    inputs,
    pack_long,
    item_table,
    tau_table,
    delta_table,
    project_weight,
    project_bias,
    merge_weight,
    merge_bias,
    first_gain,
    first_shift,
    expand_weight,
    expand_bias,
    reduce_weight,
    reduce_bias,
    second_gain,
    second_shift,
    grad_output,
):
    n, d = inputs.shape
    hid = expand_weight.shape[1] // 2
    mrows = merge_weight.shape[0] // 2
    core, side = lax.axis_index("core"), lax.axis_index("tensor")
    outer = lax.axis_size("outer")
    y_bit, z_bit = lax.axis_index("outer") % 2, lax.axis_index("outer") // 2 % 2
    place = jnp.stack([core, side * (n // LONG)]).astype(jnp.int32)

    split = project_bias.size
    biases = flip(jnp.concatenate([project_bias.reshape(-1), expand_bias]), "tensor")
    project_near = flip(lax.dynamic_slice_in_dim(project_weight, core * PAIR, PAIR, 2), "tensor")
    rest = jnp.concatenate(
        [
            lax.dynamic_slice_in_dim(expand_weight, core * hid, hid, 1),
            lax.dynamic_slice_in_dim(reduce_weight, core * hid, hid, 0),
            lax.dynamic_slice_in_dim(merge_weight, core * mrows, mrows, 0),
        ],
        axis=0,
    )
    rest_near = flip(rest, "tensor")
    x, biases = lax.optimization_barrier((inputs, biases))

    table = (place, pack_long, item_table, tau_table)
    q0, k0, v0, o0, r0, p0 = attend(
        *table, delta_table, x, project_weight, project_weight, project_bias, True
    )
    project_near, o0 = lax.optimization_barrier((project_near, o0))
    project_far = flip(project_near, "core")
    q1, k1, v1, o1, r1, p1 = attend(
        *table, delta_table, inputs, project_near, project_far, biases[:split].reshape(project_bias.shape), False
    )
    rest_near, o1 = lax.optimization_barrier((rest_near, o1))
    rest_far = flip(rest_near, "core")
    block_output, dh1, grad_att, act, du, n1, dh2, dh1b, sums, sbe, send = feed(
        place, o0, o1, inputs, grad_output, merge_weight, expand_weight, reduce_weight,
        rest_near, rest_far, expand_bias[None], biases[None, split:],
        [v[None] for v in (merge_bias, first_gain, first_shift, reduce_bias, second_gain, second_shift)],
    )
    saved = ((q0, k0, v0, grad_att, o0, r0, p0), (q1, k1, v1, grad_att, o1, r1, p1))
    back = lambda x, *quarters: attend_back(*table, saved, x, quarters)

    got = flip(send, "core")
    keep = feed_grad(place, act, du, n1, dh2, dh1b, o0, o1, sums, sbe)
    got, keep = lax.optimization_barrier((got, keep))
    part = keep.shape[1] // 2
    half = part // 2
    a, b = (keep[:, :part], got[:, :part]), (keep[:, part:], got[:, part:])
    a_x = add_low(a[0][1], a[1][1])
    b_y = add_low(*(piece(v, 1 - y_bit, half) for v in b))
    x, a_x, b_y = lax.optimization_barrier((inputs, a_x, b_y))
    a_x, b_y = flip(a_x, "tensor"), flip(b_y, "outer", 1)
    d01, g01, d11, g11 = back(x, (0, 1), (1, 1))
    got01, got11 = flip(g01, "core"), flip(g11, "core")
    a_x, b_y, d11 = lax.optimization_barrier((a_x, b_y, d11))
    a = add_low(a[0][0], a[1][0], a_x)
    b = add_low(*(piece(v, y_bit, half) for v in b), b_y)
    a_y, b_x = piece(a, 1 - y_bit, half), b[1]
    x, a_y, b_x = lax.optimization_barrier((x, a_y, b_x))
    a_y, b_x = flip(a_y, "outer", 1), flip(b_x, "tensor")
    d10, g10 = back(x, (1, 0))
    a_y, b_x, d10 = lax.optimization_barrier((a_y, b_x, d10))
    far = add_low(g10, got11)
    total = jnp.concatenate([add_low(piece(a, y_bit, half), a_y), add_low(b[0], b_x)])
    to_z = piece(total, 1 - z_bit, half)
    x, far, to_z = lax.optimization_barrier((x, far, to_z))
    far, to_z = flip(far, "tensor"), flip(to_z, "outer", 2)
    d00, g00 = back(x, (0, 0))
    far, to_z, d00 = lax.optimization_barrier((far, to_z, d00))
    feed_part = add_low(piece(total, z_bit, half), to_z)

    mine = add_low(g00, got01, far)
    rows = mine.shape[0] // 2
    to_y = flip(piece(mine, 1 - y_bit, rows), "outer", 1)
    if outer > 4:
        came = flip(feed_part, "outer", 4)
    project_part = add_low(piece(mine, y_bit, rows), to_y)
    to_z = flip(project_part, "outer", 2)
    d00, project_part = lax.optimization_barrier((d00, project_part))
    dx = input_grad(place, dh1, project_weight, project_near, project_far, (d00, d01, d10, d11))
    if outer > 4:
        came, to_z, dx = lax.optimization_barrier((came, to_z, dx))
        feed_part = add_low(feed_part, came)
    project_part = add_low(project_part, to_z)
    by_y, by_z = flip(feed_part, "outer", 1), flip(feed_part, "outer", 2)
    if outer > 4:
        project_part = add_low(project_part, flip(project_part, "outer", 4))
    mid = half // 2
    cross = jnp.concatenate([flip(by_z[:mid], "outer", 1), flip(by_y[mid:], "outer", 2)])
    project_total = in_order(y_bit, project_part, flip(project_part, "outer", 1))
    same = in_order(z_bit, feed_part, by_z)
    other = in_order(z_bit, by_y, cross)
    total = jnp.concatenate(
        [in_order(y_bit, same[:half], other[:half]), in_order(y_bit, same[half:], other[half:])]
    )
    feed_sum = in_order(core, total[None], flip(total, "core")[None]).astype(F32)
    project_sum = in_order(core, project_total[None], flip(project_total, "core")[None]).astype(F32)

    weight = project_sum[:, : 3 * d].reshape(2, 3, d, PAIR)
    small = feed_sum[:, hid + d + mrows :]
    return (
        block_output,
        dx,
        jnp.concatenate([weight[0], weight[1]], axis=-1),
        jnp.concatenate([project_sum[0, 3 * d : 3 * d + 2], project_sum[1, 3 * d : 3 * d + 2]], axis=-1),
        feed_sum[:, hid + d : hid + d + mrows].reshape(2 * mrows, d),
        small[0, 1],
        small[0, 2],
        small[0, 3],
        jnp.concatenate([feed_sum[0, hid : hid + d], feed_sum[1, hid : hid + d]], axis=1),
        small[:, 0].reshape(-1),
        feed_sum[:, :hid].reshape(2 * hid, d),
        small[1, 1],
        small[1, 2],
        small[1, 3],
    )


def rows_fit(mesh):
    size = mesh.shape["dp"]
    return mesh.shape["tensor"] == 2 and size in (8, 16)


def solution(mesh):
    if rows_fit(mesh):
        mesh = Mesh(mesh.devices.reshape(-1, 2, 2), ("outer", "core", "tensor"))
        body, dp = row_layer, ("outer", "core")
    else:
        body, dp = split_layer, ("dp",)
    all_ = P(dp + ("tensor",), None)
    placed = (
        all_,
        P(dp),
        P(dp),
        P(),
        P(),
        P(None, None, "tensor"),
        P(None, "tensor"),
        P("tensor", None),
        P(),
        P(),
        P(),
        P(None, "tensor"),
        P("tensor"),
        P("tensor", None),
        P(),
        P(),
        P(),
        all_,
    )
    return jax.shard_map(
        body,
        mesh=mesh,
        in_specs=placed,
        out_specs=(
            all_,
            all_,
            P(None, None, "tensor"),
            P(None, "tensor"),
            P("tensor", None),
            P(),
            P(),
            P(),
            P(None, "tensor"),
            P("tensor"),
            P("tensor", None),
            P(),
            P(),
            P(),
        ),
        check_vma=False,
    )
```

```python
import functools
import jax
import jax.numpy as jnp
from jax import lax
from jax.experimental import pallas as pl
from jax.experimental.pallas import tpu as pltpu
from jax.sharding import Mesh, PartitionSpec as P

HEAD = 64
SHORT = 96
LONG = 384
TABLE = 64
PAIR = 2 * HEAD
SMALL = 128
SMALL_PAIR = 32
BIAS_ROWS = 64
LOG2E = 1.4426950408889634
F32 = jnp.float32
BF16 = jnp.bfloat16


def layer_norm(values, gain, shift):
    mean = jnp.mean(values, axis=-1, keepdims=True)
    centred = values - mean
    spread = jnp.mean(centred * centred, axis=-1, keepdims=True)
    return centred * lax.rsqrt(spread + 1e-05) * gain + shift


def exact_gelu(values):
    return jax.nn.gelu(values, approximate=False)


def describe(pack_long, item_table, tau_table, delta_table):
    packs = pack_long.shape[0]
    per = LONG // SHORT
    count = packs * LONG
    longer = jnp.broadcast_to(pack_long[:, None] == 1, (packs, LONG)).reshape(count)
    lead_row = jnp.broadcast_to(item_table.reshape(packs, per)[:, :1], (packs, LONG)).reshape(count)
    each_row = jnp.broadcast_to(item_table[:, None], (packs * per, SHORT)).reshape(count)
    table_row = jnp.where(longer, lead_row, each_row)
    places = jnp.arange(count, dtype=jnp.int32)
    position = jnp.where(longer, places % LONG, places % SHORT)
    segment = jnp.where(longer, places // LONG * per, places // SHORT)
    picker = (table_row[:, None] == jnp.arange(TABLE, dtype=jnp.int32)[None, :]).astype(jnp.float32)
    tau_row = jnp.sum(picker * tau_table[None, :], axis=1)
    picked = jnp.dot(
        picker, delta_table, precision=lax.Precision.HIGHEST, preferred_element_type=jnp.float32
    )
    placed = position[:, None] == jnp.arange(LONG, dtype=jnp.int32)[None, :]
    delta_row = jnp.sum(jnp.where(placed, picked, 0.0), axis=1)
    return (tau_row, delta_row, segment)


def project(rows_all, project_weight, project_bias):
    query = (
        jnp.dot(rows_all, project_weight[0], preferred_element_type=jnp.float32) + project_bias[0]
    ).astype(jnp.bfloat16)
    keys = jnp.dot(rows_all, project_weight[1], preferred_element_type=jnp.float32).astype(
        jnp.bfloat16
    )
    values = (
        jnp.dot(rows_all, project_weight[2], preferred_element_type=jnp.float32) + project_bias[1]
    ).astype(jnp.bfloat16)
    return (query, keys, values)


def split_blocks(arrays):
    width = 2 * LONG
    return tuple((a.reshape((a.shape[0] // width, width) + a.shape[1:]) for a in arrays))


def block_scores(block_q, block_k, block_tau, block_delta, block_seg):
    raw = jnp.einsum("qhd,khd->hqk", block_q, block_k, preferred_element_type=jnp.float32)
    scores = (block_tau[None, :, None] * raw + block_delta[None, None, :]) * HEAD ** (-0.5)
    same = block_seg[:, None] == block_seg[None, :]
    return jnp.where(same[None], scores, -1e30)


def attend_forward(query, keys, values, tau_row, delta_row, segment):
    heads = query.shape[1] // HEAD
    shaped = tuple((a.reshape(a.shape[0], heads, HEAD) for a in (query, keys, values)))

    def one_block(parts):
        block_q, block_k, block_v, block_tau, block_delta, block_seg = parts
        scores = block_scores(block_q, block_k, block_tau, block_delta, block_seg)
        top = jnp.max(scores, axis=-1, keepdims=True)
        expo = jnp.exp(scores - top)
        totals = jnp.sum(expo, axis=-1, keepdims=True)
        weights = (expo / totals).astype(jnp.bfloat16)
        mixed = jnp.einsum("hqk,khd->qhd", weights, block_v, preferred_element_type=jnp.float32)
        return (
            mixed.reshape(mixed.shape[0], heads * HEAD).astype(jnp.bfloat16),
            top + jnp.log(totals),
        )

    attended, logsum = lax.map(one_block, split_blocks(shaped + (tau_row, delta_row, segment)))
    return (attended.reshape(query.shape), logsum)


def attend_backward(query, keys, values, grad_att, logsum, tau_row, delta_row, segment):
    heads = query.shape[1] // HEAD
    shaped = tuple((a.reshape(a.shape[0], heads, HEAD) for a in (query, keys, values, grad_att)))
    blocked = split_blocks(shaped + (tau_row, delta_row, segment))

    def one_block(parts):
        block_q, block_k, block_v, block_g, block_lse, block_tau, block_delta, block_seg = parts
        scores = block_scores(block_q, block_k, block_tau, block_delta, block_seg)
        probs = jnp.exp(scores - block_lse)
        dprob = jnp.einsum("qhd,khd->hqk", block_g, block_v, preferred_element_type=jnp.float32)
        dscore = probs * (dprob - jnp.sum(dprob * probs, axis=-1, keepdims=True))
        lowered = (dscore * HEAD ** (-0.5) * block_tau[None, :, None]).astype(jnp.bfloat16)
        grad_q = jnp.einsum("hqk,khd->qhd", lowered, block_k, preferred_element_type=jnp.float32)
        grad_k = jnp.einsum("hqk,qhd->khd", lowered, block_q, preferred_element_type=jnp.float32)
        grad_v = jnp.einsum(
            "hqk,qhd->khd", probs.astype(jnp.bfloat16), block_g, preferred_element_type=jnp.float32
        )
        width = block_q.shape[0]
        return tuple(
            (g.reshape(width, heads * HEAD).astype(jnp.bfloat16) for g in (grad_q, grad_k, grad_v))
        )

    grads = lax.map(one_block, blocked[:4] + (logsum,) + blocked[4:])
    return tuple((g.reshape(query.shape) for g in grads))


def row_term(left, right, form):
    return jnp.einsum(form, left, right, preferred_element_type=jnp.float32)


def feed_backward(feed_rows, preact_rows, active_rows, grad_fed, reduce_matrix):
    grad_reduce_weight = jnp.einsum(
        "tf,td->fd", active_rows, grad_fed, preferred_element_type=jnp.float32
    )
    grad_active = jnp.einsum(
        "td,fd->tf", grad_fed, reduce_matrix, preferred_element_type=jnp.float32
    )
    grad_preact = jax.vjp(exact_gelu, preact_rows)[1](grad_active)[0].astype(jnp.bfloat16)
    grad_expand_bias = jnp.sum(grad_preact.astype(jnp.float32), axis=0)
    grad_expand_weight = jnp.einsum(
        "td,tf->df", feed_rows, grad_preact, preferred_element_type=jnp.float32
    )
    return (grad_reduce_weight, grad_preact, grad_expand_bias, grad_expand_weight)


def split_layer(
    inputs,
    pack_long,
    item_table,
    tau_table,
    delta_table,
    project_weight,
    project_bias,
    merge_weight,
    merge_bias,
    first_gain,
    first_shift,
    expand_weight,
    expand_bias,
    reduce_weight,
    reduce_bias,
    second_gain,
    second_shift,
    grad_output,
):
    tau_row, delta_row, segment = describe(pack_long, item_table, tau_table, delta_table)
    rows_all = lax.all_gather(inputs, "tensor", axis=0, tiled=True)
    query, keys, values = project(rows_all, project_weight, project_bias)
    attended, logsum = attend_forward(query, keys, values, tau_row, delta_row, segment)
    mixed_part = lax.psum_scatter(
        row_term(attended, merge_weight, "tc,cd->td"), "tensor", scatter_dimension=0, tiled=True
    )
    first_sum = inputs.astype(jnp.float32) + (mixed_part + merge_bias)
    normed, first_back = jax.vjp(layer_norm, first_sum, first_gain, first_shift)
    normed_low = normed.astype(jnp.bfloat16)
    feed_all = lax.all_gather(normed_low, "tensor", axis=0, tiled=True)
    preact = jnp.dot(feed_all, expand_weight, preferred_element_type=jnp.float32) + expand_bias
    active = exact_gelu(preact).astype(jnp.bfloat16)
    fed_part = lax.psum_scatter(
        row_term(active, reduce_weight, "tf,fd->td"), "tensor", scatter_dimension=0, tiled=True
    )
    second_sum = normed + (fed_part + reduce_bias)
    block_output, second_back = jax.vjp(layer_norm, second_sum, second_gain, second_shift)
    grad_second, grad_gain_b, grad_shift_b = second_back(grad_output.astype(jnp.float32))
    grad_reduce_bias = jnp.sum(grad_second, axis=0)
    grad_fed = lax.all_gather(grad_second.astype(jnp.bfloat16), "tensor", axis=0, tiled=True)
    feed_again = lax.all_gather(normed_low, "tensor", axis=0, tiled=True)
    preact_again = (
        jnp.dot(feed_again, expand_weight, preferred_element_type=jnp.float32) + expand_bias
    )
    active_again = exact_gelu(preact_again).astype(jnp.bfloat16)
    grad_reduce_weight, grad_preact, grad_expand_bias, grad_expand_weight = feed_backward(
        feed_again, preact_again, active_again, grad_fed, reduce_weight
    )
    grad_normed = grad_second + lax.psum_scatter(
        row_term(grad_preact, expand_weight, "tf,df->td"), "tensor", scatter_dimension=0, tiled=True
    )
    grad_first, grad_gain_a, grad_shift_a = first_back(grad_normed)
    grad_merge_bias = jnp.sum(grad_first, axis=0)
    grad_att = lax.all_gather(grad_first.astype(jnp.bfloat16), "tensor", axis=0, tiled=True)
    grad_merge_weight = jnp.einsum(
        "tc,td->cd", attended, grad_att, preferred_element_type=jnp.float32
    )
    grad_attended = jnp.einsum(
        "td,cd->tc", grad_att, merge_weight, preferred_element_type=jnp.float32
    ).astype(jnp.bfloat16)
    rows_again = lax.all_gather(inputs, "tensor", axis=0, tiled=True)
    query_again, keys_again, values_again = project(rows_again, project_weight, project_bias)
    grad_q, grad_k, grad_v = attend_backward(
        query_again, keys_again, values_again, grad_attended, logsum, tau_row, delta_row, segment
    )
    grad_stack = jnp.stack((grad_q, grad_k, grad_v), axis=1)
    grad_project_weight = jnp.einsum(
        "td,tjc->jdc", rows_again, grad_stack, preferred_element_type=jnp.float32
    )
    grad_project_bias = jnp.stack(
        (jnp.sum(grad_q.astype(jnp.float32), axis=0), jnp.sum(grad_v.astype(jnp.float32), axis=0))
    )
    input_grad = grad_first + lax.psum_scatter(
        row_term(grad_stack, project_weight, "tjc,jdc->td").astype(jnp.bfloat16),
        "tensor",
        scatter_dimension=0,
        tiled=True,
    ).astype(jnp.float32)
    summed_all = (
        lax.psum(grad_project_weight.astype(jnp.bfloat16), "dp").astype(jnp.float32),
        lax.psum(grad_project_bias.astype(jnp.bfloat16), "dp").astype(jnp.float32),
        lax.psum(grad_merge_weight.astype(jnp.bfloat16), "dp").astype(jnp.float32),
        lax.psum(grad_expand_weight.astype(jnp.bfloat16), "dp").astype(jnp.float32),
        lax.psum(grad_expand_bias.astype(jnp.bfloat16), "dp").astype(jnp.float32),
        lax.psum(grad_reduce_weight.astype(jnp.bfloat16), "dp").astype(jnp.float32),
    )
    summed_attention = summed_all[:3]
    summed_feed = summed_all[3:]
    small = lax.psum(
        (grad_merge_bias, grad_gain_a, grad_shift_a, grad_reduce_bias, grad_gain_b, grad_shift_b),
        ("dp", "tensor"),
    )
    return (
        block_output,
        input_grad,
        summed_attention[0],
        summed_attention[1],
        summed_attention[2],
        small[0],
        small[1],
        small[2],
        summed_feed[0],
        summed_feed[1],
        summed_feed[2],
        small[3],
        small[4],
        small[5],
    )


def mm(a, b):
    return lax.dot_general(a, b, (((1,), (0,)), ((), ())), preferred_element_type=F32)


def mm_nt(a, b):
    return lax.dot_general(a, b, (((1,), (1,)), ((), ())), preferred_element_type=F32)


def mm_tn(a, b):
    return lax.dot_general(a, b, (((0,), (0,)), ((), ())), preferred_element_type=F32)


def col_sum(v):
    return jnp.sum(v, axis=0, keepdims=True)


def row_mean(v):
    return jnp.mean(v, axis=1, keepdims=True)


def pack_rows(pack, long_ref, item_ref):
    per = LONG // SHORT
    longer = long_ref[pack] == 1
    rows = [jnp.where(longer, item_ref[pack * per], item_ref[pack * per + k]) for k in range(per)]
    return longer, rows


def pack_tau(rows, tau_ref):
    slot = lax.broadcasted_iota(jnp.int32, (LONG, 1), 0) // SHORT
    tau = jnp.full((LONG, 1), tau_ref[rows[0]], F32)
    for k in range(1, LONG // SHORT):
        tau = jnp.where(slot == k, tau_ref[rows[k]], tau)
    return tau


def pack_bias(longer, rows, delta_ref):
    slot_r = lax.broadcasted_iota(jnp.int32, (LONG, 1), 0) // SHORT
    slot_c = lax.broadcasted_iota(jnp.int32, (1, LONG), 1) // SHORT
    shift = delta_ref[pl.ds(rows[0], 1), :]
    for k in range(1, LONG // SHORT):
        piece = jnp.broadcast_to(delta_ref[pl.ds(rows[k], 1), :], (8, LONG))
        piece = pltpu.roll(piece, SHORT * k, 1)[0:1]
        shift = jnp.where(jnp.logical_and(jnp.logical_not(longer), slot_c == k), piece, shift)
    mask = jnp.logical_or(longer, slot_r == slot_c)
    return jnp.where(mask, shift * (HEAD**-0.5 * LOG2E), -1e30)


def forward_kernel(
    place, long_ref, item_ref, tau_ref, delta_ref, x_ref, wa_ref, wb_ref, ba_ref, bb_ref, *refs, own,
):
    step = pl.program_id(0)
    if own:
        q_ref, k_ref, v_ref, o_ref, r_ref, p_ref, w_ref, bias_ref = refs
    else:
        o0_ref, mk_ref, ms_ref, bm_ref = refs[:4]
        q_ref, k_ref, v_ref, o_ref, r_ref, p_ref, xh_ref, rs_ref, w_ref, bias_ref, wm_ref = refs[4:]

    @pl.when(step == 0)
    def _():
        if not own:
            merge_rows(wm_ref, mk_ref, ms_ref, wa_ref.at[3 * x_ref.shape[1]:], wb_ref.at[3 * x_ref.shape[1]:])
        for k, ref in enumerate((wa_ref, wb_ref)):
            for j in range(3):
                w_ref[j, :, k * PAIR:(k + 1) * PAIR] = projection(ref, j, x_ref.shape[1])

    longer, rows = pack_rows(step + place[1], long_ref, item_ref)
    bias_ref[...] = pack_bias(longer, rows, delta_ref)
    tau = pack_tau(rows, tau_ref) * (HEAD**-0.5 * LOG2E)
    x = x_ref[...]
    if own:
        q_bias, v_bias = [jnp.concatenate([ba_ref[j:j + 1], bb_ref[j:j + 1]], axis=1) for j in range(2)]
    else:
        b = joined_rows(ba_ref[...])
        q_bias, v_bias = [
            jnp.where(
                place[0] == 0,
                jnp.concatenate([b[k:k + 1], b[k + 1:k + 2]], axis=1),
                jnp.concatenate([b[k + 1:k + 2], b[k:k + 1]], axis=1),
            )
            for k in (0, 2)
        ]
    q = (mm(x, w_ref[0]) + q_bias).astype(BF16)
    k = mm(x, w_ref[1]).astype(BF16)
    v = (mm(x, w_ref[2]) + v_bias).astype(BF16)
    q_ref[...] = q
    k_ref[...] = k
    v_ref[...] = v
    scaled = (q.astype(F32) * tau).astype(BF16)
    vf = v.astype(F32)
    first = lax.broadcasted_iota(jnp.int32, (1, PAIR), 1) < HEAD
    heads = q.shape[1] // HEAD

    def score(h):
        at = slice(h * HEAD, (h + 1) * HEAD)
        return mm_nt(scaled[:, at], k[:, at])

    def soften(s):
        s = s + bias_ref[...]
        return jnp.exp2(s - jnp.max(s, axis=1, keepdims=True)).astype(BF16)

    mixed = []

    def mix(h, w):
        p_ref[0, h] = w
        at = slice(h // 2 * PAIR, (h // 2 + 1) * PAIR)
        own = first if h % 2 == 0 else jnp.logical_not(first)
        mixed.append(mm(w, jnp.where(own, vf[:, at], 1.0).astype(BF16)))
        if h % 2 == 1:
            a, b = mixed[-2:]
            r = 1.0 / pltpu.roll(jnp.where(first, b, a), HEAD, 1)
            r_ref[:, at] = r
            o_ref[:, at] = (jnp.where(first, a, b) * r).astype(BF16)

    s = score(0)
    held = None
    for h in range(heads):
        later = score(h + 1) if h + 1 < heads else None
        w = soften(s)
        if held is not None:
            mix(h - 1, held)
        held, s = w, later
    mix(heads - 1, held)
    if not own:
        half = wm_ref.shape[0] // 2
        mixed = mm(o0_ref[...], wm_ref[:half]) + mm(o_ref[...], wm_ref[half:])
        h1 = x.astype(F32) + (mixed + bm_ref[...])
        c = h1 - row_mean(h1)
        rs = lax.rsqrt(row_mean(c * c) + 1e-05)
        xh_ref[...] = c * rs
        rs_ref[...] = jnp.broadcast_to(rs, rs_ref.shape)


def merge_rows(out_ref, keep_ref, other_ref, near_ref, far_ref):
    rows = keep_ref.shape[0]
    out_ref[0:rows] = keep_ref[...]
    out_ref[rows:2 * rows] = other_ref[...]
    for m, ref in ((2, near_ref), (3, far_ref)):
        for k in range(out_ref.shape[1] // PAIR):
            out_ref[m * rows:(m + 1) * rows, k * PAIR:(k + 1) * PAIR] = ref[k * rows:(k + 1) * rows]


def whole(shape):
    return pl.BlockSpec(shape, lambda *_: (0,) * len(shape), pipeline_mode=pl.Buffered(1))


def smem():
    return pl.BlockSpec(memory_space=pltpu.SMEM)


def kernel_params(mib):
    return pltpu.CompilerParams(vmem_limit_bytes=mib * 2**20)


def cost(us):
    return pl.CostEstimate(flops=int(us * 1.0e6), bytes_accessed=0, transcendentals=0)


def projection(ref, j, d):
    return ref[j] if len(ref.shape) == 3 else ref[j * d:(j + 1) * d]


def bias_block(d):
    return pl.BlockSpec((BIAS_ROWS, PAIR), lambda *_: (4 * d // BIAS_ROWS, 0), pipeline_mode=pl.Buffered(1))


def attend(place, long_, item, tau, delta, x, wa, wb, bias, own, o0=None, merge=None, merge_bias=None):
    n, d = x.shape
    packs = n // LONG
    cols = 2 * PAIR
    row = lambda c: pl.BlockSpec((LONG, c), lambda i, *_: (i, 0))
    if own:
        weights = [
            pl.BlockSpec((3, d, PAIR), lambda i, place, *_, h=h: (0, 0, place[0] ^ h), pipeline_mode=pl.Buffered(1))
            for h in (0, 1)
        ]
        biases = [pl.BlockSpec((2, PAIR), lambda i, place, *_, h=h: (0, place[0] ^ h)) for h in (0, 1)]
    else:
        weights, biases = [whole(wa.shape), whole(wb.shape)], [bias_block(d)] * 2
    out = jax.ShapeDtypeStruct((n, cols), BF16)
    heads = cols // HEAD
    more_in, more_out, more_shapes, more_scratch, more = [], [], [], [], []
    if not own:
        mrows = merge.shape[0] // 2
        more_in = [row(cols)]
        more_in += [
            pl.BlockSpec((mrows, d), lambda i, place, *_, h=h: (place[0] ^ h, 0), pipeline_mode=pl.Buffered(1))
            for h in (0, 1)
        ]
        more_in += [whole((1, d))]
        more_out = [row(d), row(PAIR)]
        more_shapes = [jax.ShapeDtypeStruct((n, d), F32), jax.ShapeDtypeStruct((n, PAIR), F32)]
        more_scratch = [pltpu.VMEM((4 * mrows, d), BF16)]
        more = [o0, merge, merge, merge_bias]
    return pl.pallas_call(
        functools.partial(forward_kernel, own=own),
        grid_spec=pltpu.PrefetchScalarGridSpec(
            num_scalar_prefetch=3,
            grid=(packs,),
            in_specs=[smem(), whole(delta.shape), row(d)]
            + weights
            + biases
            + more_in,
            out_specs=[row(cols)] * 5
            + [pl.BlockSpec((1, heads, LONG, LONG), lambda i, *_: (i, 0, 0, 0))]
            + more_out,
            scratch_shapes=[pltpu.VMEM((3, d, cols), BF16), pltpu.VMEM((LONG, LONG), F32)] + more_scratch,
        ),
        out_shape=[out] * 4
        + [
            jax.ShapeDtypeStruct((n, cols), F32),
            jax.ShapeDtypeStruct((packs, heads, LONG, LONG), BF16),
        ]
        + more_shapes,
        compiler_params=kernel_params(63),
        cost_estimate=cost(1 if own else 4000),
        name="attend_own" if own else "attend_other",
    )(place, long_, item, tau, delta, x, wa, wb, bias, bias, *more)


def gelu_parts(u):
    phi = 0.5 + 0.5 * lax.erf(u * 0.7071067811865476)
    return phi, jnp.exp2(u * u * (-0.5 * LOG2E))


def feed_kernel(
    place, o0_ref, o1_ref, xh_ref, rs1_ref, gy_ref, mk_ref, ms_ref, mnear_ref, mfar_ref,
    ek_ref, es_ref, rk_ref, rs_ref,
    near_ref, far_ref, b0_ref, b1_ref, b2_ref, g1_ref, h1_ref, br_ref, g2_ref, h2_ref,
    out_ref, do_ref, act_ref, du_ref, n1_ref, dh2_ref, dh1b_ref, sum_ref, sbe_ref, send_ref,
    wm_ref, act_all, du_all, gp_ref, n1_all, dh2_all, dh1b_all, o_all, *, tiles, tile,
):
    step = pl.program_id(0)
    d = xh_ref.shape[1]
    hid = ek_ref.shape[1]
    mrows = mk_ref.shape[0]
    expand = (ek_ref, es_ref, near_ref.at[0:d], far_ref.at[0:d])
    reduce_ = (rk_ref, rs_ref, near_ref.at[d:d + hid], far_ref.at[d:d + hid])

    @pl.when(step == 0)
    def _():
        merge_rows(wm_ref, mk_ref, ms_ref, mnear_ref, mfar_ref)

    @pl.when(step < tiles)
    def _():
        here = pl.ds(pl.multiple_of(step * tile, tile), tile)
        g1, b1, br, g2, b2 = [ref[...] for ref in (g1_ref, h1_ref, br_ref, g2_ref, h2_ref)]
        b = joined_rows(b2_ref[...])
        wide = hid // PAIR
        parts = [
            jnp.concatenate([b[4 + wide * k + m:5 + wide * k + m] for m in range(wide)], axis=1) for k in range(2)
        ]
        first = place[0] == 0
        be = [b0_ref[...], b1_ref[...], jnp.where(first, *parts), jnp.where(first, *parts[::-1])]
        o_all[here, :mrows] = o0_ref[...]
        o_all[here, mrows:] = o1_ref[...]
        xh, rs = xh_ref[...], rs1_ref[:, 0:1]
        n1 = xh * g1 + b1
        low = n1.astype(BF16)
        n1_ref[...] = low
        n1_all[here] = low
        u = mm(low, expand[0][...])
        fed = n1 + br
        for k in range(4):
            later = mm(low, expand[k + 1][...]) if k < 3 else None
            at = slice(k * hid, (k + 1) * hid)
            u = u + be[k]
            phi, e = gelu_parts(u)
            act = (u * phi).astype(BF16)
            mine = slice(k // 2 * hid, (k // 2 + 1) * hid)
            if k % 2 == 0:
                act_ref[:, mine] = act
            else:
                act_all[here, mine] = act
            gp_ref[:, at] = (phi + u * (e * 0.3989422804014327)).astype(BF16)
            fed = fed + mm(act, reduce_[k][...])
            u = later
        c2 = fed - row_mean(fed)
        rs2 = lax.rsqrt(row_mean(c2 * c2) + 1e-05)
        xh2 = c2 * rs2
        out_ref[...] = xh2 * g2 + b2
        gy = gy_ref[...].astype(F32)
        gg = gy * g2
        dh2 = rs2 * ((gg - row_mean(gg)) - xh2 * row_mean(gg * xh2))
        dh2b = dh2.astype(BF16)
        dh2_ref[...] = dh2b
        dh2_all[here] = dh2b
        dn = dh2
        sbe = []
        da = mm_nt(dh2b, reduce_[0][...])
        for k in range(4):
            later = mm_nt(dh2b, reduce_[k + 1][...]) if k < 3 else None
            at = slice(k * hid, (k + 1) * hid)
            du = (da * gp_ref[:, at].astype(F32)).astype(BF16)
            mine = slice(k // 2 * hid, (k // 2 + 1) * hid)
            if k % 2 == 0:
                du_ref[:, mine] = du
            else:
                du_all[here, mine] = du
            sbe.append(col_sum(du.astype(F32)))
            dn = dn + mm_nt(du, expand[k][...])
            da = later
        gg1 = dn * g1
        dh1 = rs * ((gg1 - row_mean(gg1)) - xh * row_mean(gg1 * xh))
        dh1b = dh1.astype(BF16)
        dh1b_ref[...] = dh1b
        dh1b_all[here] = dh1b
        do_ref[...] = mm_nt(dh1b, wm_ref[...]).astype(BF16)
        sums = [col_sum(dh1), col_sum(dn * xh), col_sum(dn), col_sum(dh2), col_sum(gy * xh2), col_sum(gy)]
        sums = jnp.concatenate(sums + [jnp.zeros((2, d), F32)], axis=0)
        sbe = jnp.broadcast_to(jnp.concatenate(sbe, axis=1), sbe_ref.shape)

        @pl.when(step == 0)
        def _():
            sum_ref[...] = sums
            sbe_ref[...] = sbe

        @pl.when(step > 0)
        def _():
            sum_ref[...] += sums
            sbe_ref[...] += sbe

    for slot in range(2):

        @pl.when(step == tiles + slot)
        def _(slot=slot):
            at = slice(slot * hid, (slot + 1) * hid)
            om = slice(slot * mrows, (slot + 1) * mrows)
            send_ref[0, 0:hid] = mm_tn(act_all[:, at], dh2_all[...]).astype(BF16)
            send_ref[0, hid:hid + d] = mm_tn(n1_all[...], du_all[:, at]).astype(BF16)
            rows = hid + d + mrows
            send_ref[0, hid + d:rows] = mm_tn(o_all[:, om], dh1b_all[...]).astype(BF16)
            send_ref[0, rows:] = small_rows(place[0] ^ 1, sum_ref[...], sbe_ref[...], slot, 1, hid)


def small_rows(which, sums, sbe, slot, h, hid):
    lo = (2 * slot + h) * hid
    part = jnp.where(which == 0, sums[0:3], sums[3:6])
    fill = jnp.zeros((SMALL - 4, sums.shape[1]), F32)
    return jnp.concatenate([sbe[0:1, lo:lo + hid], part, fill], axis=0).astype(BF16)


def feed(place, o0, o1, xh, rs1, gy, merge, mnear, mfar, expand, reduce_, near, far, be0, be1, vecs):
    n, d = xh.shape
    tile = 2 * LONG
    tiles = n // tile
    mrows, hid = merge.shape[0] // 2, expand.shape[1] // 2
    full_hid = 4 * hid
    at = lambda i: jnp.minimum(i, tiles - 1)
    row = lambda c: pl.BlockSpec((tile, c), lambda i, *_: (at(i), 0))
    once = pl.Buffered(1)
    by_row = lambda shape, h: pl.BlockSpec(shape, lambda i, place: (place[0] ^ h, 0), pipeline_mode=once)
    by_col = lambda shape, h: pl.BlockSpec(shape, lambda i, place: (0, place[0] ^ h), pipeline_mode=once)
    S = jax.ShapeDtypeStruct
    grows = hid + d + mrows + SMALL
    bias = lambda h: pl.BlockSpec((1, hid), lambda i, place: (0, place[0] ^ h), pipeline_mode=once)
    return pl.pallas_call(
        functools.partial(feed_kernel, tiles=tiles, tile=tile),
        grid_spec=pltpu.PrefetchScalarGridSpec(
            num_scalar_prefetch=1,
            grid=(tiles + 2,),
            in_specs=[pl.BlockSpec((tile, mrows), lambda i, *_: (at(i), 1))] * 2
            + [row(d), row(rs1.shape[1]), row(d)]
            + [by_row((mrows, d), h) for h in (0, 1)]
            + [pl.BlockSpec((d, PAIR), lambda *_: (3, 0), pipeline_mode=once)] * 2
            + [by_col((d, hid), h) for h in (0, 1)]
            + [by_row((hid, d), h) for h in (0, 1)]
            + [whole(near.shape), whole(far.shape)]
            + [bias(0), bias(1), bias_block(d)]
            + [whole((1, d))] * 5,
            out_specs=[row(d), row(d), row(2 * hid), row(2 * hid), row(d), row(d), row(d)]
            + [
                pl.BlockSpec((8, d), lambda i, *_: (0, 0)),
                pl.BlockSpec((8, full_hid), lambda i, *_: (0, 0)),
                pl.BlockSpec((1, grows, d), lambda i, *_: (jnp.maximum(i - tiles, 0), 0, 0)),
            ],
            scratch_shapes=[
                pltpu.VMEM((4 * mrows, d), BF16),
                pltpu.VMEM((n, 2 * hid), BF16),
                pltpu.VMEM((n, 2 * hid), BF16),
                pltpu.VMEM((tile, full_hid), BF16),
                pltpu.VMEM((n, d), BF16),
                pltpu.VMEM((n, d), BF16),
                pltpu.VMEM((n, d), BF16),
                pltpu.VMEM((n, 2 * mrows), BF16),
            ],
        ),
        out_shape=[S((n, d), F32), S((n, d), BF16)]
        + [S((n, 2 * hid), BF16)] * 2
        + [S((n, d), BF16)] * 3
        + [S((8, d), F32), S((8, full_hid), F32), S((2, grows, d), BF16)],
        compiler_params=kernel_params(63),
        cost_estimate=cost(60),
        name="feed",
    )(
        place, o0, o1, xh, rs1, gy, merge, merge, mnear, mfar, expand, expand, reduce_, reduce_,
        near, far, be0, be0, be1, *vecs,
    )


def feed_grad_kernel(
    place, act_hbm, du_hbm, n1_hbm, dh2_hbm, dh1b_hbm, o0_hbm, o1_hbm, sum_ref, sbe_ref, keep_hbm,
    act, du, n1, dh2, dh1b, o, keep, sems, out_sems,
):
    hid, d, mrows = act.shape[2], n1.shape[1], o.shape[2]

    def fetch(src, dst, k):
        copy = pltpu.make_async_copy(src, dst, sems.at[k])
        copy.start()
        return copy

    cols = lambda s: (slice(None), pl.ds(s * hid, hid))
    heads = lambda ref: ref.at[:, pl.ds(0, mrows)]
    third = n1.shape[0] // 3
    parts = [pl.ds(k * third, third) for k in range(3)]
    order = tuple(
        pair
        for p in parts
        for pair in ((act_hbm.at[p, pl.ds(hid, hid)], act.at[1, p]), (dh2_hbm.at[p], dh2.at[p]))
    ) + (
        (n1_hbm, n1), (du_hbm.at[cols(1)], du.at[1]),
        (heads(o1_hbm), o.at[1]), (dh1b_hbm, dh1b),
        (act_hbm.at[cols(0)], act.at[0]), (du_hbm.at[cols(0)], du.at[0]), (heads(o0_hbm), o.at[0]),
    )
    copies = [fetch(src, dst, k) for k, (src, dst) in enumerate(order)]
    flush = []
    rows = hid + d + mrows
    for slot, waits in ((1, (0, 6, 8, 10)), (0, (10, 11, 12, 13))):
        if slot == 1:
            total = None
            for k, p in enumerate(parts):
                copies[2 * k].wait()
                copies[2 * k + 1].wait()
                term = mm_tn(act[slot, p], dh2[p])
                total = term if total is None else total + term
        else:
            copies[10].wait()
            total = mm_tn(act[slot], dh2[...])
        keep[slot, 0:hid] = total.astype(BF16)
        for k in range(waits[1], waits[2]):
            copies[k].wait()
        keep[slot, hid:hid + d] = mm_tn(n1[...], du[slot]).astype(BF16)
        for k in range(waits[2], waits[3]):
            copies[k].wait()
        keep[slot, hid + d:rows] = mm_tn(o[slot], dh1b[...]).astype(BF16)
        keep[slot, rows:] = small_rows(place[0], sum_ref[...], sbe_ref[...], slot, 0, hid)
        out = pltpu.make_async_copy(keep.at[slot], keep_hbm.at[slot], out_sems.at[slot])
        out.start()
        flush.append(out)
    for out in flush:
        out.wait()


def feed_grad(place, act, du, n1, dh2, dh1b, o0, o1, sums, sbe):
    n, d = n1.shape
    hid, mrows = act.shape[1] // 2, o0.shape[1] // 2
    grows = hid + d + mrows + SMALL
    hbm = pl.BlockSpec(memory_space=pl.ANY)
    return pl.pallas_call(
        feed_grad_kernel,
        in_specs=[smem()] + [hbm] * 7 + [whole(sums.shape), whole(sbe.shape)],
        out_specs=hbm,
        out_shape=jax.ShapeDtypeStruct((2, grows, d), BF16),
        scratch_shapes=[
            pltpu.VMEM((2, n, hid), BF16),
            pltpu.VMEM((2, n, hid), BF16),
            pltpu.VMEM((n, d), BF16),
            pltpu.VMEM((n, d), BF16),
            pltpu.VMEM((n, d), BF16),
            pltpu.VMEM((2, n, mrows), BF16),
            pltpu.VMEM((2, grows, d), BF16),
            pltpu.SemaphoreType.DMA((13,)),
            pltpu.SemaphoreType.DMA((2,)),
        ],
        compiler_params=kernel_params(58),
        cost_estimate=cost(9),
        name="feed_grad",
    )(place, act, du, n1, dh2, dh1b, o0, o1, sums, sbe)


def backward_kernel(place, long_ref, item_ref, tau_ref, *refs, sets, steps, group):
    step = pl.program_id(0)
    width = group * LONG
    per = [refs[7 * s:7 * s + 7] for s in range(sets)]
    x_ref = refs[7 * sets]
    outs = refs[7 * sets + 1:7 * sets + 1 + 2 * sets]
    x_all, d_all = refs[-2:]
    x_all[pl.ds(pl.multiple_of(step * width, width), width)] = x_ref[...]
    lane = lax.broadcasted_iota(jnp.int32, (1, PAIR), 1)
    first = lane < HEAD
    ready = []
    for m in range(group):
        _, rows = pack_rows(step * group + m + place[1], long_ref, item_ref)
        tau = pack_tau(rows, tau_ref) * HEAD**-0.5
        here = slice(m * LONG, (m + 1) * LONG)
        for s in range(sets):
            _, _, v_ref, g_ref, o_ref, r_ref, _ = per[s]
            g = g_ref[here].astype(F32) * r_ref[here]
            low = g.astype(BF16)
            scaled = (g * tau).astype(BF16).astype(F32)
            d = scaled * o_ref[here].astype(F32)
            v = v_ref[here].astype(F32)
            for j in range(2):
                own = first if j == 0 else jnp.logical_not(first)
                spare = HEAD if j == 0 else 0
                dd = jnp.sum(jnp.where(own, d, 0.0), axis=1, keepdims=True)
                high = dd.astype(BF16).astype(F32)
                left = jnp.where(lane == spare, -high, jnp.where(lane == spare + 1, high - dd, 0.0))
                left = jnp.where(own, scaled, left).astype(BF16)
                ones = jnp.where(jnp.logical_or(lane == spare, lane == spare + 1), 1.0, 0.0)
                right = jnp.where(own, v, ones).astype(BF16)
                ready.append((left, right, low[:, j * HEAD:(j + 1) * HEAD], m, s, j))
    res = []
    t = mm_nt(*ready[0][:2])
    for n, (_, _, low, m, s, j) in enumerate(ready):
        later = mm_nt(*ready[n + 1][:2]) if n + 1 < len(ready) else None
        q_ref, k_ref, _, _, _, _, p_ref = per[s]
        here = slice(m * LONG, (m + 1) * LONG)
        at = slice(j * HEAD, (j + 1) * HEAD)
        w = p_ref[m, j]
        r = (w.astype(F32) * t).astype(BF16)
        res.append((mm(r, k_ref[here, at]), mm_tn(q_ref[here, at], r), mm_tn(low, w)))
        t = later
        if j == 1:
            a, b = res[-2:]
            out = [jnp.concatenate([a[0], b[0]], axis=1).astype(BF16)]
            out += [jnp.concatenate([a[k], b[k]], axis=0).T.astype(BF16) for k in (1, 2)]
            spot = pl.ds(pl.multiple_of(step * width + m * LONG, LONG), LONG)
            for k in range(3):
                outs[2 * s][here, k * PAIR:(k + 1) * PAIR] = out[k]
                d_all[spot, (3 * s + k) * PAIR:(3 * s + k + 1) * PAIR] = out[k]

    @pl.when(step == steps - 1)
    def _():
        depth = x_ref.shape[1]
        res = mm_tn(x_all[...], d_all[...]).astype(BF16)
        for s in range(sets):
            grad_ref = outs[2 * s + 1]
            for k in range(3):
                grad_ref[k * depth:(k + 1) * depth] = res[:, (3 * s + k) * PAIR:(3 * s + k + 1) * PAIR]
            cols = [slice((3 * s + k) * PAIR, (3 * s + k + 1) * PAIR) for k in (0, 2)]
            dq, dv = [col_sum(d_all[:, at].astype(F32)) for at in cols]
            small = jnp.concatenate([dq, dv, jnp.zeros((SMALL_PAIR - 2, PAIR), F32)], axis=0)
            grad_ref[3 * depth:] = small.astype(BF16)


def attend_back(place, long_, item, tau, saved, x, quarters):
    n, d = x.shape
    sets = len(quarters)
    group = 2 // sets
    width = group * LONG
    steps = n // width
    col = lambda c: pl.BlockSpec((width, PAIR), lambda i, *_: (i, c))
    S = jax.ShapeDtypeStruct
    rows = 3 * d + SMALL_PAIR
    specs, operands = [], []
    for slot, h in quarters:
        p = saved[slot][-1]
        specs += [col(h)] * 3 + [col(2 * slot + h)] + [col(h)] * 2
        specs += [pl.BlockSpec((group, 2) + p.shape[2:], lambda i, *_, h=h: (i, h, 0, 0))]
        operands += list(saved[slot])
    return pl.pallas_call(
        functools.partial(backward_kernel, sets=sets, steps=steps, group=group),
        grid_spec=pltpu.PrefetchScalarGridSpec(
            num_scalar_prefetch=3,
            grid=(steps,),
            in_specs=[smem()] + specs + [pl.BlockSpec((width, d), lambda i, *_: (i, 0))],
            out_specs=[
                pl.BlockSpec((width, 3 * PAIR), lambda i, *_: (i, 0)),
                pl.BlockSpec((rows, PAIR), lambda i, *_: (0, 0)),
            ]
            * sets,
            scratch_shapes=[pltpu.VMEM((n, d), BF16), pltpu.VMEM((n, sets * 3 * PAIR), BF16)],
        ),
        out_shape=[S((n, 3 * PAIR), BF16), S((rows, PAIR), BF16)] * sets,
        compiler_params=kernel_params(58),
        cost_estimate=cost(8),
        name="attend_back_" + "_".join("%d%d" % q for q in quarters),
    )(place, long_, item, tau, *operands, x)


def input_grad_kernel(place, dh1_ref, ka_ref, sa_ref, near_ref, far_ref, *refs):
    d_refs, (out_ref, w_ref) = refs[:4], refs[-2:]

    @pl.when(pl.program_id(0) == 0)
    def _():
        for j in range(3):
            for k, ref in enumerate((ka_ref, sa_ref, near_ref, far_ref)):
                lo = (k * 3 + j) * PAIR
                w_ref[:, lo:lo + PAIR] = projection(ref, j, w_ref.shape[0])

    d = jnp.concatenate([ref[...] for ref in d_refs], axis=1)
    out_ref[...] = dh1_ref[...].astype(F32) + mm_nt(d, w_ref[...])


def input_grad(place, dh1, weight, near, far, grads, part, held=None):
    n, d = dh1.shape
    tile = LONG
    steps = n // tile // 2
    cols = grads[0].shape[1]
    row = lambda c: pl.BlockSpec((tile, c), lambda i, *_: (part * steps + i, 0))
    pick = lambda h: pl.BlockSpec((3, d, PAIR), lambda i, place: (0, 0, place[0] ^ h), pipeline_mode=pl.Buffered(1))
    extra = [] if held is None else [held]
    return pl.pallas_call(
        input_grad_kernel,
        grid_spec=pltpu.PrefetchScalarGridSpec(
            num_scalar_prefetch=1,
            grid=(steps,),
            in_specs=[row(d), pick(0), pick(1), whole(near.shape), whole(far.shape)]
            + [row(cols)] * 4
            + [pl.BlockSpec(memory_space=pl.ANY)] * len(extra),
            out_specs=row(d),
            scratch_shapes=[pltpu.VMEM((d, 4 * cols), BF16)],
        ),
        out_shape=jax.ShapeDtypeStruct((n, d), F32),
        input_output_aliases={10: 0} if extra else {},
        compiler_params=kernel_params(58),
        cost_estimate=cost(8000),
        name="input_grad%d" % part,
    )(place, dh1, weight, weight, near, far, *grads, *extra)


def flip(v, axis, mask=1):
    size = lax.axis_size(axis)
    return lax.ppermute(v, axis, [(i, i ^ mask) for i in range(size)])


def add_low(*parts):
    return functools.reduce(lambda a, b: a + b, [p.astype(F32) for p in parts]).astype(BF16)


def piece(v, which, rows):
    return lax.dynamic_slice_in_dim(v, which * rows, rows, v.ndim - 2)


def in_order(bit, own, other):
    return jnp.where(bit == 0, jnp.concatenate([own, other]), jnp.concatenate([other, own]))


def split_rows(v):
    high = v.astype(BF16)
    left = v - high.astype(F32)
    mid = left.astype(BF16)
    low = (left - mid.astype(F32)).astype(BF16)
    return jnp.concatenate([high, mid, low, jnp.zeros_like(high)], axis=0)


def joined_rows(v):
    rows = v.shape[0] // 4
    v = v.astype(F32)
    return v[:rows] + v[rows:2 * rows] + v[2 * rows:3 * rows]


def prepare_kernel(
    project_hbm, expand_hbm, reduce_hbm, merge_hbm, pb_ref, eb_ref,
    project_half, rest_half, place_ref, sems, *, packs,
):
    core, side, outer = lax.axis_index("core"), lax.axis_index("tensor"), lax.axis_index("outer")
    hid, d, mrows = expand_hbm.shape[1] // 2, expand_hbm.shape[0], merge_hbm.shape[0] // 2
    half = lambda n: pl.ds(pl.multiple_of(core * n, n), n)
    copies = [
        (project_hbm.at[j, :, half(PAIR)], project_half.at[pl.ds(j * d, d)]) for j in range(3)
    ] + [
        (expand_hbm.at[:, half(hid)], rest_half.at[pl.ds(0, d)]),
        (reduce_hbm.at[half(hid)], rest_half.at[pl.ds(d, hid)]),
    ] + [
        (merge_hbm.at[half(mrows), pl.ds(k * PAIR, PAIR)], project_half.at[pl.ds(3 * d + k * mrows, mrows)])
        for k in range(d // PAIR)
    ]
    copies = [pltpu.make_async_copy(src, dst, sems.at[k]) for k, (src, dst) in enumerate(copies)]
    for copy in copies:
        copy.start()
    at = lambda k: slice(k * PAIR, (k + 1) * PAIR)
    rows = [pb_ref[j:j + 1, at(k)] for j in range(2) for k in range(2)]
    rows += [eb_ref[:, at(k)] for k in range(eb_ref.shape[1] // PAIR)]
    fill = jnp.zeros((BIAS_ROWS // 4 - len(rows), PAIR), F32)
    project_half[4 * d:] = split_rows(jnp.concatenate(rows + [fill], axis=0))
    place_ref[0] = core
    place_ref[1] = side * packs
    place_ref[2] = outer % 2
    for copy in copies:
        copy.wait()


def prepare(project, expand, reduce_, merge, project_bias, expand_bias, packs):
    d, hid = expand.shape[0], expand.shape[1] // 2
    S = jax.ShapeDtypeStruct
    hbm = pl.BlockSpec(memory_space=pl.ANY)
    return pl.pallas_call(
        functools.partial(prepare_kernel, packs=packs),
        in_specs=[hbm] * 4 + [whole(project_bias.shape), whole((1, 2 * hid))],
        out_specs=[whole((4 * d + BIAS_ROWS, PAIR)), whole((d + hid, d)), smem()],
        out_shape=[
            S((4 * d + BIAS_ROWS, PAIR), BF16), S((d + hid, d), BF16), S((3,), jnp.int32),
        ],
        scratch_shapes=[pltpu.SemaphoreType.DMA((9,))],
        compiler_params=kernel_params(63),
        cost_estimate=cost(3),
        name="prepare",
    )(project, expand, reduce_, merge, project_bias, expand_bias[None])


def combine_kernel(place, keep_ref, got_ref, ax_ref, a0_ref, send_ref, keep_out_ref):
    step = pl.program_id(0)
    total = (keep_ref[...].astype(F32) + got_ref[...].astype(F32)).astype(BF16)

    @pl.when(step < 2)
    def _():
        a0_ref[...] = total[0]
        ax_ref[...] = total[1]

    @pl.when(step == 2)
    def _():
        send_ref[...] = total

    @pl.when(step == 3)
    def _():
        keep_out_ref[...] = total


def combine(place, keep, got):
    _, rows, d = keep.shape
    half = rows // 4
    S = jax.ShapeDtypeStruct
    pick = lambda i, place: (0, jnp.where(i < 2, i, jnp.where(i == 2, 3 - place[2], 2 + place[2])), 0)
    first = pl.BlockSpec((half, d), lambda i, *_: (jnp.minimum(i, 1), 0))
    both = pl.BlockSpec((2, half, d), lambda i, *_: (0, 0, 0))
    return pl.pallas_call(
        combine_kernel,
        grid_spec=pltpu.PrefetchScalarGridSpec(
            num_scalar_prefetch=1,
            grid=(4,),
            in_specs=[pl.BlockSpec((2, half, d), pick)] * 2,
            out_specs=[first, first, both, both],
        ),
        out_shape=[S((2 * half, d), BF16)] * 2 + [S((2, half, d), BF16)] * 2,
        compiler_params=kernel_params(20),
        cost_estimate=cost(3),
        name="combine",
    )(place, keep, got)


def unpack_kernel(place, own_ref, other_ref, reduce_ref, expand_ref, merge_ref, small_ref, *, steps):
    k = pl.program_id(1)
    hid, d, mrows = reduce_ref.shape[0] * steps, expand_ref.shape[0] * steps, merge_ref.shape[0] * steps

    def put(ref):
        at = lambda base, rows: pl.ds(pl.multiple_of(base + k * rows, rows), rows)
        reduce_ref[...] = ref[at(0, hid // steps)].astype(F32)
        expand_ref[...] = ref[at(hid, d // steps)].astype(F32)
        merge_ref[...] = ref[at(hid + d, mrows // steps)].astype(F32)
        small_ref[...] = ref[hid + d + mrows:hid + d + mrows + 8].astype(F32)

    pl.when(pl.program_id(0) == 0)(lambda: put(own_ref))
    pl.when(pl.program_id(0) == 1)(lambda: put(other_ref))


def unpack(place, own, other, hid, mrows):
    d = own.shape[1]
    steps = 1
    S = jax.ShapeDtypeStruct
    rows = lambda r: pl.BlockSpec((r // steps, d), lambda i, k, place: ((place[0] ^ i) * steps + k, 0))
    return pl.pallas_call(
        functools.partial(unpack_kernel, steps=steps),
        grid_spec=pltpu.PrefetchScalarGridSpec(
            num_scalar_prefetch=1,
            grid=(2, steps),
            in_specs=[whole(own.shape)] * 2,
            out_specs=[
                rows(hid),
                pl.BlockSpec((d // steps, hid), lambda i, k, place: (k, place[0] ^ i)),
                rows(mrows),
                pl.BlockSpec((8, d), lambda i, k, place: (place[0] ^ i, 0)),
            ],
        ),
        out_shape=[S((2 * hid, d), F32), S((d, 2 * hid), F32), S((2 * mrows, d), F32), S((16, d), F32)],
        compiler_params=kernel_params(20),
        cost_estimate=cost(3),
        name="unpack",
    )(place, own, other)


def by_bits(bits, pieces):
    v = jnp.stack(pieces)
    v = jnp.where(bits % 2 == 0, v, jnp.stack([v[1], v[0], v[3], v[2]]))
    v = jnp.where(bits // 2 == 0, v, jnp.stack([v[2], v[3], v[0], v[1]]))
    return v.reshape((-1,) + v.shape[2:])


def row_layer(
    inputs,
    pack_long,
    item_table,
    tau_table,
    delta_table,
    project_weight,
    project_bias,
    merge_weight,
    merge_bias,
    first_gain,
    first_shift,
    expand_weight,
    expand_bias,
    reduce_weight,
    reduce_bias,
    second_gain,
    second_shift,
    grad_output,
):
    n, d = inputs.shape
    hid = expand_weight.shape[1] // 2
    mrows = merge_weight.shape[0] // 2
    core = lax.axis_index("core")
    outer = lax.axis_size("outer")
    y_bit, z_bit = lax.axis_index("outer") % 2, lax.axis_index("outer") // 2 % 2
    project_half, rest_half, place = prepare(
        project_weight, expand_weight, reduce_weight, merge_weight, project_bias, expand_bias, n // LONG
    )
    project_near = flip(project_half, "tensor")
    rest_near = flip(rest_half, "tensor")

    table = (place, pack_long, item_table, tau_table)
    q0, k0, v0, o0, r0, p0 = attend(
        *table, delta_table, inputs, project_weight, project_weight, project_bias, True
    )
    project_near, o0 = lax.optimization_barrier((project_near, o0))
    project_far = flip(project_near, "core")
    q1, k1, v1, o1, r1, p1, xh, rs = attend(
        *table, delta_table, inputs, project_near, project_far, project_near, False,
        o0, merge_weight, merge_bias[None],
    )
    rest_near, o1 = lax.optimization_barrier((rest_near, o1))
    rest_far = flip(rest_near, "core")
    block_output, grad_att, act, du, n1, dh2, dh1b, sums, sbe, send = feed(
        place, o0, o1, xh, rs, grad_output, merge_weight, project_near, project_far, expand_weight, reduce_weight,
        rest_near, rest_far, expand_bias[None], project_near,
        [v[None] for v in (first_gain, first_shift, reduce_bias, second_gain, second_shift)],
    )
    saved = ((q0, k0, v0, grad_att, o0, r0, p0), (q1, k1, v1, grad_att, o1, r1, p1))
    back = lambda x, *quarters: attend_back(*table, saved, x, quarters)

    got = flip(send, "core")
    keep = feed_grad(place, act, du, n1, dh2, dh1b, o0, o1, sums, sbe)
    got, keep = lax.optimization_barrier((got, keep))
    half = keep.shape[1] // 4
    a_x, a, b_y, b = combine(place, keep, got)
    x, a_x, b_y = lax.optimization_barrier((inputs, a_x, b_y))
    a_x, b_y = flip(a_x, "tensor"), flip(b_y, "outer", 1)
    d01, g01, d11, g11 = back(x, (0, 1), (1, 1))
    got01, got11 = flip(g01, "core"), flip(g11, "core")
    a_x, b_y, d11 = lax.optimization_barrier((a_x, b_y, d11))
    a, b = add_low(a, a_x), add_low(b, b_y)
    a_y, b_x = piece(a, 1 - y_bit, half), b[1]
    x, a_y, b_x = lax.optimization_barrier((x, a_y, b_x))
    a_y, b_x = flip(a_y, "outer", 1), flip(b_x, "tensor")
    d10, g10 = back(x, (1, 0))
    a_y, b_x, d10 = lax.optimization_barrier((a_y, b_x, d10))
    far = add_low(g10, got11)
    total = jnp.concatenate([add_low(piece(a, y_bit, half), a_y), add_low(b[0], b_x)])
    to_z = piece(total, 1 - z_bit, half)
    x, far, to_z = lax.optimization_barrier((x, far, to_z))
    far, to_z = flip(far, "tensor"), flip(to_z, "outer", 2)
    d00, g00 = back(x, (0, 0))
    far, to_z, d00 = lax.optimization_barrier((far, to_z, d00))
    feed_part = add_low(piece(total, z_bit, half), to_z)

    mine = add_low(g00, got01, far)
    rows = mine.shape[0] // 4
    to_y = flip(piece(mine, 1 - y_bit, 2 * rows), "outer", 1)
    came = flip(feed_part, "outer", 4)
    dx = functools.partial(input_grad, place, dh1b, project_weight, project_near, project_far)
    mine = add_low(piece(mine, y_bit, 2 * rows), to_y)
    to_z = piece(mine, 1 - z_bit, rows)
    d00, to_z, mine = lax.optimization_barrier((d00, to_z, mine))
    to_z = flip(to_z, "outer", 2)
    dx0 = dx((d00, d01, d10, d11), 0)
    to_z, came, dx0 = lax.optimization_barrier((to_z, came, dx0))
    project_part = add_low(piece(mine, z_bit, rows), to_z)
    feed_part = add_low(feed_part, came)
    project_part, feed_part, d00 = lax.optimization_barrier((project_part, feed_part, d00))
    came = flip(project_part, "outer", 4) if outer > 4 else jnp.zeros_like(project_part)
    by_y, by_z = flip(feed_part, "outer", 1), flip(feed_part, "outer", 2)
    dx1 = dx((d00, d01, d10, d11), 1, dx0)
    came, dx1, by_y, by_z = lax.optimization_barrier((came, dx1, by_y, by_z))
    mid = feed_part.shape[0] // 2
    cross = flip(by_z[:mid], "outer", 1), flip(by_y[mid:], "outer", 2)
    project_part = add_low(project_part, came)
    others = [flip(project_part, "outer", mask) for mask in (2, 1, 3)]
    cross, others = lax.optimization_barrier((cross, others))
    feed_pieces = [feed_part, by_y, by_z, jnp.concatenate(cross)]
    project_pieces = [project_part] + others
    total = by_bits(z_bit * 2 + y_bit, feed_pieces)
    reduce_grad, expand_grad, merge_grad, small = unpack(place, total, flip(total, "core"), hid, mrows)
    total = by_bits(y_bit * 2 + z_bit, project_pieces)
    project_sum = in_order(core, total[None], flip(total, "core")[None]).astype(F32)

    weight = project_sum[:, : 3 * d].reshape(2, 3, d, PAIR)
    return (
        block_output,
        dx1,
        jnp.concatenate([weight[0], weight[1]], axis=-1),
        jnp.concatenate([project_sum[0, 3 * d : 3 * d + 2], project_sum[1, 3 * d : 3 * d + 2]], axis=-1),
        merge_grad,
        small[1],
        small[2],
        small[3],
        expand_grad,
        small[0::8].reshape(-1),
        reduce_grad,
        small[9],
        small[10],
        small[11],
    )


def rows_fit(mesh):
    size = mesh.shape["dp"]
    return mesh.shape["tensor"] == 2 and size in (8, 16)


def solution(mesh):
    if rows_fit(mesh):
        mesh = Mesh(mesh.devices.reshape(-1, 2, 2), ("outer", "core", "tensor"))
        body, dp = row_layer, ("outer", "core")
    else:
        body, dp = split_layer, ("dp",)
    all_ = P(dp + ("tensor",), None)
    placed = (
        all_,
        P(dp),
        P(dp),
        P(),
        P(),
        P(None, None, "tensor"),
        P(None, "tensor"),
        P("tensor", None),
        P(),
        P(),
        P(),
        P(None, "tensor"),
        P("tensor"),
        P("tensor", None),
        P(),
        P(),
        P(),
        all_,
    )
    return jax.shard_map(
        body,
        mesh=mesh,
        in_specs=placed,
        out_specs=(
            all_,
            all_,
            P(None, None, "tensor"),
            P(None, "tensor"),
            P("tensor", None),
            P(),
            P(),
            P(),
            P(None, "tensor"),
            P("tensor"),
            P("tensor", None),
            P(),
            P(),
            P(),
        ),
        check_vma=False,
    )
```

```python
import functools
import jax
import jax.numpy as jnp
from jax import lax
from jax.experimental import pallas as pl
from jax.experimental.pallas import tpu as pltpu
from jax.sharding import Mesh, PartitionSpec as P

HEAD = 64
SHORT = 96
LONG = 384
TABLE = 64
PAIR = 2 * HEAD
SMALL = 128
SMALL_PAIR = 32
BIAS_ROWS = 64
LOG2E = 1.4426950408889634
F32 = jnp.float32
BF16 = jnp.bfloat16


def layer_norm(values, gain, shift):
    mean = jnp.mean(values, axis=-1, keepdims=True)
    centred = values - mean
    spread = jnp.mean(centred * centred, axis=-1, keepdims=True)
    return centred * lax.rsqrt(spread + 1e-05) * gain + shift


def exact_gelu(values):
    return jax.nn.gelu(values, approximate=False)


def describe(pack_long, item_table, tau_table, delta_table):
    packs = pack_long.shape[0]
    per = LONG // SHORT
    count = packs * LONG
    longer = jnp.broadcast_to(pack_long[:, None] == 1, (packs, LONG)).reshape(count)
    lead_row = jnp.broadcast_to(item_table.reshape(packs, per)[:, :1], (packs, LONG)).reshape(count)
    each_row = jnp.broadcast_to(item_table[:, None], (packs * per, SHORT)).reshape(count)
    table_row = jnp.where(longer, lead_row, each_row)
    places = jnp.arange(count, dtype=jnp.int32)
    position = jnp.where(longer, places % LONG, places % SHORT)
    segment = jnp.where(longer, places // LONG * per, places // SHORT)
    picker = (table_row[:, None] == jnp.arange(TABLE, dtype=jnp.int32)[None, :]).astype(jnp.float32)
    tau_row = jnp.sum(picker * tau_table[None, :], axis=1)
    picked = jnp.dot(
        picker, delta_table, precision=lax.Precision.HIGHEST, preferred_element_type=jnp.float32
    )
    placed = position[:, None] == jnp.arange(LONG, dtype=jnp.int32)[None, :]
    delta_row = jnp.sum(jnp.where(placed, picked, 0.0), axis=1)
    return (tau_row, delta_row, segment)


def project(rows_all, project_weight, project_bias):
    query = (
        jnp.dot(rows_all, project_weight[0], preferred_element_type=jnp.float32) + project_bias[0]
    ).astype(jnp.bfloat16)
    keys = jnp.dot(rows_all, project_weight[1], preferred_element_type=jnp.float32).astype(
        jnp.bfloat16
    )
    values = (
        jnp.dot(rows_all, project_weight[2], preferred_element_type=jnp.float32) + project_bias[1]
    ).astype(jnp.bfloat16)
    return (query, keys, values)


def split_blocks(arrays):
    width = 2 * LONG
    return tuple((a.reshape((a.shape[0] // width, width) + a.shape[1:]) for a in arrays))


def block_scores(block_q, block_k, block_tau, block_delta, block_seg):
    raw = jnp.einsum("qhd,khd->hqk", block_q, block_k, preferred_element_type=jnp.float32)
    scores = (block_tau[None, :, None] * raw + block_delta[None, None, :]) * HEAD ** (-0.5)
    same = block_seg[:, None] == block_seg[None, :]
    return jnp.where(same[None], scores, -1e30)


def attend_forward(query, keys, values, tau_row, delta_row, segment):
    heads = query.shape[1] // HEAD
    shaped = tuple((a.reshape(a.shape[0], heads, HEAD) for a in (query, keys, values)))

    def one_block(parts):
        block_q, block_k, block_v, block_tau, block_delta, block_seg = parts
        scores = block_scores(block_q, block_k, block_tau, block_delta, block_seg)
        top = jnp.max(scores, axis=-1, keepdims=True)
        expo = jnp.exp(scores - top)
        totals = jnp.sum(expo, axis=-1, keepdims=True)
        weights = (expo / totals).astype(jnp.bfloat16)
        mixed = jnp.einsum("hqk,khd->qhd", weights, block_v, preferred_element_type=jnp.float32)
        return (
            mixed.reshape(mixed.shape[0], heads * HEAD).astype(jnp.bfloat16),
            top + jnp.log(totals),
        )

    attended, logsum = lax.map(one_block, split_blocks(shaped + (tau_row, delta_row, segment)))
    return (attended.reshape(query.shape), logsum)


def attend_backward(query, keys, values, grad_att, logsum, tau_row, delta_row, segment):
    heads = query.shape[1] // HEAD
    shaped = tuple((a.reshape(a.shape[0], heads, HEAD) for a in (query, keys, values, grad_att)))
    blocked = split_blocks(shaped + (tau_row, delta_row, segment))

    def one_block(parts):
        block_q, block_k, block_v, block_g, block_lse, block_tau, block_delta, block_seg = parts
        scores = block_scores(block_q, block_k, block_tau, block_delta, block_seg)
        probs = jnp.exp(scores - block_lse)
        dprob = jnp.einsum("qhd,khd->hqk", block_g, block_v, preferred_element_type=jnp.float32)
        dscore = probs * (dprob - jnp.sum(dprob * probs, axis=-1, keepdims=True))
        lowered = (dscore * HEAD ** (-0.5) * block_tau[None, :, None]).astype(jnp.bfloat16)
        grad_q = jnp.einsum("hqk,khd->qhd", lowered, block_k, preferred_element_type=jnp.float32)
        grad_k = jnp.einsum("hqk,qhd->khd", lowered, block_q, preferred_element_type=jnp.float32)
        grad_v = jnp.einsum(
            "hqk,qhd->khd", probs.astype(jnp.bfloat16), block_g, preferred_element_type=jnp.float32
        )
        width = block_q.shape[0]
        return tuple(
            (g.reshape(width, heads * HEAD).astype(jnp.bfloat16) for g in (grad_q, grad_k, grad_v))
        )

    grads = lax.map(one_block, blocked[:4] + (logsum,) + blocked[4:])
    return tuple((g.reshape(query.shape) for g in grads))


def row_term(left, right, form):
    return jnp.einsum(form, left, right, preferred_element_type=jnp.float32)


def feed_backward(feed_rows, preact_rows, active_rows, grad_fed, reduce_matrix):
    grad_reduce_weight = jnp.einsum(
        "tf,td->fd", active_rows, grad_fed, preferred_element_type=jnp.float32
    )
    grad_active = jnp.einsum(
        "td,fd->tf", grad_fed, reduce_matrix, preferred_element_type=jnp.float32
    )
    grad_preact = jax.vjp(exact_gelu, preact_rows)[1](grad_active)[0].astype(jnp.bfloat16)
    grad_expand_bias = jnp.sum(grad_preact.astype(jnp.float32), axis=0)
    grad_expand_weight = jnp.einsum(
        "td,tf->df", feed_rows, grad_preact, preferred_element_type=jnp.float32
    )
    return (grad_reduce_weight, grad_preact, grad_expand_bias, grad_expand_weight)


def split_layer(
    inputs,
    pack_long,
    item_table,
    tau_table,
    delta_table,
    project_weight,
    project_bias,
    merge_weight,
    merge_bias,
    first_gain,
    first_shift,
    expand_weight,
    expand_bias,
    reduce_weight,
    reduce_bias,
    second_gain,
    second_shift,
    grad_output,
):
    tau_row, delta_row, segment = describe(pack_long, item_table, tau_table, delta_table)
    rows_all = lax.all_gather(inputs, "tensor", axis=0, tiled=True)
    query, keys, values = project(rows_all, project_weight, project_bias)
    attended, logsum = attend_forward(query, keys, values, tau_row, delta_row, segment)
    mixed_part = lax.psum_scatter(
        row_term(attended, merge_weight, "tc,cd->td"), "tensor", scatter_dimension=0, tiled=True
    )
    first_sum = inputs.astype(jnp.float32) + (mixed_part + merge_bias)
    normed, first_back = jax.vjp(layer_norm, first_sum, first_gain, first_shift)
    normed_low = normed.astype(jnp.bfloat16)
    feed_all = lax.all_gather(normed_low, "tensor", axis=0, tiled=True)
    preact = jnp.dot(feed_all, expand_weight, preferred_element_type=jnp.float32) + expand_bias
    active = exact_gelu(preact).astype(jnp.bfloat16)
    fed_part = lax.psum_scatter(
        row_term(active, reduce_weight, "tf,fd->td"), "tensor", scatter_dimension=0, tiled=True
    )
    second_sum = normed + (fed_part + reduce_bias)
    block_output, second_back = jax.vjp(layer_norm, second_sum, second_gain, second_shift)
    grad_second, grad_gain_b, grad_shift_b = second_back(grad_output.astype(jnp.float32))
    grad_reduce_bias = jnp.sum(grad_second, axis=0)
    grad_fed = lax.all_gather(grad_second.astype(jnp.bfloat16), "tensor", axis=0, tiled=True)
    feed_again = lax.all_gather(normed_low, "tensor", axis=0, tiled=True)
    preact_again = (
        jnp.dot(feed_again, expand_weight, preferred_element_type=jnp.float32) + expand_bias
    )
    active_again = exact_gelu(preact_again).astype(jnp.bfloat16)
    grad_reduce_weight, grad_preact, grad_expand_bias, grad_expand_weight = feed_backward(
        feed_again, preact_again, active_again, grad_fed, reduce_weight
    )
    grad_normed = grad_second + lax.psum_scatter(
        row_term(grad_preact, expand_weight, "tf,df->td"), "tensor", scatter_dimension=0, tiled=True
    )
    grad_first, grad_gain_a, grad_shift_a = first_back(grad_normed)
    grad_merge_bias = jnp.sum(grad_first, axis=0)
    grad_att = lax.all_gather(grad_first.astype(jnp.bfloat16), "tensor", axis=0, tiled=True)
    grad_merge_weight = jnp.einsum(
        "tc,td->cd", attended, grad_att, preferred_element_type=jnp.float32
    )
    grad_attended = jnp.einsum(
        "td,cd->tc", grad_att, merge_weight, preferred_element_type=jnp.float32
    ).astype(jnp.bfloat16)
    rows_again = lax.all_gather(inputs, "tensor", axis=0, tiled=True)
    query_again, keys_again, values_again = project(rows_again, project_weight, project_bias)
    grad_q, grad_k, grad_v = attend_backward(
        query_again, keys_again, values_again, grad_attended, logsum, tau_row, delta_row, segment
    )
    grad_stack = jnp.stack((grad_q, grad_k, grad_v), axis=1)
    grad_project_weight = jnp.einsum(
        "td,tjc->jdc", rows_again, grad_stack, preferred_element_type=jnp.float32
    )
    grad_project_bias = jnp.stack(
        (jnp.sum(grad_q.astype(jnp.float32), axis=0), jnp.sum(grad_v.astype(jnp.float32), axis=0))
    )
    input_grad = grad_first + lax.psum_scatter(
        row_term(grad_stack, project_weight, "tjc,jdc->td").astype(jnp.bfloat16),
        "tensor",
        scatter_dimension=0,
        tiled=True,
    ).astype(jnp.float32)
    summed_all = (
        lax.psum(grad_project_weight.astype(jnp.bfloat16), "dp").astype(jnp.float32),
        lax.psum(grad_project_bias.astype(jnp.bfloat16), "dp").astype(jnp.float32),
        lax.psum(grad_merge_weight.astype(jnp.bfloat16), "dp").astype(jnp.float32),
        lax.psum(grad_expand_weight.astype(jnp.bfloat16), "dp").astype(jnp.float32),
        lax.psum(grad_expand_bias.astype(jnp.bfloat16), "dp").astype(jnp.float32),
        lax.psum(grad_reduce_weight.astype(jnp.bfloat16), "dp").astype(jnp.float32),
    )
    summed_attention = summed_all[:3]
    summed_feed = summed_all[3:]
    small = lax.psum(
        (grad_merge_bias, grad_gain_a, grad_shift_a, grad_reduce_bias, grad_gain_b, grad_shift_b),
        ("dp", "tensor"),
    )
    return (
        block_output,
        input_grad,
        summed_attention[0],
        summed_attention[1],
        summed_attention[2],
        small[0],
        small[1],
        small[2],
        summed_feed[0],
        summed_feed[1],
        summed_feed[2],
        small[3],
        small[4],
        small[5],
    )


def mm(a, b):
    return lax.dot_general(a, b, (((1,), (0,)), ((), ())), preferred_element_type=F32)


def mm_nt(a, b):
    return lax.dot_general(a, b, (((1,), (1,)), ((), ())), preferred_element_type=F32)


def mm_tn(a, b):
    return lax.dot_general(a, b, (((0,), (0,)), ((), ())), preferred_element_type=F32)


def col_sum(v):
    return jnp.sum(v, axis=0, keepdims=True)


def row_mean(v):
    return jnp.mean(v, axis=1, keepdims=True)


def pack_rows(pack, long_ref, item_ref):
    per = LONG // SHORT
    longer = long_ref[pack] == 1
    rows = [jnp.where(longer, item_ref[pack * per], item_ref[pack * per + k]) for k in range(per)]
    return longer, rows


def pack_tau(rows, tau_ref):
    slot = lax.broadcasted_iota(jnp.int32, (LONG, 1), 0) // SHORT
    tau = jnp.full((LONG, 1), tau_ref[rows[0]], F32)
    for k in range(1, LONG // SHORT):
        tau = jnp.where(slot == k, tau_ref[rows[k]], tau)
    return tau


def pack_bias(longer, rows, delta_ref):
    slot_r = lax.broadcasted_iota(jnp.int32, (LONG, 1), 0) // SHORT
    slot_c = lax.broadcasted_iota(jnp.int32, (1, LONG), 1) // SHORT
    shift = delta_ref[pl.ds(rows[0], 1), :]
    for k in range(1, LONG // SHORT):
        piece = jnp.broadcast_to(delta_ref[pl.ds(rows[k], 1), :], (8, LONG))
        piece = pltpu.roll(piece, SHORT * k, 1)[0:1]
        shift = jnp.where(jnp.logical_and(jnp.logical_not(longer), slot_c == k), piece, shift)
    mask = jnp.logical_or(longer, slot_r == slot_c)
    return jnp.where(mask, shift * (HEAD**-0.5 * LOG2E), -1e30)


def forward_kernel(
    place, long_ref, item_ref, tau_ref, delta_ref, x_ref, wa_ref, wb_ref, ba_ref, bb_ref, *refs, own,
):
    step = pl.program_id(0)
    if own:
        q_ref, k_ref, v_ref, o_ref, r_ref, p_ref, w_ref, bias_ref = refs
    else:
        o0_ref, mk_ref, ms_ref, bm_ref = refs[:4]
        q_ref, k_ref, v_ref, o_ref, r_ref, p_ref, xh_ref, rs_ref, w_ref, bias_ref, wm_ref = refs[4:]

    @pl.when(step == 0)
    def _():
        if not own:
            merge_rows(wm_ref, mk_ref, ms_ref, wa_ref.at[3 * x_ref.shape[1]:], wb_ref.at[3 * x_ref.shape[1]:])
        for k, ref in enumerate((wa_ref, wb_ref)):
            for j in range(3):
                w_ref[j, :, k * PAIR:(k + 1) * PAIR] = projection(ref, j, x_ref.shape[1])

    longer, rows = pack_rows(step + place[1], long_ref, item_ref)
    bias_ref[...] = pack_bias(longer, rows, delta_ref)
    tau = pack_tau(rows, tau_ref) * (HEAD**-0.5 * LOG2E)
    x = x_ref[...]
    if own:
        q_bias, v_bias = [jnp.concatenate([ba_ref[j:j + 1], bb_ref[j:j + 1]], axis=1) for j in range(2)]
    else:
        b = joined_rows(ba_ref[...])
        q_bias, v_bias = [
            jnp.where(
                place[0] == 0,
                jnp.concatenate([b[k:k + 1], b[k + 1:k + 2]], axis=1),
                jnp.concatenate([b[k + 1:k + 2], b[k:k + 1]], axis=1),
            )
            for k in (0, 2)
        ]
    q = (mm(x, w_ref[0]) + q_bias).astype(BF16)
    k = mm(x, w_ref[1]).astype(BF16)
    v = (mm(x, w_ref[2]) + v_bias).astype(BF16)
    q_ref[...] = q
    k_ref[...] = k
    v_ref[...] = v
    scaled = (q.astype(F32) * tau).astype(BF16)
    vf = v.astype(F32)
    first = lax.broadcasted_iota(jnp.int32, (1, PAIR), 1) < HEAD
    heads = q.shape[1] // HEAD

    def score(h):
        at = slice(h * HEAD, (h + 1) * HEAD)
        return mm_nt(scaled[:, at], k[:, at])

    def soften(s):
        s = s + bias_ref[...]
        return jnp.exp2(s - jnp.max(s, axis=1, keepdims=True)).astype(BF16)

    mixed = []

    def mix(h, w):
        p_ref[0, h] = w
        at = slice(h // 2 * PAIR, (h // 2 + 1) * PAIR)
        own = first if h % 2 == 0 else jnp.logical_not(first)
        mixed.append(mm(w, jnp.where(own, vf[:, at], 1.0).astype(BF16)))
        if h % 2 == 1:
            a, b = mixed[-2:]
            r = 1.0 / pltpu.roll(jnp.where(first, b, a), HEAD, 1)
            r_ref[:, at] = r
            o_ref[:, at] = (jnp.where(first, a, b) * r).astype(BF16)

    s = score(0)
    held = None
    for h in range(heads):
        later = score(h + 1) if h + 1 < heads else None
        w = soften(s)
        if held is not None:
            mix(h - 1, held)
        held, s = w, later
    mix(heads - 1, held)
    if not own:
        half = wm_ref.shape[0] // 2
        mixed = mm(o0_ref[...], wm_ref[:half]) + mm(o_ref[...], wm_ref[half:])
        h1 = x.astype(F32) + (mixed + bm_ref[...])
        c = h1 - row_mean(h1)
        rs = lax.rsqrt(row_mean(c * c) + 1e-05)
        xh_ref[...] = c * rs
        rs_ref[...] = jnp.broadcast_to(rs, rs_ref.shape)


def merge_rows(out_ref, keep_ref, other_ref, near_ref, far_ref):
    rows = keep_ref.shape[0]
    out_ref[0:rows] = keep_ref[...]
    out_ref[rows:2 * rows] = other_ref[...]
    for m, ref in ((2, near_ref), (3, far_ref)):
        for k in range(out_ref.shape[1] // PAIR):
            out_ref[m * rows:(m + 1) * rows, k * PAIR:(k + 1) * PAIR] = ref[k * rows:(k + 1) * rows]


def whole(shape):
    return pl.BlockSpec(shape, lambda *_: (0,) * len(shape), pipeline_mode=pl.Buffered(1))


def smem():
    return pl.BlockSpec(memory_space=pltpu.SMEM)


def kernel_params(mib):
    return pltpu.CompilerParams(vmem_limit_bytes=mib * 2**20)


def cost(us):
    return pl.CostEstimate(flops=int(us * 1.0e6), bytes_accessed=0, transcendentals=0)


def projection(ref, j, d):
    return ref[j] if len(ref.shape) == 3 else ref[j * d:(j + 1) * d]


def bias_block(d):
    return pl.BlockSpec((BIAS_ROWS, PAIR), lambda *_: (4 * d // BIAS_ROWS, 0), pipeline_mode=pl.Buffered(1))


def attend(place, long_, item, tau, delta, x, wa, wb, bias, own, o0=None, merge=None, merge_bias=None):
    n, d = x.shape
    packs = n // LONG
    cols = 2 * PAIR
    row = lambda c: pl.BlockSpec((LONG, c), lambda i, *_: (i, 0))
    if own:
        weights = [
            pl.BlockSpec((3, d, PAIR), lambda i, place, *_, h=h: (0, 0, place[0] ^ h), pipeline_mode=pl.Buffered(1))
            for h in (0, 1)
        ]
        biases = [pl.BlockSpec((2, PAIR), lambda i, place, *_, h=h: (0, place[0] ^ h)) for h in (0, 1)]
    else:
        weights, biases = [whole(wa.shape), whole(wb.shape)], [bias_block(d)] * 2
    out = jax.ShapeDtypeStruct((n, cols), BF16)
    heads = cols // HEAD
    more_in, more_out, more_shapes, more_scratch, more = [], [], [], [], []
    if not own:
        mrows = merge.shape[0] // 2
        more_in = [row(cols)]
        more_in += [
            pl.BlockSpec((mrows, d), lambda i, place, *_, h=h: (place[0] ^ h, 0), pipeline_mode=pl.Buffered(1))
            for h in (0, 1)
        ]
        more_in += [whole((1, d))]
        more_out = [row(d), row(PAIR)]
        more_shapes = [jax.ShapeDtypeStruct((n, d), F32), jax.ShapeDtypeStruct((n, PAIR), F32)]
        more_scratch = [pltpu.VMEM((4 * mrows, d), BF16)]
        more = [o0, merge, merge, merge_bias]
    return pl.pallas_call(
        functools.partial(forward_kernel, own=own),
        grid_spec=pltpu.PrefetchScalarGridSpec(
            num_scalar_prefetch=3,
            grid=(packs,),
            in_specs=[smem(), whole(delta.shape), row(d)]
            + weights
            + biases
            + more_in,
            out_specs=[row(cols)] * 5
            + [pl.BlockSpec((1, heads, LONG, LONG), lambda i, *_: (i, 0, 0, 0))]
            + more_out,
            scratch_shapes=[pltpu.VMEM((3, d, cols), BF16), pltpu.VMEM((LONG, LONG), F32)] + more_scratch,
        ),
        out_shape=[out] * 4
        + [
            jax.ShapeDtypeStruct((n, cols), F32),
            jax.ShapeDtypeStruct((packs, heads, LONG, LONG), BF16),
        ]
        + more_shapes,
        compiler_params=kernel_params(63),
        cost_estimate=cost(1 if own else 4000),
        name="attend_own" if own else "attend_other",
    )(place, long_, item, tau, delta, x, wa, wb, bias, bias, *more)


def gelu_parts(u):
    phi = 0.5 + 0.5 * lax.erf(u * 0.7071067811865476)
    return phi, jnp.exp2(u * u * (-0.5 * LOG2E))


def feed_kernel(
    place, o0_ref, o1_ref, xh_ref, rs1_ref, gy_ref, mk_ref, ms_ref, mnear_ref, mfar_ref,
    ek_ref, es_ref, rk_ref, rs_ref,
    near_ref, far_ref, b0_ref, b1_ref, b2_ref, g1_ref, h1_ref, br_ref, g2_ref, h2_ref,
    out_ref, do_ref, act_ref, du_ref, n1_ref, dh2_ref, dh1b_ref, sum_ref, sbe_ref, send_ref,
    wm_ref, act_all, du_all, gp_ref, n1_all, dh2_all, dh1b_all, o_all, *, tiles, tile,
):
    step = pl.program_id(0)
    d = xh_ref.shape[1]
    hid = ek_ref.shape[1]
    mrows = mk_ref.shape[0]
    expand = (ek_ref, es_ref, near_ref.at[0:d], far_ref.at[0:d])
    reduce_ = (rk_ref, rs_ref, near_ref.at[d:d + hid], far_ref.at[d:d + hid])

    @pl.when(step == 0)
    def _():
        merge_rows(wm_ref, mk_ref, ms_ref, mnear_ref, mfar_ref)

    @pl.when(step < tiles)
    def _():
        here = pl.ds(pl.multiple_of(step * tile, tile), tile)
        g1, b1, br, g2, b2 = [ref[...] for ref in (g1_ref, h1_ref, br_ref, g2_ref, h2_ref)]
        b = joined_rows(b2_ref[...])
        wide = hid // PAIR
        parts = [
            jnp.concatenate([b[4 + wide * k + m:5 + wide * k + m] for m in range(wide)], axis=1) for k in range(2)
        ]
        first = place[0] == 0
        be = [b0_ref[...], b1_ref[...], jnp.where(first, *parts), jnp.where(first, *parts[::-1])]
        o_all[here, :mrows] = o0_ref[...]
        o_all[here, mrows:] = o1_ref[...]
        xh, rs = xh_ref[...], rs1_ref[:, 0:1]
        n1 = xh * g1 + b1
        low = n1.astype(BF16)
        n1_ref[...] = low
        n1_all[here] = low
        u = mm(low, expand[0][...])
        fed = n1 + br
        for k in range(4):
            later = mm(low, expand[k + 1][...]) if k < 3 else None
            at = slice(k * hid, (k + 1) * hid)
            u = u + be[k]
            phi, e = gelu_parts(u)
            act = (u * phi).astype(BF16)
            mine = slice(k // 2 * hid, (k // 2 + 1) * hid)
            if k % 2 == 0:
                act_ref[:, mine] = act
            else:
                act_all[here, mine] = act
            gp_ref[:, at] = (phi + u * (e * 0.3989422804014327)).astype(BF16)
            fed = fed + mm(act, reduce_[k][...])
            u = later
        c2 = fed - row_mean(fed)
        rs2 = lax.rsqrt(row_mean(c2 * c2) + 1e-05)
        xh2 = c2 * rs2
        out_ref[...] = xh2 * g2 + b2
        gy = gy_ref[...].astype(F32)
        gg = gy * g2
        dh2 = rs2 * ((gg - row_mean(gg)) - xh2 * row_mean(gg * xh2))
        dh2b = dh2.astype(BF16)
        dh2_ref[...] = dh2b
        dh2_all[here] = dh2b
        dn = dh2
        sbe = []
        da = mm_nt(dh2b, reduce_[0][...])
        for k in range(4):
            later = mm_nt(dh2b, reduce_[k + 1][...]) if k < 3 else None
            at = slice(k * hid, (k + 1) * hid)
            du = (da * gp_ref[:, at].astype(F32)).astype(BF16)
            mine = slice(k // 2 * hid, (k // 2 + 1) * hid)
            if k % 2 == 0:
                du_ref[:, mine] = du
            else:
                du_all[here, mine] = du
            sbe.append(col_sum(du.astype(F32)))
            dn = dn + mm_nt(du, expand[k][...])
            da = later
        gg1 = dn * g1
        dh1 = rs * ((gg1 - row_mean(gg1)) - xh * row_mean(gg1 * xh))
        dh1b = dh1.astype(BF16)
        dh1b_ref[...] = dh1b
        dh1b_all[here] = dh1b
        do_ref[...] = mm_nt(dh1b, wm_ref[...]).astype(BF16)
        sums = [col_sum(dh1), col_sum(dn * xh), col_sum(dn), col_sum(dh2), col_sum(gy * xh2), col_sum(gy)]
        sums = jnp.concatenate(sums + [jnp.zeros((2, d), F32)], axis=0)
        sbe = jnp.broadcast_to(jnp.concatenate(sbe, axis=1), sbe_ref.shape)

        @pl.when(step == 0)
        def _():
            sum_ref[...] = sums
            sbe_ref[...] = sbe

        @pl.when(step > 0)
        def _():
            sum_ref[...] += sums
            sbe_ref[...] += sbe

    for slot in range(2):

        @pl.when(step == tiles + slot)
        def _(slot=slot):
            at = slice(slot * hid, (slot + 1) * hid)
            om = slice(slot * mrows, (slot + 1) * mrows)
            send_ref[0, 0:hid] = mm_tn(act_all[:, at], dh2_all[...]).astype(BF16)
            send_ref[0, hid:hid + d] = mm_tn(n1_all[...], du_all[:, at]).astype(BF16)
            rows = hid + d + mrows
            send_ref[0, hid + d:rows] = mm_tn(o_all[:, om], dh1b_all[...]).astype(BF16)
            send_ref[0, rows:] = small_rows(place[0] ^ 1, sum_ref[...], sbe_ref[...], slot, 1, hid)


def small_rows(which, sums, sbe, slot, h, hid):
    lo = (2 * slot + h) * hid
    part = jnp.where(which == 0, sums[0:3], sums[3:6])
    fill = jnp.zeros((SMALL - 4, sums.shape[1]), F32)
    return jnp.concatenate([sbe[0:1, lo:lo + hid], part, fill], axis=0).astype(BF16)


def feed(place, o0, o1, xh, rs1, gy, merge, mnear, mfar, expand, reduce_, near, far, be0, be1, vecs):
    n, d = xh.shape
    tile = 2 * LONG
    tiles = n // tile
    mrows, hid = merge.shape[0] // 2, expand.shape[1] // 2
    full_hid = 4 * hid
    at = lambda i: jnp.minimum(i, tiles - 1)
    row = lambda c: pl.BlockSpec((tile, c), lambda i, *_: (at(i), 0))
    once = pl.Buffered(1)
    by_row = lambda shape, h: pl.BlockSpec(shape, lambda i, place: (place[0] ^ h, 0), pipeline_mode=once)
    by_col = lambda shape, h: pl.BlockSpec(shape, lambda i, place: (0, place[0] ^ h), pipeline_mode=once)
    S = jax.ShapeDtypeStruct
    grows = hid + d + mrows + SMALL
    bias = lambda h: pl.BlockSpec((1, hid), lambda i, place: (0, place[0] ^ h), pipeline_mode=once)
    return pl.pallas_call(
        functools.partial(feed_kernel, tiles=tiles, tile=tile),
        grid_spec=pltpu.PrefetchScalarGridSpec(
            num_scalar_prefetch=1,
            grid=(tiles + 2,),
            in_specs=[pl.BlockSpec((tile, mrows), lambda i, *_: (at(i), 1))] * 2
            + [row(d), row(rs1.shape[1]), row(d)]
            + [by_row((mrows, d), h) for h in (0, 1)]
            + [pl.BlockSpec((d, PAIR), lambda *_: (3, 0), pipeline_mode=once)] * 2
            + [by_col((d, hid), h) for h in (0, 1)]
            + [by_row((hid, d), h) for h in (0, 1)]
            + [whole(near.shape), whole(far.shape)]
            + [bias(0), bias(1), bias_block(d)]
            + [whole((1, d))] * 5,
            out_specs=[row(d), row(d), row(2 * hid), row(2 * hid), row(d), row(d), row(d)]
            + [
                pl.BlockSpec((8, d), lambda i, *_: (0, 0)),
                pl.BlockSpec((8, full_hid), lambda i, *_: (0, 0)),
                pl.BlockSpec((1, grows, d), lambda i, *_: (jnp.maximum(i - tiles, 0), 0, 0)),
            ],
            scratch_shapes=[
                pltpu.VMEM((4 * mrows, d), BF16),
                pltpu.VMEM((n, 2 * hid), BF16),
                pltpu.VMEM((n, 2 * hid), BF16),
                pltpu.VMEM((tile, full_hid), BF16),
                pltpu.VMEM((n, d), BF16),
                pltpu.VMEM((n, d), BF16),
                pltpu.VMEM((n, d), BF16),
                pltpu.VMEM((n, 2 * mrows), BF16),
            ],
        ),
        out_shape=[S((n, d), F32), S((n, d), BF16)]
        + [S((n, 2 * hid), BF16)] * 2
        + [S((n, d), BF16)] * 3
        + [S((8, d), F32), S((8, full_hid), F32), S((2, grows, d), BF16)],
        compiler_params=kernel_params(63),
        cost_estimate=cost(60),
        name="feed",
    )(
        place, o0, o1, xh, rs1, gy, merge, merge, mnear, mfar, expand, expand, reduce_, reduce_,
        near, far, be0, be0, be1, *vecs,
    )


def feed_grad_kernel(
    place, act_hbm, du_hbm, n1_hbm, dh2_hbm, dh1b_hbm, o0_hbm, o1_hbm, sum_ref, sbe_ref, keep_hbm,
    act, du, n1, dh2, dh1b, o, keep, sems, out_sems,
):
    hid, d, mrows = act.shape[2], n1.shape[1], o.shape[2]

    def fetch(src, dst, k):
        copy = pltpu.make_async_copy(src, dst, sems.at[k])
        copy.start()
        return copy

    cols = lambda s: (slice(None), pl.ds(s * hid, hid))
    heads = lambda ref: ref.at[:, pl.ds(0, mrows)]
    third = n1.shape[0] // 3
    parts = [pl.ds(k * third, third) for k in range(3)]
    order = tuple(
        pair
        for p in parts
        for pair in ((act_hbm.at[p, pl.ds(hid, hid)], act.at[1, p]), (dh2_hbm.at[p], dh2.at[p]))
    ) + (
        (n1_hbm, n1), (du_hbm.at[cols(1)], du.at[1]),
        (heads(o1_hbm), o.at[1]), (dh1b_hbm, dh1b),
        (act_hbm.at[cols(0)], act.at[0]), (du_hbm.at[cols(0)], du.at[0]), (heads(o0_hbm), o.at[0]),
    )
    copies = [fetch(src, dst, k) for k, (src, dst) in enumerate(order)]
    flush = []
    rows = hid + d + mrows
    for slot, waits in ((1, (0, 6, 8, 10)), (0, (10, 11, 12, 13))):
        if slot == 1:
            total = None
            for k, p in enumerate(parts):
                copies[2 * k].wait()
                copies[2 * k + 1].wait()
                term = mm_tn(act[slot, p], dh2[p])
                total = term if total is None else total + term
        else:
            copies[10].wait()
            total = mm_tn(act[slot], dh2[...])
        keep[slot, 0:hid] = total.astype(BF16)
        for k in range(waits[1], waits[2]):
            copies[k].wait()
        keep[slot, hid:hid + d] = mm_tn(n1[...], du[slot]).astype(BF16)
        for k in range(waits[2], waits[3]):
            copies[k].wait()
        keep[slot, hid + d:rows] = mm_tn(o[slot], dh1b[...]).astype(BF16)
        keep[slot, rows:] = small_rows(place[0], sum_ref[...], sbe_ref[...], slot, 0, hid)
        out = pltpu.make_async_copy(keep.at[slot], keep_hbm.at[slot], out_sems.at[slot])
        out.start()
        flush.append(out)
    for out in flush:
        out.wait()


def feed_grad(place, act, du, n1, dh2, dh1b, o0, o1, sums, sbe):
    n, d = n1.shape
    hid, mrows = act.shape[1] // 2, o0.shape[1] // 2
    grows = hid + d + mrows + SMALL
    hbm = pl.BlockSpec(memory_space=pl.ANY)
    return pl.pallas_call(
        feed_grad_kernel,
        in_specs=[smem()] + [hbm] * 7 + [whole(sums.shape), whole(sbe.shape)],
        out_specs=hbm,
        out_shape=jax.ShapeDtypeStruct((2, grows, d), BF16),
        scratch_shapes=[
            pltpu.VMEM((2, n, hid), BF16),
            pltpu.VMEM((2, n, hid), BF16),
            pltpu.VMEM((n, d), BF16),
            pltpu.VMEM((n, d), BF16),
            pltpu.VMEM((n, d), BF16),
            pltpu.VMEM((2, n, mrows), BF16),
            pltpu.VMEM((2, grows, d), BF16),
            pltpu.SemaphoreType.DMA((13,)),
            pltpu.SemaphoreType.DMA((2,)),
        ],
        compiler_params=kernel_params(58),
        cost_estimate=cost(9),
        name="feed_grad",
    )(place, act, du, n1, dh2, dh1b, o0, o1, sums, sbe)


def backward_kernel(place, long_ref, item_ref, tau_ref, *refs, sets, steps, group):
    step = pl.program_id(0)
    width = group * LONG
    per = [refs[7 * s:7 * s + 7] for s in range(sets)]
    x_hbm = refs[7 * sets]
    outs = refs[7 * sets + 1:7 * sets + 1 + 2 * sets]
    x_all, d_all, sem = refs[-3:]
    fetch = pltpu.make_async_copy(x_hbm, x_all, sem)

    @pl.when(step == 0)
    def _():
        fetch.start()

    lane = lax.broadcasted_iota(jnp.int32, (1, PAIR), 1)
    first = lane < HEAD
    ready = []
    for m in range(group):
        _, rows = pack_rows(step * group + m + place[1], long_ref, item_ref)
        tau = pack_tau(rows, tau_ref) * HEAD**-0.5
        here = slice(m * LONG, (m + 1) * LONG)
        for s in range(sets):
            _, _, v_ref, g_ref, o_ref, r_ref, _ = per[s]
            g = g_ref[here].astype(F32) * r_ref[here]
            low = g.astype(BF16)
            scaled = (g * tau).astype(BF16).astype(F32)
            d = scaled * o_ref[here].astype(F32)
            v = v_ref[here].astype(F32)
            for j in range(2):
                own = first if j == 0 else jnp.logical_not(first)
                spare = HEAD if j == 0 else 0
                dd = jnp.sum(jnp.where(own, d, 0.0), axis=1, keepdims=True)
                high = dd.astype(BF16).astype(F32)
                left = jnp.where(lane == spare, -high, jnp.where(lane == spare + 1, high - dd, 0.0))
                left = jnp.where(own, scaled, left).astype(BF16)
                ones = jnp.where(jnp.logical_or(lane == spare, lane == spare + 1), 1.0, 0.0)
                right = jnp.where(own, v, ones).astype(BF16)
                ready.append((left, right, low[:, j * HEAD:(j + 1) * HEAD], m, s, j))
    res = []
    t = mm_nt(*ready[0][:2])
    for n, (_, _, low, m, s, j) in enumerate(ready):
        later = mm_nt(*ready[n + 1][:2]) if n + 1 < len(ready) else None
        q_ref, k_ref, _, _, _, _, p_ref = per[s]
        here = slice(m * LONG, (m + 1) * LONG)
        at = slice(j * HEAD, (j + 1) * HEAD)
        w = p_ref[m, j]
        r = (w.astype(F32) * t).astype(BF16)
        res.append((mm(r, k_ref[here, at]), mm_tn(q_ref[here, at], r), mm_tn(low, w)))
        t = later
        if j == 1:
            a, b = res[-2:]
            out = [jnp.concatenate([a[0], b[0]], axis=1).astype(BF16)]
            out += [jnp.concatenate([a[k], b[k]], axis=0).T.astype(BF16) for k in (1, 2)]
            spot = pl.ds(pl.multiple_of(step * width + m * LONG, LONG), LONG)
            for k in range(3):
                outs[2 * s][here, k * PAIR:(k + 1) * PAIR] = out[k]
                d_all[spot, (3 * s + k) * PAIR:(3 * s + k + 1) * PAIR] = out[k]

    @pl.when(step == steps - 1)
    def _():
        fetch.wait()
        depth = x_all.shape[1]
        res = mm_tn(x_all[...], d_all[...]).astype(BF16)
        for s in range(sets):
            grad_ref = outs[2 * s + 1]
            for k in range(3):
                grad_ref[k * depth:(k + 1) * depth] = res[:, (3 * s + k) * PAIR:(3 * s + k + 1) * PAIR]
            cols = [slice((3 * s + k) * PAIR, (3 * s + k + 1) * PAIR) for k in (0, 2)]
            dq, dv = [col_sum(d_all[:, at].astype(F32)) for at in cols]
            small = jnp.concatenate([dq, dv, jnp.zeros((SMALL_PAIR - 2, PAIR), F32)], axis=0)
            grad_ref[3 * depth:] = small.astype(BF16)


def attend_back(place, long_, item, tau, saved, x, quarters):
    n, d = x.shape
    sets = len(quarters)
    group = 2 // sets
    width = group * LONG
    steps = n // width
    col = lambda c: pl.BlockSpec((width, PAIR), lambda i, *_: (i, c))
    S = jax.ShapeDtypeStruct
    rows = 3 * d + SMALL_PAIR
    specs, operands = [], []
    for slot, h in quarters:
        p = saved[slot][-1]
        specs += [col(h)] * 3 + [col(2 * slot + h)] + [col(h)] * 2
        specs += [pl.BlockSpec((group, 2) + p.shape[2:], lambda i, *_, h=h: (i, h, 0, 0))]
        operands += list(saved[slot])
    return pl.pallas_call(
        functools.partial(backward_kernel, sets=sets, steps=steps, group=group),
        grid_spec=pltpu.PrefetchScalarGridSpec(
            num_scalar_prefetch=3,
            grid=(steps,),
            in_specs=[smem()] + specs + [pl.BlockSpec(memory_space=pl.ANY)],
            out_specs=[
                pl.BlockSpec((width, 3 * PAIR), lambda i, *_: (i, 0)),
                pl.BlockSpec((rows, PAIR), lambda i, *_: (0, 0)),
            ]
            * sets,
            scratch_shapes=[
                pltpu.VMEM((n, d), BF16), pltpu.VMEM((n, sets * 3 * PAIR), BF16), pltpu.SemaphoreType.DMA,
            ],
        ),
        out_shape=[S((n, 3 * PAIR), BF16), S((rows, PAIR), BF16)] * sets,
        compiler_params=kernel_params(58),
        cost_estimate=cost(8),
        name="attend_back_" + "_".join("%d%d" % q for q in quarters),
    )(place, long_, item, tau, *operands, x)


def input_grad_kernel(place, dh1_ref, ka_ref, sa_ref, near_ref, far_ref, *refs):
    d_refs, (out_ref, w_ref) = refs[:4], refs[-2:]

    @pl.when(pl.program_id(0) == 0)
    def _():
        for j in range(3):
            for k, ref in enumerate((ka_ref, sa_ref, near_ref, far_ref)):
                lo = (k * 3 + j) * PAIR
                w_ref[:, lo:lo + PAIR] = projection(ref, j, w_ref.shape[0])

    d = jnp.concatenate([ref[...] for ref in d_refs], axis=1)
    out_ref[...] = dh1_ref[...].astype(F32) + mm_nt(d, w_ref[...])


def input_grad(place, dh1, weight, near, far, grads, part, held=None):
    n, d = dh1.shape
    tile = LONG
    begin, end = [n // tile * k // 3 for k in ((0, 2) if part == 0 else (2, 3))]
    steps = end - begin
    cols = grads[0].shape[1]
    row = lambda c: pl.BlockSpec((tile, c), lambda i, *_: (begin + i, 0))
    pick = lambda h: pl.BlockSpec((3, d, PAIR), lambda i, place: (0, 0, place[0] ^ h), pipeline_mode=pl.Buffered(1))
    extra = [] if held is None else [held]
    return pl.pallas_call(
        input_grad_kernel,
        grid_spec=pltpu.PrefetchScalarGridSpec(
            num_scalar_prefetch=1,
            grid=(steps,),
            in_specs=[row(d), pick(0), pick(1), whole(near.shape), whole(far.shape)]
            + [row(cols)] * 4
            + [pl.BlockSpec(memory_space=pl.ANY)] * len(extra),
            out_specs=row(d),
            scratch_shapes=[pltpu.VMEM((d, 4 * cols), BF16)],
        ),
        out_shape=jax.ShapeDtypeStruct((n, d), F32),
        input_output_aliases={10: 0} if extra else {},
        compiler_params=kernel_params(58),
        cost_estimate=cost(8000),
        name="input_grad%d" % part,
    )(place, dh1, weight, weight, near, far, *grads, *extra)


def flip(v, axis, mask=1):
    size = lax.axis_size(axis)
    return lax.ppermute(v, axis, [(i, i ^ mask) for i in range(size)])


def add_low(*parts):
    return functools.reduce(lambda a, b: a + b, [p.astype(F32) for p in parts]).astype(BF16)


def piece(v, which, rows):
    return lax.dynamic_slice_in_dim(v, which * rows, rows, v.ndim - 2)


def split_rows(v):
    high = v.astype(BF16)
    left = v - high.astype(F32)
    mid = left.astype(BF16)
    low = (left - mid.astype(F32)).astype(BF16)
    return jnp.concatenate([high, mid, low, jnp.zeros_like(high)], axis=0)


def joined_rows(v):
    rows = v.shape[0] // 4
    v = v.astype(F32)
    return v[:rows] + v[rows:2 * rows] + v[2 * rows:3 * rows]


def pull(copies, sems):
    copies = [pltpu.make_async_copy(src, dst, sems.at[k]) for k, (src, dst) in enumerate(copies)]
    for copy in copies:
        copy.start()
    return copies


def prepare_kernel(project_hbm, merge_hbm, pb_ref, eb_ref, out_ref, place_ref, sems, *, packs):
    core, side, outer = lax.axis_index("core"), lax.axis_index("tensor"), lax.axis_index("outer")
    d, mrows = project_hbm.shape[1], merge_hbm.shape[0] // 2
    half = lambda n: pl.ds(pl.multiple_of(core * n, n), n)
    copies = pull(
        [(project_hbm.at[j, :, half(PAIR)], out_ref.at[pl.ds(j * d, d)]) for j in range(3)]
        + [
            (merge_hbm.at[half(mrows), pl.ds(k * PAIR, PAIR)], out_ref.at[pl.ds(3 * d + k * mrows, mrows)])
            for k in range(d // PAIR)
        ],
        sems,
    )
    at = lambda k: slice(k * PAIR, (k + 1) * PAIR)
    rows = [pb_ref[j:j + 1, at(k)] for j in range(2) for k in range(2)]
    rows += [eb_ref[:, at(k)] for k in range(eb_ref.shape[1] // PAIR)]
    fill = jnp.zeros((BIAS_ROWS // 4 - len(rows), PAIR), F32)
    out_ref[4 * d:] = split_rows(jnp.concatenate(rows + [fill], axis=0))
    place_ref[0] = core
    place_ref[1] = side * packs
    place_ref[2] = outer % 2
    for copy in copies:
        copy.wait()


def prepare_rest_kernel(place, expand_hbm, reduce_hbm, out_ref, sems):
    hid, d = expand_hbm.shape[1] // 2, expand_hbm.shape[0]
    half = pl.ds(pl.multiple_of(place[0] * hid, hid), hid)
    pairs = [(expand_hbm.at[:, half], out_ref.at[pl.ds(0, d)]), (reduce_hbm.at[half], out_ref.at[pl.ds(d, hid)])]
    for copy in pull(pairs, sems):
        copy.wait()


def prepare(project, merge, project_bias, expand_bias, packs):
    d, hidden = merge.shape[1], expand_bias.shape[0]
    S = jax.ShapeDtypeStruct
    hbm = pl.BlockSpec(memory_space=pl.ANY)
    return pl.pallas_call(
        functools.partial(prepare_kernel, packs=packs),
        in_specs=[hbm] * 2 + [whole(project_bias.shape), whole((1, hidden))],
        out_specs=[whole((4 * d + BIAS_ROWS, PAIR)), smem()],
        out_shape=[S((4 * d + BIAS_ROWS, PAIR), BF16), S((3,), jnp.int32)],
        scratch_shapes=[pltpu.SemaphoreType.DMA((3 + d // PAIR,))],
        compiler_params=kernel_params(63),
        cost_estimate=cost(3),
        name="prepare",
    )(project, merge, project_bias, expand_bias[None])


def prepare_rest(place, expand, reduce_):
    d, hid = expand.shape[0], expand.shape[1] // 2
    hbm = pl.BlockSpec(memory_space=pl.ANY)
    return pl.pallas_call(
        prepare_rest_kernel,
        in_specs=[smem(), hbm, hbm],
        out_specs=whole((d + hid, d)),
        out_shape=jax.ShapeDtypeStruct((d + hid, d), BF16),
        scratch_shapes=[pltpu.SemaphoreType.DMA((2,))],
        compiler_params=kernel_params(63),
        cost_estimate=cost(3),
        name="prepare_rest",
    )(place, expand, reduce_)


def combine_kernel(place, keep_ref, got_ref, ax_ref, a0_ref, send_ref, keep_out_ref):
    step = pl.program_id(0)
    total = (keep_ref[...].astype(F32) + got_ref[...].astype(F32)).astype(BF16)

    @pl.when(step < 2)
    def _():
        a0_ref[...] = total[0]
        ax_ref[...] = total[1]

    @pl.when(step == 2)
    def _():
        send_ref[...] = total

    @pl.when(step == 3)
    def _():
        keep_out_ref[...] = total


def combine(place, keep, got):
    _, rows, d = keep.shape
    half = rows // 4
    S = jax.ShapeDtypeStruct
    pick = lambda i, place: (0, jnp.where(i < 2, i, jnp.where(i == 2, 3 - place[2], 2 + place[2])), 0)
    first = pl.BlockSpec((half, d), lambda i, *_: (jnp.minimum(i, 1), 0))
    both = pl.BlockSpec((2, half, d), lambda i, *_: (0, 0, 0))
    return pl.pallas_call(
        combine_kernel,
        grid_spec=pltpu.PrefetchScalarGridSpec(
            num_scalar_prefetch=1,
            grid=(4,),
            in_specs=[pl.BlockSpec((2, half, d), pick)] * 2,
            out_specs=[first, first, both, both],
        ),
        out_shape=[S((2 * half, d), BF16)] * 2 + [S((2, half, d), BF16)] * 2,
        compiler_params=kernel_params(20),
        cost_estimate=cost(3),
        name="combine",
    )(place, keep, got)


def unpack_kernel(place, from_ref, part_ref, *refs, small_at):
    if small_at is None:
        reduce_ref, expand_ref, merge_ref, project_ref, bias_ref = refs
    else:
        own_ref, refs = refs[0], refs[6:]
        reduce_ref, expand_ref, merge_ref, project_ref, bias_ref, hidden_ref = refs[:6]
        own, other = own_ref[0:8].astype(F32), from_ref[small_at:small_at + 8].astype(F32)
        low, high = [jnp.where(place[0] == k, own, other) for k in range(2)]
        hidden_ref[...] = jnp.concatenate([low[0:1], high[0:1]], axis=1).reshape(hidden_ref.shape)
        for k, ref in enumerate(refs[6:]):
            half = low if k < 3 else high
            ref[...] = half[k % 3 + 1:k % 3 + 2].reshape(ref.shape)
    hid, d, mrows = reduce_ref.shape[0], expand_ref.shape[0], merge_ref.shape[0]
    reduce_ref[...] = from_ref[0:hid].astype(F32)
    expand_ref[...] = from_ref[hid:hid + d].astype(F32)
    merge_ref[...] = from_ref[hid + d:hid + d + mrows].astype(F32)
    for j in range(3):
        project_ref[j] = part_ref[j * d:(j + 1) * d].astype(F32)
    bias_ref[...] = part_ref[3 * d:3 * d + 8].astype(F32)[0:2]


def unpack(place, own, other, own_part, other_part, hid, mrows):
    d = own.shape[1]
    small_at = hid + d + mrows
    S = jax.ShapeDtypeStruct
    shapes = [S((2 * hid, d), F32), S((d, 2 * hid), F32), S((2 * mrows, d), F32)]
    shapes += [S((3, d, 2 * PAIR), F32), S((2, 2 * PAIR), F32)]

    def call(which, operands, in_specs, out_shape, out_specs, **more):
        rows = lambda r: pl.BlockSpec((r, d), lambda i, place: (place[0] ^ which, 0))
        blocks = [rows(hid), pl.BlockSpec((d, hid), lambda i, place: (0, place[0] ^ which)), rows(mrows)]
        blocks += [
            pl.BlockSpec((3, d, PAIR), lambda i, place: (0, 0, place[0] ^ which)),
            pl.BlockSpec((2, PAIR), lambda i, place: (0, place[0] ^ which)),
        ]
        return pl.pallas_call(
            functools.partial(unpack_kernel, small_at=small_at if which else None),
            grid_spec=pltpu.PrefetchScalarGridSpec(
                num_scalar_prefetch=1, grid=(1,), in_specs=in_specs, out_specs=blocks + out_specs,
            ),
            out_shape=out_shape,
            compiler_params=kernel_params(24),
            cost_estimate=cost(3),
            name="unpack%d" % which,
            **more,
        )(place, *operands)

    held = call(0, [own, own_part], [whole(own.shape), whole(own_part.shape)], shapes, [])
    one = lambda size: pl.BlockSpec((size,), lambda *_: (0,))
    hbm = pl.BlockSpec(memory_space=pl.ANY)
    return call(
        1,
        [other, other_part, own] + list(held),
        [whole(other.shape), whole(other_part.shape)]
        + [pl.BlockSpec((SMALL, d), lambda *_: (small_at // SMALL, 0))]
        + [hbm] * 5,
        shapes + [S((2 * hid,), F32)] + [S((d,), F32)] * 6,
        [one(2 * hid)] + [one(d)] * 6,
        input_output_aliases={4: 0, 5: 1, 6: 2, 7: 3, 8: 4},
    )


def by_bits(bits, pieces):
    v = jnp.stack(pieces)
    v = jnp.where(bits % 2 == 0, v, jnp.stack([v[1], v[0], v[3], v[2]]))
    v = jnp.where(bits // 2 == 0, v, jnp.stack([v[2], v[3], v[0], v[1]]))
    return v.reshape((-1,) + v.shape[2:])


def row_layer(
    inputs,
    pack_long,
    item_table,
    tau_table,
    delta_table,
    project_weight,
    project_bias,
    merge_weight,
    merge_bias,
    first_gain,
    first_shift,
    expand_weight,
    expand_bias,
    reduce_weight,
    reduce_bias,
    second_gain,
    second_shift,
    grad_output,
):
    n, d = inputs.shape
    hid = expand_weight.shape[1] // 2
    mrows = merge_weight.shape[0] // 2
    outer = lax.axis_size("outer")
    y_bit, z_bit = lax.axis_index("outer") % 2, lax.axis_index("outer") // 2 % 2
    project_half, place = prepare(project_weight, merge_weight, project_bias, expand_bias, n // LONG)
    project_near = flip(project_half, "tensor")
    rest_half = prepare_rest(place, expand_weight, reduce_weight)
    rest_near = flip(rest_half, "tensor")

    table = (place, pack_long, item_table, tau_table)
    q0, k0, v0, o0, r0, p0 = attend(
        *table, delta_table, inputs, project_weight, project_weight, project_bias, True
    )
    project_near, o0 = lax.optimization_barrier((project_near, o0))
    project_far = flip(project_near, "core")
    q1, k1, v1, o1, r1, p1, xh, rs = attend(
        *table, delta_table, inputs, project_near, project_far, project_near, False,
        o0, merge_weight, merge_bias[None],
    )
    rest_near, o1 = lax.optimization_barrier((rest_near, o1))
    rest_far = flip(rest_near, "core")
    block_output, grad_att, act, du, n1, dh2, dh1b, sums, sbe, send = feed(
        place, o0, o1, xh, rs, grad_output, merge_weight, project_near, project_far, expand_weight, reduce_weight,
        rest_near, rest_far, expand_bias[None], project_near,
        [v[None] for v in (first_gain, first_shift, reduce_bias, second_gain, second_shift)],
    )
    saved = ((q0, k0, v0, grad_att, o0, r0, p0), (q1, k1, v1, grad_att, o1, r1, p1))
    back = lambda x, *quarters: attend_back(*table, saved, x, quarters)

    got = flip(send, "core")
    keep = feed_grad(place, act, du, n1, dh2, dh1b, o0, o1, sums, sbe)
    got, keep = lax.optimization_barrier((got, keep))
    half = keep.shape[1] // 4
    a_x, a, b_y, b = combine(place, keep, got)
    x, a_x, b_y = lax.optimization_barrier((inputs, a_x, b_y))
    a_x, b_y = flip(a_x, "tensor"), flip(b_y, "outer", 1)
    d01, g01, d11, g11 = back(x, (0, 1), (1, 1))
    got01, got11 = flip(g01, "core"), flip(g11, "core")
    a_x, b_y, d11 = lax.optimization_barrier((a_x, b_y, d11))
    a, b = add_low(a, a_x), add_low(b, b_y)
    a_y, b_x = piece(a, 1 - y_bit, half), b[1]
    x, a_y, b_x = lax.optimization_barrier((x, a_y, b_x))
    a_y, b_x = flip(a_y, "outer", 1), flip(b_x, "tensor")
    d10, g10 = back(x, (1, 0))
    a_y, b_x, d10 = lax.optimization_barrier((a_y, b_x, d10))
    far = add_low(g10, got11)
    total = jnp.concatenate([add_low(piece(a, y_bit, half), a_y), add_low(b[0], b_x)])
    to_z = piece(total, 1 - z_bit, half)
    x, far, to_z = lax.optimization_barrier((x, far, to_z))
    far, to_z = flip(far, "tensor"), flip(to_z, "outer", 2)
    d00, g00 = back(x, (0, 0))
    far, to_z, d00 = lax.optimization_barrier((far, to_z, d00))
    feed_part = add_low(piece(total, z_bit, half), to_z)
    feed_part, g00 = lax.optimization_barrier((feed_part, g00))

    mine = add_low(g00, got01, far)
    rows = mine.shape[0] // 4
    to_y = flip(piece(mine, 1 - y_bit, 2 * rows), "outer", 1)
    came = flip(feed_part, "outer", 4)
    dx = functools.partial(input_grad, place, dh1b, project_weight, project_near, project_far)
    mine = add_low(piece(mine, y_bit, 2 * rows), to_y)
    to_z = piece(mine, 1 - z_bit, rows)
    d00, to_z, mine = lax.optimization_barrier((d00, to_z, mine))
    to_z = flip(to_z, "outer", 2)
    dx0 = dx((d00, d01, d10, d11), 0)
    to_z, came, dx0 = lax.optimization_barrier((to_z, came, dx0))
    project_part = add_low(piece(mine, z_bit, rows), to_z)
    feed_part = add_low(feed_part, came)
    project_part, feed_part, d00 = lax.optimization_barrier((project_part, feed_part, d00))
    came = flip(project_part, "outer", 4) if outer > 4 else jnp.zeros_like(project_part)
    by_y, by_z = flip(feed_part, "outer", 1), flip(feed_part, "outer", 2)
    dx1 = dx((d00, d01, d10, d11), 1, dx0)
    came, dx1, by_y, by_z = lax.optimization_barrier((came, dx1, by_y, by_z))
    mid = feed_part.shape[0] // 2
    cross = flip(by_z[:mid], "outer", 1), flip(by_y[mid:], "outer", 2)
    project_part = add_low(project_part, came)
    others = [flip(project_part, "outer", mask) for mask in (2, 1, 3)]
    cross, others = lax.optimization_barrier((cross, others))
    feed_pieces = [feed_part, by_y, by_z, jnp.concatenate(cross)]
    project_pieces = [project_part] + others
    total = by_bits(z_bit * 2 + y_bit, feed_pieces)
    project_total = by_bits(y_bit * 2 + z_bit, project_pieces)
    reduce_grad, expand_grad, merge_grad, project_grad, bias_grad, hidden, *small = unpack(
        place, total, flip(total, "core"), project_total, flip(project_total, "core"), hid, mrows
    )
    return (
        block_output,
        dx1,
        project_grad,
        bias_grad,
        merge_grad,
        *small[:3],
        expand_grad,
        hidden,
        reduce_grad,
        *small[3:],
    )


def rows_fit(mesh):
    size = mesh.shape["dp"]
    return mesh.shape["tensor"] == 2 and size in (8, 16)


def solution(mesh):
    if rows_fit(mesh):
        mesh = Mesh(mesh.devices.reshape(-1, 2, 2), ("outer", "core", "tensor"))
        body, dp = row_layer, ("outer", "core")
    else:
        body, dp = split_layer, ("dp",)
    all_ = P(dp + ("tensor",), None)
    placed = (
        all_,
        P(dp),
        P(dp),
        P(),
        P(),
        P(None, None, "tensor"),
        P(None, "tensor"),
        P("tensor", None),
        P(),
        P(),
        P(),
        P(None, "tensor"),
        P("tensor"),
        P("tensor", None),
        P(),
        P(),
        P(),
        all_,
    )
    return jax.shard_map(
        body,
        mesh=mesh,
        in_specs=placed,
        out_specs=(
            all_,
            all_,
            P(None, None, "tensor"),
            P(None, "tensor"),
            P("tensor", None),
            P(),
            P(),
            P(),
            P(None, "tensor"),
            P("tensor"),
            P("tensor", None),
            P(),
            P(),
            P(),
        ),
        check_vma=False,
    )
```

```python
import functools
import jax
import jax.numpy as jnp
from jax import lax
from jax.experimental import pallas as pl
from jax.experimental.pallas import tpu as pltpu
from jax.sharding import Mesh, PartitionSpec as P

HEAD = 64
SHORT = 96
LONG = 384
TABLE = 64
PAIR = 2 * HEAD
SMALL = 128
SMALL_PAIR = 32
BIAS_ROWS = 64
LOG2E = 1.4426950408889634
F32 = jnp.float32
BF16 = jnp.bfloat16


def layer_norm(values, gain, shift):
    mean = jnp.mean(values, axis=-1, keepdims=True)
    centred = values - mean
    spread = jnp.mean(centred * centred, axis=-1, keepdims=True)
    return centred * lax.rsqrt(spread + 1e-05) * gain + shift


def exact_gelu(values):
    return jax.nn.gelu(values, approximate=False)


def describe(pack_long, item_table, tau_table, delta_table):
    packs = pack_long.shape[0]
    per = LONG // SHORT
    count = packs * LONG
    longer = jnp.broadcast_to(pack_long[:, None] == 1, (packs, LONG)).reshape(count)
    lead_row = jnp.broadcast_to(item_table.reshape(packs, per)[:, :1], (packs, LONG)).reshape(count)
    each_row = jnp.broadcast_to(item_table[:, None], (packs * per, SHORT)).reshape(count)
    table_row = jnp.where(longer, lead_row, each_row)
    places = jnp.arange(count, dtype=jnp.int32)
    position = jnp.where(longer, places % LONG, places % SHORT)
    segment = jnp.where(longer, places // LONG * per, places // SHORT)
    picker = (table_row[:, None] == jnp.arange(TABLE, dtype=jnp.int32)[None, :]).astype(jnp.float32)
    tau_row = jnp.sum(picker * tau_table[None, :], axis=1)
    picked = jnp.dot(
        picker, delta_table, precision=lax.Precision.HIGHEST, preferred_element_type=jnp.float32
    )
    placed = position[:, None] == jnp.arange(LONG, dtype=jnp.int32)[None, :]
    delta_row = jnp.sum(jnp.where(placed, picked, 0.0), axis=1)
    return (tau_row, delta_row, segment)


def project(rows_all, project_weight, project_bias):
    query = (
        jnp.dot(rows_all, project_weight[0], preferred_element_type=jnp.float32) + project_bias[0]
    ).astype(jnp.bfloat16)
    keys = jnp.dot(rows_all, project_weight[1], preferred_element_type=jnp.float32).astype(
        jnp.bfloat16
    )
    values = (
        jnp.dot(rows_all, project_weight[2], preferred_element_type=jnp.float32) + project_bias[1]
    ).astype(jnp.bfloat16)
    return (query, keys, values)


def split_blocks(arrays):
    width = 2 * LONG
    return tuple((a.reshape((a.shape[0] // width, width) + a.shape[1:]) for a in arrays))


def block_scores(block_q, block_k, block_tau, block_delta, block_seg):
    raw = jnp.einsum("qhd,khd->hqk", block_q, block_k, preferred_element_type=jnp.float32)
    scores = (block_tau[None, :, None] * raw + block_delta[None, None, :]) * HEAD ** (-0.5)
    same = block_seg[:, None] == block_seg[None, :]
    return jnp.where(same[None], scores, -1e30)


def attend_forward(query, keys, values, tau_row, delta_row, segment):
    heads = query.shape[1] // HEAD
    shaped = tuple((a.reshape(a.shape[0], heads, HEAD) for a in (query, keys, values)))

    def one_block(parts):
        block_q, block_k, block_v, block_tau, block_delta, block_seg = parts
        scores = block_scores(block_q, block_k, block_tau, block_delta, block_seg)
        top = jnp.max(scores, axis=-1, keepdims=True)
        expo = jnp.exp(scores - top)
        totals = jnp.sum(expo, axis=-1, keepdims=True)
        weights = (expo / totals).astype(jnp.bfloat16)
        mixed = jnp.einsum("hqk,khd->qhd", weights, block_v, preferred_element_type=jnp.float32)
        return (
            mixed.reshape(mixed.shape[0], heads * HEAD).astype(jnp.bfloat16),
            top + jnp.log(totals),
        )

    attended, logsum = lax.map(one_block, split_blocks(shaped + (tau_row, delta_row, segment)))
    return (attended.reshape(query.shape), logsum)


def attend_backward(query, keys, values, grad_att, logsum, tau_row, delta_row, segment):
    heads = query.shape[1] // HEAD
    shaped = tuple((a.reshape(a.shape[0], heads, HEAD) for a in (query, keys, values, grad_att)))
    blocked = split_blocks(shaped + (tau_row, delta_row, segment))

    def one_block(parts):
        block_q, block_k, block_v, block_g, block_lse, block_tau, block_delta, block_seg = parts
        scores = block_scores(block_q, block_k, block_tau, block_delta, block_seg)
        probs = jnp.exp(scores - block_lse)
        dprob = jnp.einsum("qhd,khd->hqk", block_g, block_v, preferred_element_type=jnp.float32)
        dscore = probs * (dprob - jnp.sum(dprob * probs, axis=-1, keepdims=True))
        lowered = (dscore * HEAD ** (-0.5) * block_tau[None, :, None]).astype(jnp.bfloat16)
        grad_q = jnp.einsum("hqk,khd->qhd", lowered, block_k, preferred_element_type=jnp.float32)
        grad_k = jnp.einsum("hqk,qhd->khd", lowered, block_q, preferred_element_type=jnp.float32)
        grad_v = jnp.einsum(
            "hqk,qhd->khd", probs.astype(jnp.bfloat16), block_g, preferred_element_type=jnp.float32
        )
        width = block_q.shape[0]
        return tuple(
            (g.reshape(width, heads * HEAD).astype(jnp.bfloat16) for g in (grad_q, grad_k, grad_v))
        )

    grads = lax.map(one_block, blocked[:4] + (logsum,) + blocked[4:])
    return tuple((g.reshape(query.shape) for g in grads))


def row_term(left, right, form):
    return jnp.einsum(form, left, right, preferred_element_type=jnp.float32)


def feed_backward(feed_rows, preact_rows, active_rows, grad_fed, reduce_matrix):
    grad_reduce_weight = jnp.einsum(
        "tf,td->fd", active_rows, grad_fed, preferred_element_type=jnp.float32
    )
    grad_active = jnp.einsum(
        "td,fd->tf", grad_fed, reduce_matrix, preferred_element_type=jnp.float32
    )
    grad_preact = jax.vjp(exact_gelu, preact_rows)[1](grad_active)[0].astype(jnp.bfloat16)
    grad_expand_bias = jnp.sum(grad_preact.astype(jnp.float32), axis=0)
    grad_expand_weight = jnp.einsum(
        "td,tf->df", feed_rows, grad_preact, preferred_element_type=jnp.float32
    )
    return (grad_reduce_weight, grad_preact, grad_expand_bias, grad_expand_weight)


def split_layer(
    inputs,
    pack_long,
    item_table,
    tau_table,
    delta_table,
    project_weight,
    project_bias,
    merge_weight,
    merge_bias,
    first_gain,
    first_shift,
    expand_weight,
    expand_bias,
    reduce_weight,
    reduce_bias,
    second_gain,
    second_shift,
    grad_output,
):
    tau_row, delta_row, segment = describe(pack_long, item_table, tau_table, delta_table)
    rows_all = lax.all_gather(inputs, "tensor", axis=0, tiled=True)
    query, keys, values = project(rows_all, project_weight, project_bias)
    attended, logsum = attend_forward(query, keys, values, tau_row, delta_row, segment)
    mixed_part = lax.psum_scatter(
        row_term(attended, merge_weight, "tc,cd->td"), "tensor", scatter_dimension=0, tiled=True
    )
    first_sum = inputs.astype(jnp.float32) + (mixed_part + merge_bias)
    normed, first_back = jax.vjp(layer_norm, first_sum, first_gain, first_shift)
    normed_low = normed.astype(jnp.bfloat16)
    feed_all = lax.all_gather(normed_low, "tensor", axis=0, tiled=True)
    preact = jnp.dot(feed_all, expand_weight, preferred_element_type=jnp.float32) + expand_bias
    active = exact_gelu(preact).astype(jnp.bfloat16)
    fed_part = lax.psum_scatter(
        row_term(active, reduce_weight, "tf,fd->td"), "tensor", scatter_dimension=0, tiled=True
    )
    second_sum = normed + (fed_part + reduce_bias)
    block_output, second_back = jax.vjp(layer_norm, second_sum, second_gain, second_shift)
    grad_second, grad_gain_b, grad_shift_b = second_back(grad_output.astype(jnp.float32))
    grad_reduce_bias = jnp.sum(grad_second, axis=0)
    grad_fed = lax.all_gather(grad_second.astype(jnp.bfloat16), "tensor", axis=0, tiled=True)
    feed_again = lax.all_gather(normed_low, "tensor", axis=0, tiled=True)
    preact_again = (
        jnp.dot(feed_again, expand_weight, preferred_element_type=jnp.float32) + expand_bias
    )
    active_again = exact_gelu(preact_again).astype(jnp.bfloat16)
    grad_reduce_weight, grad_preact, grad_expand_bias, grad_expand_weight = feed_backward(
        feed_again, preact_again, active_again, grad_fed, reduce_weight
    )
    grad_normed = grad_second + lax.psum_scatter(
        row_term(grad_preact, expand_weight, "tf,df->td"), "tensor", scatter_dimension=0, tiled=True
    )
    grad_first, grad_gain_a, grad_shift_a = first_back(grad_normed)
    grad_merge_bias = jnp.sum(grad_first, axis=0)
    grad_att = lax.all_gather(grad_first.astype(jnp.bfloat16), "tensor", axis=0, tiled=True)
    grad_merge_weight = jnp.einsum(
        "tc,td->cd", attended, grad_att, preferred_element_type=jnp.float32
    )
    grad_attended = jnp.einsum(
        "td,cd->tc", grad_att, merge_weight, preferred_element_type=jnp.float32
    ).astype(jnp.bfloat16)
    rows_again = lax.all_gather(inputs, "tensor", axis=0, tiled=True)
    query_again, keys_again, values_again = project(rows_again, project_weight, project_bias)
    grad_q, grad_k, grad_v = attend_backward(
        query_again, keys_again, values_again, grad_attended, logsum, tau_row, delta_row, segment
    )
    grad_stack = jnp.stack((grad_q, grad_k, grad_v), axis=1)
    grad_project_weight = jnp.einsum(
        "td,tjc->jdc", rows_again, grad_stack, preferred_element_type=jnp.float32
    )
    grad_project_bias = jnp.stack(
        (jnp.sum(grad_q.astype(jnp.float32), axis=0), jnp.sum(grad_v.astype(jnp.float32), axis=0))
    )
    input_grad = grad_first + lax.psum_scatter(
        row_term(grad_stack, project_weight, "tjc,jdc->td").astype(jnp.bfloat16),
        "tensor",
        scatter_dimension=0,
        tiled=True,
    ).astype(jnp.float32)
    summed_all = (
        lax.psum(grad_project_weight.astype(jnp.bfloat16), "dp").astype(jnp.float32),
        lax.psum(grad_project_bias.astype(jnp.bfloat16), "dp").astype(jnp.float32),
        lax.psum(grad_merge_weight.astype(jnp.bfloat16), "dp").astype(jnp.float32),
        lax.psum(grad_expand_weight.astype(jnp.bfloat16), "dp").astype(jnp.float32),
        lax.psum(grad_expand_bias.astype(jnp.bfloat16), "dp").astype(jnp.float32),
        lax.psum(grad_reduce_weight.astype(jnp.bfloat16), "dp").astype(jnp.float32),
    )
    summed_attention = summed_all[:3]
    summed_feed = summed_all[3:]
    small = lax.psum(
        (grad_merge_bias, grad_gain_a, grad_shift_a, grad_reduce_bias, grad_gain_b, grad_shift_b),
        ("dp", "tensor"),
    )
    return (
        block_output,
        input_grad,
        summed_attention[0],
        summed_attention[1],
        summed_attention[2],
        small[0],
        small[1],
        small[2],
        summed_feed[0],
        summed_feed[1],
        summed_feed[2],
        small[3],
        small[4],
        small[5],
    )


def mm(a, b):
    return lax.dot_general(a, b, (((1,), (0,)), ((), ())), preferred_element_type=F32)


def mm_nt(a, b):
    return lax.dot_general(a, b, (((1,), (1,)), ((), ())), preferred_element_type=F32)


def mm_tn(a, b):
    return lax.dot_general(a, b, (((0,), (0,)), ((), ())), preferred_element_type=F32)


def col_sum(v):
    return jnp.sum(v, axis=0, keepdims=True)


def row_mean(v):
    return jnp.mean(v, axis=1, keepdims=True)


def pack_rows(pack, long_ref, item_ref):
    per = LONG // SHORT
    longer = long_ref[pack] == 1
    rows = [jnp.where(longer, item_ref[pack * per], item_ref[pack * per + k]) for k in range(per)]
    return longer, rows


def pack_tau(rows, tau_ref):
    slot = lax.broadcasted_iota(jnp.int32, (LONG, 1), 0) // SHORT
    tau = jnp.full((LONG, 1), tau_ref[rows[0]], F32)
    for k in range(1, LONG // SHORT):
        tau = jnp.where(slot == k, tau_ref[rows[k]], tau)
    return tau


def pack_bias(longer, rows, delta_ref):
    slot_r = lax.broadcasted_iota(jnp.int32, (LONG, 1), 0) // SHORT
    slot_c = lax.broadcasted_iota(jnp.int32, (1, LONG), 1) // SHORT
    shift = delta_ref[pl.ds(rows[0], 1), :]
    for k in range(1, LONG // SHORT):
        piece = jnp.broadcast_to(delta_ref[pl.ds(rows[k], 1), :], (8, LONG))
        piece = pltpu.roll(piece, SHORT * k, 1)[0:1]
        shift = jnp.where(jnp.logical_and(jnp.logical_not(longer), slot_c == k), piece, shift)
    mask = jnp.logical_or(longer, slot_r == slot_c)
    return jnp.where(mask, shift * (HEAD**-0.5 * LOG2E), -1e30)


def forward_kernel(
    place, long_ref, item_ref, tau_ref, delta_ref, x_ref, wa_ref, wb_ref, ba_ref, bb_ref, *refs, own,
):
    step = pl.program_id(0)
    if own:
        q_ref, k_ref, v_ref, o_ref, r_ref, p_ref, w_ref, bias_ref = refs
    else:
        o0_ref, mk_ref, ms_ref, bm_ref = refs[:4]
        q_ref, k_ref, v_ref, o_ref, r_ref, p_ref, xh_ref, rs_ref, w_ref, bias_ref, wm_ref = refs[4:]

    @pl.when(step == 0)
    def _():
        if not own:
            merge_rows(wm_ref, mk_ref, ms_ref, wa_ref.at[3 * x_ref.shape[1]:], wb_ref.at[3 * x_ref.shape[1]:])
        for k, ref in enumerate((wa_ref, wb_ref)):
            for j in range(3):
                w_ref[j, :, k * PAIR:(k + 1) * PAIR] = projection(ref, j, x_ref.shape[1])

    longer, rows = pack_rows(step + place[1], long_ref, item_ref)
    bias_ref[...] = pack_bias(longer, rows, delta_ref)
    tau = pack_tau(rows, tau_ref) * (HEAD**-0.5 * LOG2E)
    x = x_ref[...]
    if own:
        q_bias, v_bias = [jnp.concatenate([ba_ref[j:j + 1], bb_ref[j:j + 1]], axis=1) for j in range(2)]
    else:
        b = joined_rows(ba_ref[...])
        q_bias, v_bias = [
            jnp.where(
                place[0] == 0,
                jnp.concatenate([b[k:k + 1], b[k + 1:k + 2]], axis=1),
                jnp.concatenate([b[k + 1:k + 2], b[k:k + 1]], axis=1),
            )
            for k in (0, 2)
        ]
    q = (mm(x, w_ref[0]) + q_bias).astype(BF16)
    k = mm(x, w_ref[1]).astype(BF16)
    v = (mm(x, w_ref[2]) + v_bias).astype(BF16)
    q_ref[...] = q
    k_ref[...] = k
    v_ref[...] = v
    scaled = (q.astype(F32) * tau).astype(BF16)
    vf = v.astype(F32)
    first = lax.broadcasted_iota(jnp.int32, (1, PAIR), 1) < HEAD
    heads = q.shape[1] // HEAD

    def score(h):
        at = slice(h * HEAD, (h + 1) * HEAD)
        return mm_nt(scaled[:, at], k[:, at])

    def soften(s):
        s = s + bias_ref[...]
        return jnp.exp2(s - jnp.max(s, axis=1, keepdims=True)).astype(BF16)

    mixed = []

    def mix(h, w):
        p_ref[0, h] = w
        at = slice(h // 2 * PAIR, (h // 2 + 1) * PAIR)
        own = first if h % 2 == 0 else jnp.logical_not(first)
        mixed.append(mm(w, jnp.where(own, vf[:, at], 1.0).astype(BF16)))
        if h % 2 == 1:
            a, b = mixed[-2:]
            r = 1.0 / pltpu.roll(jnp.where(first, b, a), HEAD, 1)
            r_ref[:, at] = r
            o_ref[:, at] = (jnp.where(first, a, b) * r).astype(BF16)

    s = score(0)
    held = None
    for h in range(heads):
        later = score(h + 1) if h + 1 < heads else None
        w = soften(s)
        if held is not None:
            mix(h - 1, held)
        held, s = w, later
    mix(heads - 1, held)
    if not own:
        half = wm_ref.shape[0] // 2
        mixed = mm(o0_ref[...], wm_ref[:half]) + mm(o_ref[...], wm_ref[half:])
        h1 = x.astype(F32) + (mixed + bm_ref[...])
        c = h1 - row_mean(h1)
        rs = lax.rsqrt(row_mean(c * c) + 1e-05)
        xh_ref[...] = c * rs
        rs_ref[...] = jnp.broadcast_to(rs, rs_ref.shape)


def merge_rows(out_ref, keep_ref, other_ref, near_ref, far_ref):
    rows = keep_ref.shape[0]
    out_ref[0:rows] = keep_ref[...]
    out_ref[rows:2 * rows] = other_ref[...]
    for m, ref in ((2, near_ref), (3, far_ref)):
        for k in range(out_ref.shape[1] // PAIR):
            out_ref[m * rows:(m + 1) * rows, k * PAIR:(k + 1) * PAIR] = ref[k * rows:(k + 1) * rows]


def whole(shape):
    return pl.BlockSpec(shape, lambda *_: (0,) * len(shape), pipeline_mode=pl.Buffered(1))


def smem():
    return pl.BlockSpec(memory_space=pltpu.SMEM)


def kernel_params(mib):
    return pltpu.CompilerParams(vmem_limit_bytes=mib * 2**20)


def cost(us):
    return pl.CostEstimate(flops=int(us * 1.0e6), bytes_accessed=0, transcendentals=0)


def projection(ref, j, d):
    return ref[j] if len(ref.shape) == 3 else ref[j * d:(j + 1) * d]


def bias_block(d):
    return pl.BlockSpec((BIAS_ROWS, PAIR), lambda *_: (4 * d // BIAS_ROWS, 0), pipeline_mode=pl.Buffered(1))


def attend(place, long_, item, tau, delta, x, wa, wb, bias, own, o0=None, merge=None, merge_bias=None):
    n, d = x.shape
    packs = n // LONG
    cols = 2 * PAIR
    row = lambda c: pl.BlockSpec((LONG, c), lambda i, *_: (i, 0))
    if own:
        weights = [
            pl.BlockSpec((3, d, PAIR), lambda i, place, *_, h=h: (0, 0, place[0] ^ h), pipeline_mode=pl.Buffered(1))
            for h in (0, 1)
        ]
        biases = [pl.BlockSpec((2, PAIR), lambda i, place, *_, h=h: (0, place[0] ^ h)) for h in (0, 1)]
    else:
        weights, biases = [whole(wa.shape), whole(wb.shape)], [bias_block(d)] * 2
    out = jax.ShapeDtypeStruct((n, cols), BF16)
    heads = cols // HEAD
    more_in, more_out, more_shapes, more_scratch, more = [], [], [], [], []
    if not own:
        mrows = merge.shape[0] // 2
        more_in = [row(cols)]
        more_in += [
            pl.BlockSpec((mrows, d), lambda i, place, *_, h=h: (place[0] ^ h, 0), pipeline_mode=pl.Buffered(1))
            for h in (0, 1)
        ]
        more_in += [whole((1, d))]
        more_out = [row(d), row(PAIR)]
        more_shapes = [jax.ShapeDtypeStruct((n, d), F32), jax.ShapeDtypeStruct((n, PAIR), F32)]
        more_scratch = [pltpu.VMEM((4 * mrows, d), BF16)]
        more = [o0, merge, merge, merge_bias]
    return pl.pallas_call(
        functools.partial(forward_kernel, own=own),
        grid_spec=pltpu.PrefetchScalarGridSpec(
            num_scalar_prefetch=3,
            grid=(packs,),
            in_specs=[smem(), whole(delta.shape), row(d)]
            + weights
            + biases
            + more_in,
            out_specs=[row(cols)] * 5
            + [pl.BlockSpec((1, heads, LONG, LONG), lambda i, *_: (i, 0, 0, 0))]
            + more_out,
            scratch_shapes=[pltpu.VMEM((3, d, cols), BF16), pltpu.VMEM((LONG, LONG), F32)] + more_scratch,
        ),
        out_shape=[out] * 4
        + [
            jax.ShapeDtypeStruct((n, cols), F32),
            jax.ShapeDtypeStruct((packs, heads, LONG, LONG), BF16),
        ]
        + more_shapes,
        compiler_params=kernel_params(63),
        cost_estimate=cost(1 if own else 4000),
        name="attend_own" if own else "attend_other",
    )(place, long_, item, tau, delta, x, wa, wb, bias, bias, *more)


def gelu_parts(u):
    phi = 0.5 + 0.5 * lax.erf(u * 0.7071067811865476)
    return phi, jnp.exp2(u * u * (-0.5 * LOG2E))


def feed_kernel(
    place, o0_ref, o1_ref, xh_ref, rs1_ref, gy_ref, mk_ref, ms_ref, mnear_ref, mfar_ref,
    ek_ref, es_ref, rk_ref, rs_ref,
    near_ref, far_ref, b0_ref, b1_ref, b2_ref, g1_ref, h1_ref, br_ref, g2_ref, h2_ref,
    out_ref, do_ref, act_ref, du_ref, n1_ref, dh2_ref, dh1b_ref, sum_ref, sbe_ref, send_ref,
    wm_ref, act_all, du_all, gp_ref, n1_all, dh2_all, dh1b_all, o_all, *, tiles, tile,
):
    step = pl.program_id(0)
    d = xh_ref.shape[1]
    hid = ek_ref.shape[1]
    mrows = mk_ref.shape[0]
    expand = (ek_ref, es_ref, near_ref.at[0:d], far_ref.at[0:d])
    reduce_ = (rk_ref, rs_ref, near_ref.at[d:d + hid], far_ref.at[d:d + hid])

    @pl.when(step == 0)
    def _():
        merge_rows(wm_ref, mk_ref, ms_ref, mnear_ref, mfar_ref)

    @pl.when(step < tiles)
    def _():
        here = pl.ds(pl.multiple_of(step * tile, tile), tile)
        g1, b1, br, g2, b2 = [ref[...] for ref in (g1_ref, h1_ref, br_ref, g2_ref, h2_ref)]
        b = joined_rows(b2_ref[...])
        wide = hid // PAIR
        parts = [
            jnp.concatenate([b[4 + wide * k + m:5 + wide * k + m] for m in range(wide)], axis=1) for k in range(2)
        ]
        first = place[0] == 0
        be = [b0_ref[...], b1_ref[...], jnp.where(first, *parts), jnp.where(first, *parts[::-1])]
        o_all[here, :mrows] = o0_ref[...]
        o_all[here, mrows:] = o1_ref[...]
        xh, rs = xh_ref[...], rs1_ref[:, 0:1]
        n1 = xh * g1 + b1
        low = n1.astype(BF16)
        n1_ref[...] = low
        n1_all[here] = low
        u = mm(low, expand[0][...])
        fed = n1 + br
        for k in range(4):
            later = mm(low, expand[k + 1][...]) if k < 3 else None
            at = slice(k * hid, (k + 1) * hid)
            u = u + be[k]
            phi, e = gelu_parts(u)
            act = (u * phi).astype(BF16)
            mine = slice(k // 2 * hid, (k // 2 + 1) * hid)
            if k % 2 == 0:
                act_ref[:, mine] = act
            else:
                act_all[here, mine] = act
            gp_ref[:, at] = (phi + u * (e * 0.3989422804014327)).astype(BF16)
            fed = fed + mm(act, reduce_[k][...])
            u = later
        c2 = fed - row_mean(fed)
        rs2 = lax.rsqrt(row_mean(c2 * c2) + 1e-05)
        xh2 = c2 * rs2
        out_ref[...] = xh2 * g2 + b2
        gy = gy_ref[...].astype(F32)
        gg = gy * g2
        dh2 = rs2 * ((gg - row_mean(gg)) - xh2 * row_mean(gg * xh2))
        dh2b = dh2.astype(BF16)
        dh2_ref[...] = dh2b
        dh2_all[here] = dh2b
        dn = dh2
        sbe = []
        da = mm_nt(dh2b, reduce_[0][...])
        for k in range(4):
            later = mm_nt(dh2b, reduce_[k + 1][...]) if k < 3 else None
            at = slice(k * hid, (k + 1) * hid)
            du = (da * gp_ref[:, at].astype(F32)).astype(BF16)
            mine = slice(k // 2 * hid, (k // 2 + 1) * hid)
            if k % 2 == 0:
                du_ref[:, mine] = du
            else:
                du_all[here, mine] = du
            sbe.append(col_sum(du.astype(F32)))
            dn = dn + mm_nt(du, expand[k][...])
            da = later
        gg1 = dn * g1
        dh1 = rs * ((gg1 - row_mean(gg1)) - xh * row_mean(gg1 * xh))
        dh1b = dh1.astype(BF16)
        dh1b_ref[...] = dh1b
        dh1b_all[here] = dh1b
        do_ref[...] = mm_nt(dh1b, wm_ref[...]).astype(BF16)
        sums = [col_sum(dh1), col_sum(dn * xh), col_sum(dn), col_sum(dh2), col_sum(gy * xh2), col_sum(gy)]
        sums = jnp.concatenate(sums + [jnp.zeros((2, d), F32)], axis=0)
        sbe = jnp.broadcast_to(jnp.concatenate(sbe, axis=1), sbe_ref.shape)

        @pl.when(step == 0)
        def _():
            sum_ref[...] = sums
            sbe_ref[...] = sbe

        @pl.when(step > 0)
        def _():
            sum_ref[...] += sums
            sbe_ref[...] += sbe

    for slot in range(2):

        @pl.when(step == tiles + slot)
        def _(slot=slot):
            at = slice(slot * hid, (slot + 1) * hid)
            om = slice(slot * mrows, (slot + 1) * mrows)
            send_ref[0, 0:hid] = mm_tn(act_all[:, at], dh2_all[...]).astype(BF16)
            send_ref[0, hid:hid + d] = mm_tn(n1_all[...], du_all[:, at]).astype(BF16)
            rows = hid + d + mrows
            send_ref[0, hid + d:rows] = mm_tn(o_all[:, om], dh1b_all[...]).astype(BF16)
            send_ref[0, rows:] = small_rows(place[0] ^ 1, sum_ref[...], sbe_ref[...], slot, 1, hid)


def small_rows(which, sums, sbe, slot, h, hid):
    lo = (2 * slot + h) * hid
    part = jnp.where(which == 0, sums[0:3], sums[3:6])
    fill = jnp.zeros((SMALL - 4, sums.shape[1]), F32)
    return jnp.concatenate([sbe[0:1, lo:lo + hid], part, fill], axis=0).astype(BF16)


def feed(place, o0, o1, xh, rs1, gy, merge, mnear, mfar, expand, reduce_, near, far, be0, be1, vecs):
    n, d = xh.shape
    tile = 2 * LONG
    tiles = n // tile
    mrows, hid = merge.shape[0] // 2, expand.shape[1] // 2
    full_hid = 4 * hid
    at = lambda i: jnp.minimum(i, tiles - 1)
    row = lambda c: pl.BlockSpec((tile, c), lambda i, *_: (at(i), 0))
    once = pl.Buffered(1)
    by_row = lambda shape, h: pl.BlockSpec(shape, lambda i, place: (place[0] ^ h, 0), pipeline_mode=once)
    by_col = lambda shape, h: pl.BlockSpec(shape, lambda i, place: (0, place[0] ^ h), pipeline_mode=once)
    S = jax.ShapeDtypeStruct
    grows = hid + d + mrows + SMALL
    bias = lambda h: pl.BlockSpec((1, hid), lambda i, place: (0, place[0] ^ h), pipeline_mode=once)
    return pl.pallas_call(
        functools.partial(feed_kernel, tiles=tiles, tile=tile),
        grid_spec=pltpu.PrefetchScalarGridSpec(
            num_scalar_prefetch=1,
            grid=(tiles + 2,),
            in_specs=[pl.BlockSpec((tile, mrows), lambda i, *_: (at(i), 1))] * 2
            + [row(d), row(rs1.shape[1]), row(d)]
            + [by_row((mrows, d), h) for h in (0, 1)]
            + [pl.BlockSpec((d, PAIR), lambda *_: (3, 0), pipeline_mode=once)] * 2
            + [by_col((d, hid), h) for h in (0, 1)]
            + [by_row((hid, d), h) for h in (0, 1)]
            + [whole(near.shape), whole(far.shape)]
            + [bias(0), bias(1), bias_block(d)]
            + [whole((1, d))] * 5,
            out_specs=[row(d), row(d), row(2 * hid), row(2 * hid), row(d), row(d), row(d)]
            + [
                pl.BlockSpec((8, d), lambda i, *_: (0, 0)),
                pl.BlockSpec((8, full_hid), lambda i, *_: (0, 0)),
                pl.BlockSpec((1, grows, d), lambda i, *_: (jnp.maximum(i - tiles, 0), 0, 0)),
            ],
            scratch_shapes=[
                pltpu.VMEM((4 * mrows, d), BF16),
                pltpu.VMEM((n, 2 * hid), BF16),
                pltpu.VMEM((n, 2 * hid), BF16),
                pltpu.VMEM((tile, full_hid), BF16),
                pltpu.VMEM((n, d), BF16),
                pltpu.VMEM((n, d), BF16),
                pltpu.VMEM((n, d), BF16),
                pltpu.VMEM((n, 2 * mrows), BF16),
            ],
        ),
        out_shape=[S((n, d), F32), S((n, d), BF16)]
        + [S((n, 2 * hid), BF16)] * 2
        + [S((n, d), BF16)] * 3
        + [S((8, d), F32), S((8, full_hid), F32), S((2, grows, d), BF16)],
        compiler_params=kernel_params(63),
        cost_estimate=cost(60),
        name="feed",
    )(
        place, o0, o1, xh, rs1, gy, merge, merge, mnear, mfar, expand, expand, reduce_, reduce_,
        near, far, be0, be0, be1, *vecs,
    )


def feed_grad_kernel(
    place, act_hbm, du_hbm, n1_hbm, dh2_hbm, dh1b_hbm, o0_hbm, o1_hbm, sum_ref, sbe_ref, keep_hbm,
    act, du, n1, dh2, dh1b, o, keep, sems, out_sems,
):
    hid, d, mrows = act.shape[2], n1.shape[1], o.shape[2]

    def fetch(src, dst, k):
        copy = pltpu.make_async_copy(src, dst, sems.at[k])
        copy.start()
        return copy

    cols = lambda s: (slice(None), pl.ds(s * hid, hid))
    heads = lambda ref: ref.at[:, pl.ds(0, mrows)]
    third = n1.shape[0] // 3
    parts = [pl.ds(k * third, third) for k in range(3)]
    order = tuple(
        pair
        for p in parts
        for pair in ((act_hbm.at[p, pl.ds(hid, hid)], act.at[1, p]), (dh2_hbm.at[p], dh2.at[p]))
    ) + (
        (n1_hbm, n1), (du_hbm.at[cols(1)], du.at[1]),
        (heads(o1_hbm), o.at[1]), (dh1b_hbm, dh1b),
        (act_hbm.at[cols(0)], act.at[0]), (du_hbm.at[cols(0)], du.at[0]), (heads(o0_hbm), o.at[0]),
    )
    copies = [fetch(src, dst, k) for k, (src, dst) in enumerate(order)]
    flush = []
    rows = hid + d + mrows
    for slot, waits in ((1, (0, 6, 8, 10)), (0, (10, 11, 12, 13))):
        if slot == 1:
            total = None
            for k, p in enumerate(parts):
                copies[2 * k].wait()
                copies[2 * k + 1].wait()
                term = mm_tn(act[slot, p], dh2[p])
                total = term if total is None else total + term
        else:
            copies[10].wait()
            total = mm_tn(act[slot], dh2[...])
        keep[slot, 0:hid] = total.astype(BF16)
        for k in range(waits[1], waits[2]):
            copies[k].wait()
        keep[slot, hid:hid + d] = mm_tn(n1[...], du[slot]).astype(BF16)
        for k in range(waits[2], waits[3]):
            copies[k].wait()
        keep[slot, hid + d:rows] = mm_tn(o[slot], dh1b[...]).astype(BF16)
        keep[slot, rows:] = small_rows(place[0], sum_ref[...], sbe_ref[...], slot, 0, hid)
        out = pltpu.make_async_copy(keep.at[slot], keep_hbm.at[slot], out_sems.at[slot])
        out.start()
        flush.append(out)
    for out in flush:
        out.wait()


def feed_grad(place, act, du, n1, dh2, dh1b, o0, o1, sums, sbe):
    n, d = n1.shape
    hid, mrows = act.shape[1] // 2, o0.shape[1] // 2
    grows = hid + d + mrows + SMALL
    hbm = pl.BlockSpec(memory_space=pl.ANY)
    return pl.pallas_call(
        feed_grad_kernel,
        in_specs=[smem()] + [hbm] * 7 + [whole(sums.shape), whole(sbe.shape)],
        out_specs=hbm,
        out_shape=jax.ShapeDtypeStruct((2, grows, d), BF16),
        scratch_shapes=[
            pltpu.VMEM((2, n, hid), BF16),
            pltpu.VMEM((2, n, hid), BF16),
            pltpu.VMEM((n, d), BF16),
            pltpu.VMEM((n, d), BF16),
            pltpu.VMEM((n, d), BF16),
            pltpu.VMEM((2, n, mrows), BF16),
            pltpu.VMEM((2, grows, d), BF16),
            pltpu.SemaphoreType.DMA((13,)),
            pltpu.SemaphoreType.DMA((2,)),
        ],
        compiler_params=kernel_params(58),
        cost_estimate=cost(9),
        name="feed_grad",
    )(place, act, du, n1, dh2, dh1b, o0, o1, sums, sbe)


def backward_kernel(place, long_ref, item_ref, tau_ref, *refs, sets, steps, group):
    step = pl.program_id(0)
    width = group * LONG
    per = [refs[7 * s:7 * s + 7] for s in range(sets)]
    x_hbm = refs[7 * sets]
    outs = refs[7 * sets + 1:7 * sets + 1 + 2 * sets]
    x_all, d_all, sem = refs[-3:]
    fetch = pltpu.make_async_copy(x_hbm, x_all, sem)

    @pl.when(step == 0)
    def _():
        fetch.start()

    lane = lax.broadcasted_iota(jnp.int32, (1, PAIR), 1)
    first = lane < HEAD
    ready = []
    for m in range(group):
        _, rows = pack_rows(step * group + m + place[1], long_ref, item_ref)
        tau = pack_tau(rows, tau_ref) * HEAD**-0.5
        here = slice(m * LONG, (m + 1) * LONG)
        for s in range(sets):
            _, _, v_ref, g_ref, o_ref, r_ref, _ = per[s]
            g = g_ref[here].astype(F32) * r_ref[here]
            low = g.astype(BF16)
            scaled = (g * tau).astype(BF16).astype(F32)
            d = scaled * o_ref[here].astype(F32)
            v = v_ref[here].astype(F32)
            for j in range(2):
                own = first if j == 0 else jnp.logical_not(first)
                spare = HEAD if j == 0 else 0
                dd = jnp.sum(jnp.where(own, d, 0.0), axis=1, keepdims=True)
                high = dd.astype(BF16).astype(F32)
                left = jnp.where(lane == spare, -high, jnp.where(lane == spare + 1, high - dd, 0.0))
                left = jnp.where(own, scaled, left).astype(BF16)
                ones = jnp.where(jnp.logical_or(lane == spare, lane == spare + 1), 1.0, 0.0)
                right = jnp.where(own, v, ones).astype(BF16)
                ready.append((left, right, low[:, j * HEAD:(j + 1) * HEAD], m, s, j))
    res = []
    t = mm_nt(*ready[0][:2])
    for n, (_, _, low, m, s, j) in enumerate(ready):
        later = mm_nt(*ready[n + 1][:2]) if n + 1 < len(ready) else None
        q_ref, k_ref, _, _, _, _, p_ref = per[s]
        here = slice(m * LONG, (m + 1) * LONG)
        at = slice(j * HEAD, (j + 1) * HEAD)
        w = p_ref[m, j]
        r = (w.astype(F32) * t).astype(BF16)
        res.append((mm(r, k_ref[here, at]), mm_tn(q_ref[here, at], r), mm_tn(low, w)))
        t = later
        if j == 1:
            a, b = res[-2:]
            out = [jnp.concatenate([a[0], b[0]], axis=1).astype(BF16)]
            out += [jnp.concatenate([a[k], b[k]], axis=0).astype(BF16).T for k in (1, 2)]
            spot = pl.ds(pl.multiple_of(step * width + m * LONG, LONG), LONG)
            for k in range(3):
                outs[2 * s][here, k * PAIR:(k + 1) * PAIR] = out[k]
                d_all[spot, (3 * s + k) * PAIR:(3 * s + k + 1) * PAIR] = out[k]

    @pl.when(step == steps - 1)
    def _():
        fetch.wait()
        depth = x_all.shape[1]
        res = mm_tn(x_all[...], d_all[...]).astype(BF16)
        for s in range(sets):
            grad_ref = outs[2 * s + 1]
            for k in range(3):
                grad_ref[k * depth:(k + 1) * depth] = res[:, (3 * s + k) * PAIR:(3 * s + k + 1) * PAIR]
            cols = [slice((3 * s + k) * PAIR, (3 * s + k + 1) * PAIR) for k in (0, 2)]
            dq, dv = [col_sum(d_all[:, at].astype(F32)) for at in cols]
            small = jnp.concatenate([dq, dv, jnp.zeros((SMALL_PAIR - 2, PAIR), F32)], axis=0)
            grad_ref[3 * depth:] = small.astype(BF16)


def attend_back(place, long_, item, tau, saved, x, quarters):
    n, d = x.shape
    sets = len(quarters)
    group = 2 // sets
    width = group * LONG
    steps = n // width
    col = lambda c: pl.BlockSpec((width, PAIR), lambda i, *_: (i, c))
    S = jax.ShapeDtypeStruct
    rows = 3 * d + SMALL_PAIR
    specs, operands = [], []
    for slot, h in quarters:
        p = saved[slot][-1]
        specs += [col(h)] * 3 + [col(2 * slot + h)] + [col(h)] * 2
        specs += [pl.BlockSpec((group, 2) + p.shape[2:], lambda i, *_, h=h: (i, h, 0, 0))]
        operands += list(saved[slot])
    return pl.pallas_call(
        functools.partial(backward_kernel, sets=sets, steps=steps, group=group),
        grid_spec=pltpu.PrefetchScalarGridSpec(
            num_scalar_prefetch=3,
            grid=(steps,),
            in_specs=[smem()] + specs + [pl.BlockSpec(memory_space=pl.ANY)],
            out_specs=[
                pl.BlockSpec((width, 3 * PAIR), lambda i, *_: (i, 0)),
                pl.BlockSpec((rows, PAIR), lambda i, *_: (0, 0)),
            ]
            * sets,
            scratch_shapes=[
                pltpu.VMEM((n, d), BF16), pltpu.VMEM((n, sets * 3 * PAIR), BF16), pltpu.SemaphoreType.DMA,
            ],
        ),
        out_shape=[S((n, 3 * PAIR), BF16), S((rows, PAIR), BF16)] * sets,
        compiler_params=kernel_params(58),
        cost_estimate=cost(8),
        name="attend_back_" + "_".join("%d%d" % q for q in quarters),
    )(place, long_, item, tau, *operands, x)


def input_grad_kernel(place, dh1_ref, ka_ref, sa_ref, near_ref, far_ref, *refs):
    d_refs, (out_ref, w_ref) = refs[:4], refs[-2:]

    @pl.when(pl.program_id(0) == 0)
    def _():
        for j in range(3):
            for k, ref in enumerate((ka_ref, sa_ref, near_ref, far_ref)):
                lo = (k * 3 + j) * PAIR
                w_ref[:, lo:lo + PAIR] = projection(ref, j, w_ref.shape[0])

    d = jnp.concatenate([ref[...] for ref in d_refs], axis=1)
    out_ref[...] = dh1_ref[...].astype(F32) + mm_nt(d, w_ref[...])


def input_grad(place, dh1, weight, near, far, grads):
    n, d = dh1.shape
    tile = LONG
    cols = grads[0].shape[1]
    row = lambda c: pl.BlockSpec((tile, c), lambda i, *_: (i, 0))
    pick = lambda h: pl.BlockSpec((3, d, PAIR), lambda i, place: (0, 0, place[0] ^ h), pipeline_mode=pl.Buffered(1))
    return pl.pallas_call(
        input_grad_kernel,
        grid_spec=pltpu.PrefetchScalarGridSpec(
            num_scalar_prefetch=1,
            grid=(n // tile,),
            in_specs=[row(d), pick(0), pick(1), whole(near.shape), whole(far.shape)] + [row(cols)] * 4,
            out_specs=row(d),
            scratch_shapes=[pltpu.VMEM((d, 4 * cols), BF16)],
        ),
        out_shape=jax.ShapeDtypeStruct((n, d), F32),
        compiler_params=kernel_params(58),
        cost_estimate=cost(8000),
        name="input_grad",
    )(place, dh1, weight, weight, near, far, *grads)


def flip(v, axis, mask=1):
    size = lax.axis_size(axis)
    return lax.ppermute(v, axis, [(i, i ^ mask) for i in range(size)])


def add_low(*parts):
    return functools.reduce(lambda a, b: a + b, [p.astype(F32) for p in parts]).astype(BF16)


def piece(v, which, rows):
    return lax.dynamic_slice_in_dim(v, which * rows, rows, v.ndim - 2)


def split_rows(v):
    high = v.astype(BF16)
    left = v - high.astype(F32)
    mid = left.astype(BF16)
    low = (left - mid.astype(F32)).astype(BF16)
    return jnp.concatenate([high, mid, low, jnp.zeros_like(high)], axis=0)


def joined_rows(v):
    rows = v.shape[0] // 4
    v = v.astype(F32)
    return v[:rows] + v[rows:2 * rows] + v[2 * rows:3 * rows]


def pull(copies, sems):
    copies = [pltpu.make_async_copy(src, dst, sems.at[k]) for k, (src, dst) in enumerate(copies)]
    for copy in copies:
        copy.start()
    return copies


def prepare_kernel(project_hbm, merge_hbm, pb_ref, eb_ref, out_ref, place_ref, sems, *, packs):
    core, side, outer = lax.axis_index("core"), lax.axis_index("tensor"), lax.axis_index("outer")
    d, mrows = project_hbm.shape[1], merge_hbm.shape[0] // 2
    half = lambda n: pl.ds(pl.multiple_of(core * n, n), n)
    copies = pull(
        [(project_hbm.at[j, :, half(PAIR)], out_ref.at[pl.ds(j * d, d)]) for j in range(3)]
        + [
            (merge_hbm.at[half(mrows), pl.ds(k * PAIR, PAIR)], out_ref.at[pl.ds(3 * d + k * mrows, mrows)])
            for k in range(d // PAIR)
        ],
        sems,
    )
    at = lambda k: slice(k * PAIR, (k + 1) * PAIR)
    rows = [pb_ref[j:j + 1, at(k)] for j in range(2) for k in range(2)]
    rows += [eb_ref[:, at(k)] for k in range(eb_ref.shape[1] // PAIR)]
    fill = jnp.zeros((BIAS_ROWS // 4 - len(rows), PAIR), F32)
    out_ref[4 * d:] = split_rows(jnp.concatenate(rows + [fill], axis=0))
    place_ref[0] = core
    place_ref[1] = side * packs
    place_ref[2] = outer % 2
    for copy in copies:
        copy.wait()


def prepare_rest_kernel(place, expand_hbm, reduce_hbm, out_ref, sems):
    hid, d = expand_hbm.shape[1] // 2, expand_hbm.shape[0]
    half = pl.ds(pl.multiple_of(place[0] * hid, hid), hid)
    pairs = [(expand_hbm.at[:, half], out_ref.at[pl.ds(0, d)]), (reduce_hbm.at[half], out_ref.at[pl.ds(d, hid)])]
    for copy in pull(pairs, sems):
        copy.wait()


def prepare(project, merge, project_bias, expand_bias, packs):
    d, hidden = merge.shape[1], expand_bias.shape[0]
    S = jax.ShapeDtypeStruct
    hbm = pl.BlockSpec(memory_space=pl.ANY)
    return pl.pallas_call(
        functools.partial(prepare_kernel, packs=packs),
        in_specs=[hbm] * 2 + [whole(project_bias.shape), whole((1, hidden))],
        out_specs=[whole((4 * d + BIAS_ROWS, PAIR)), smem()],
        out_shape=[S((4 * d + BIAS_ROWS, PAIR), BF16), S((3,), jnp.int32)],
        scratch_shapes=[pltpu.SemaphoreType.DMA((3 + d // PAIR,))],
        compiler_params=kernel_params(63),
        cost_estimate=cost(3),
        name="prepare",
    )(project, merge, project_bias, expand_bias[None])


def prepare_rest(place, expand, reduce_):
    d, hid = expand.shape[0], expand.shape[1] // 2
    hbm = pl.BlockSpec(memory_space=pl.ANY)
    return pl.pallas_call(
        prepare_rest_kernel,
        in_specs=[smem(), hbm, hbm],
        out_specs=whole((d + hid, d)),
        out_shape=jax.ShapeDtypeStruct((d + hid, d), BF16),
        scratch_shapes=[pltpu.SemaphoreType.DMA((2,))],
        compiler_params=kernel_params(63),
        cost_estimate=cost(3),
        name="prepare_rest",
    )(place, expand, reduce_)


def combine_kernel(place, keep_ref, got_ref, ax_ref, a0_ref, send_ref, keep_out_ref):
    step = pl.program_id(0)
    total = (keep_ref[...].astype(F32) + got_ref[...].astype(F32)).astype(BF16)

    @pl.when(step < 2)
    def _():
        a0_ref[...] = total[0]
        ax_ref[...] = total[1]

    @pl.when(step == 2)
    def _():
        send_ref[...] = total

    @pl.when(step == 3)
    def _():
        keep_out_ref[...] = total


def combine(place, keep, got):
    _, rows, d = keep.shape
    half = rows // 4
    S = jax.ShapeDtypeStruct
    pick = lambda i, place: (0, jnp.where(i < 2, i, jnp.where(i == 2, 3 - place[2], 2 + place[2])), 0)
    first = pl.BlockSpec((half, d), lambda i, *_: (jnp.minimum(i, 1), 0))
    both = pl.BlockSpec((2, half, d), lambda i, *_: (0, 0, 0))
    return pl.pallas_call(
        combine_kernel,
        grid_spec=pltpu.PrefetchScalarGridSpec(
            num_scalar_prefetch=1,
            grid=(4,),
            in_specs=[pl.BlockSpec((2, half, d), pick)] * 2,
            out_specs=[first, first, both, both],
        ),
        out_shape=[S((2 * half, d), BF16)] * 2 + [S((2, half, d), BF16)] * 2,
        compiler_params=kernel_params(20),
        cost_estimate=cost(3),
        name="combine",
    )(place, keep, got)


def halves_kernel(place, *refs):
    parts, (send_ref, keep_ref) = refs[:-2], refs[-2:]
    total = functools.reduce(lambda a, b: a + b, [ref[...].astype(F32) for ref in parts]).astype(BF16)

    @pl.when(pl.program_id(0) == 0)
    def _():
        send_ref[...] = total

    @pl.when(pl.program_id(0) == 1)
    def _():
        keep_ref[...] = total


def halves(place, *parts):
    rows, cols = parts[0].shape[0] // 2, parts[0].shape[1]
    return pl.pallas_call(
        halves_kernel,
        grid_spec=pltpu.PrefetchScalarGridSpec(
            num_scalar_prefetch=1,
            grid=(2,),
            in_specs=[pl.BlockSpec((rows, cols), lambda i, place: (place[2] ^ (1 - i), 0))] * len(parts),
            out_specs=[pl.BlockSpec((rows, cols), lambda i, *_: (0, 0))] * 2,
        ),
        out_shape=[jax.ShapeDtypeStruct((rows, cols), BF16)] * 2,
        compiler_params=kernel_params(20),
        cost_estimate=cost(8000),
        name="halves",
    )(place, *parts)


def unpack_kernel(place, from_ref, part_ref, *refs, small_at):
    if small_at is None:
        reduce_ref, expand_ref, merge_ref, project_ref, bias_ref = refs
    else:
        own_ref, refs = refs[0], refs[6:]
        reduce_ref, expand_ref, merge_ref, project_ref, bias_ref, hidden_ref = refs[:6]
        own, other = own_ref[0:8].astype(F32), from_ref[small_at:small_at + 8].astype(F32)
        low, high = [jnp.where(place[0] == k, own, other) for k in range(2)]
        hidden_ref[...] = jnp.concatenate([low[0:1], high[0:1]], axis=1).reshape(hidden_ref.shape)
        for k, ref in enumerate(refs[6:]):
            half = low if k < 3 else high
            ref[...] = half[k % 3 + 1:k % 3 + 2].reshape(ref.shape)
    hid, d, mrows = reduce_ref.shape[0], expand_ref.shape[0], merge_ref.shape[0]
    reduce_ref[...] = from_ref[0:hid].astype(F32)
    expand_ref[...] = from_ref[hid:hid + d].astype(F32)
    merge_ref[...] = from_ref[hid + d:hid + d + mrows].astype(F32)
    for j in range(3):
        project_ref[j] = part_ref[j * d:(j + 1) * d].astype(F32)
    bias_ref[...] = part_ref[3 * d:3 * d + 8].astype(F32)[0:2]


def unpack(place, own, other, own_part, other_part, hid, mrows):
    d = own.shape[1]
    small_at = hid + d + mrows
    S = jax.ShapeDtypeStruct
    shapes = [S((2 * hid, d), F32), S((d, 2 * hid), F32), S((2 * mrows, d), F32)]
    shapes += [S((3, d, 2 * PAIR), F32), S((2, 2 * PAIR), F32)]

    def call(which, operands, in_specs, out_shape, out_specs, **more):
        rows = lambda r: pl.BlockSpec((r, d), lambda i, place: (place[0] ^ which, 0))
        blocks = [rows(hid), pl.BlockSpec((d, hid), lambda i, place: (0, place[0] ^ which)), rows(mrows)]
        blocks += [
            pl.BlockSpec((3, d, PAIR), lambda i, place: (0, 0, place[0] ^ which)),
            pl.BlockSpec((2, PAIR), lambda i, place: (0, place[0] ^ which)),
        ]
        return pl.pallas_call(
            functools.partial(unpack_kernel, small_at=small_at if which else None),
            grid_spec=pltpu.PrefetchScalarGridSpec(
                num_scalar_prefetch=1, grid=(1,), in_specs=in_specs, out_specs=blocks + out_specs,
            ),
            out_shape=out_shape,
            compiler_params=kernel_params(24),
            cost_estimate=cost(3),
            name="unpack%d" % which,
            **more,
        )(place, *operands)

    held = call(0, [own, own_part], [whole(own.shape), whole(own_part.shape)], shapes, [])
    one = lambda size: pl.BlockSpec((size,), lambda *_: (0,))
    hbm = pl.BlockSpec(memory_space=pl.ANY)
    return call(
        1,
        [other, other_part, own] + list(held),
        [whole(other.shape), whole(other_part.shape)]
        + [pl.BlockSpec((SMALL, d), lambda *_: (small_at // SMALL, 0))]
        + [hbm] * 5,
        shapes + [S((2 * hid,), F32)] + [S((d,), F32)] * 6,
        [one(2 * hid)] + [one(d)] * 6,
        input_output_aliases={4: 0, 5: 1, 6: 2, 7: 3, 8: 4},
    )


def by_bits(bits, pieces):
    v = jnp.stack(pieces)
    v = jnp.where(bits % 2 == 0, v, jnp.stack([v[1], v[0], v[3], v[2]]))
    v = jnp.where(bits // 2 == 0, v, jnp.stack([v[2], v[3], v[0], v[1]]))
    return v.reshape((-1,) + v.shape[2:])


def row_layer(
    inputs,
    pack_long,
    item_table,
    tau_table,
    delta_table,
    project_weight,
    project_bias,
    merge_weight,
    merge_bias,
    first_gain,
    first_shift,
    expand_weight,
    expand_bias,
    reduce_weight,
    reduce_bias,
    second_gain,
    second_shift,
    grad_output,
):
    n, d = inputs.shape
    hid = expand_weight.shape[1] // 2
    mrows = merge_weight.shape[0] // 2
    outer = lax.axis_size("outer")
    y_bit, z_bit = lax.axis_index("outer") % 2, lax.axis_index("outer") // 2 % 2
    project_half, place = prepare(project_weight, merge_weight, project_bias, expand_bias, n // LONG)
    project_near = flip(project_half, "tensor")
    rest_half = prepare_rest(place, expand_weight, reduce_weight)
    rest_near = flip(rest_half, "tensor")

    table = (place, pack_long, item_table, tau_table)
    q0, k0, v0, o0, r0, p0 = attend(
        *table, delta_table, inputs, project_weight, project_weight, project_bias, True
    )
    project_near, o0 = lax.optimization_barrier((project_near, o0))
    project_far = flip(project_near, "core")
    q1, k1, v1, o1, r1, p1, xh, rs = attend(
        *table, delta_table, inputs, project_near, project_far, project_near, False,
        o0, merge_weight, merge_bias[None],
    )
    rest_near, o1 = lax.optimization_barrier((rest_near, o1))
    rest_far = flip(rest_near, "core")
    block_output, grad_att, act, du, n1, dh2, dh1b, sums, sbe, send = feed(
        place, o0, o1, xh, rs, grad_output, merge_weight, project_near, project_far, expand_weight, reduce_weight,
        rest_near, rest_far, expand_bias[None], project_near,
        [v[None] for v in (first_gain, first_shift, reduce_bias, second_gain, second_shift)],
    )
    saved = ((q0, k0, v0, grad_att, o0, r0, p0), (q1, k1, v1, grad_att, o1, r1, p1))
    back = lambda x, *quarters: attend_back(*table, saved, x, quarters)

    got = flip(send, "core")
    keep = feed_grad(place, act, du, n1, dh2, dh1b, o0, o1, sums, sbe)
    got, keep = lax.optimization_barrier((got, keep))
    half = keep.shape[1] // 4
    a_x, a, b_y, b = combine(place, keep, got)
    x, a_x, b_y = lax.optimization_barrier((inputs, a_x, b_y))
    a_x, b_y = flip(a_x, "tensor"), flip(b_y, "outer", 1)
    d01, g01, d11, g11 = back(x, (0, 1), (1, 1))
    got01, got11 = flip(g01, "core"), flip(g11, "core")
    a_x, b_y, d11 = lax.optimization_barrier((a_x, b_y, d11))
    a, b = add_low(a, a_x), add_low(b, b_y)
    a_y, b_x = piece(a, 1 - y_bit, half), b[1]
    x, a_y, b_x = lax.optimization_barrier((x, a_y, b_x))
    a_y, b_x = flip(a_y, "outer", 1), flip(b_x, "tensor")
    d10, g10 = back(x, (1, 0))
    a_y, b_x, d10 = lax.optimization_barrier((a_y, b_x, d10))
    far = add_low(g10, got11)
    total = jnp.concatenate([add_low(piece(a, y_bit, half), a_y), add_low(b[0], b_x)])
    to_z = piece(total, 1 - z_bit, half)
    x, far, to_z = lax.optimization_barrier((x, far, to_z))
    far, to_z = flip(far, "tensor"), flip(to_z, "outer", 2)
    d00, g00 = back(x, (0, 0))
    far, to_z, d00 = lax.optimization_barrier((far, to_z, d00))
    feed_part = add_low(piece(total, z_bit, half), to_z)
    feed_part, g00 = lax.optimization_barrier((feed_part, g00))

    to_y, mine = halves(place, g00, got01, far)
    rows = mine.shape[0] // 2
    to_y = flip(to_y, "outer", 1)
    came = flip(feed_part, "outer", 4)
    dx = functools.partial(input_grad, place, dh1b, project_weight, project_near, project_far)
    mine = add_low(mine, to_y)
    to_z = piece(mine, 1 - z_bit, rows)
    d00, to_z, mine = lax.optimization_barrier((d00, to_z, mine))
    to_z = flip(to_z, "outer", 2)
    dx0 = dx((d00, d01, d10, d11))
    to_z, came, dx0 = lax.optimization_barrier((to_z, came, dx0))
    project_part = add_low(piece(mine, z_bit, rows), to_z)
    feed_part = add_low(feed_part, came)
    project_part, feed_part, d00 = lax.optimization_barrier((project_part, feed_part, d00))
    came = flip(project_part, "outer", 4) if outer > 4 else jnp.zeros_like(project_part)
    by_y, by_z = flip(feed_part, "outer", 1), flip(feed_part, "outer", 2)
    came, by_y, by_z = lax.optimization_barrier((came, by_y, by_z))
    mid = feed_part.shape[0] // 2
    cross = flip(by_z[:mid], "outer", 1), flip(by_y[mid:], "outer", 2)
    project_part = add_low(project_part, came)
    others = [flip(project_part, "outer", mask) for mask in (2, 1, 3)]
    cross, others = lax.optimization_barrier((cross, others))
    feed_pieces = [feed_part, by_y, by_z, jnp.concatenate(cross)]
    project_pieces = [project_part] + others
    total = by_bits(z_bit * 2 + y_bit, feed_pieces)
    project_total = by_bits(y_bit * 2 + z_bit, project_pieces)
    reduce_grad, expand_grad, merge_grad, project_grad, bias_grad, hidden, *small = unpack(
        place, total, flip(total, "core"), project_total, flip(project_total, "core"), hid, mrows
    )
    return (
        block_output,
        dx0,
        project_grad,
        bias_grad,
        merge_grad,
        *small[:3],
        expand_grad,
        hidden,
        reduce_grad,
        *small[3:],
    )


def rows_fit(mesh):
    size = mesh.shape["dp"]
    return mesh.shape["tensor"] == 2 and size in (8, 16)


def solution(mesh):
    if rows_fit(mesh):
        mesh = Mesh(mesh.devices.reshape(-1, 2, 2), ("outer", "core", "tensor"))
        body, dp = row_layer, ("outer", "core")
    else:
        body, dp = split_layer, ("dp",)
    all_ = P(dp + ("tensor",), None)
    placed = (
        all_,
        P(dp),
        P(dp),
        P(),
        P(),
        P(None, None, "tensor"),
        P(None, "tensor"),
        P("tensor", None),
        P(),
        P(),
        P(),
        P(None, "tensor"),
        P("tensor"),
        P("tensor", None),
        P(),
        P(),
        P(),
        all_,
    )
    return jax.shard_map(
        body,
        mesh=mesh,
        in_specs=placed,
        out_specs=(
            all_,
            all_,
            P(None, None, "tensor"),
            P(None, "tensor"),
            P("tensor", None),
            P(),
            P(),
            P(),
            P(None, "tensor"),
            P("tensor"),
            P("tensor", None),
            P(),
            P(),
            P(),
        ),
        check_vma=False,
    )
```

```python
import functools
import jax
import jax.numpy as jnp
from jax import lax
from jax.experimental import pallas as pl
from jax.experimental.pallas import tpu as pltpu
from jax.sharding import Mesh, PartitionSpec as P

HEAD = 64
SHORT = 96
LONG = 384
TABLE = 64
PAIR = 2 * HEAD
SMALL = 128
SMALL_PAIR = 32
BIAS_ROWS = 64
LOG2E = 1.4426950408889634
F32 = jnp.float32
BF16 = jnp.bfloat16


def layer_norm(values, gain, shift):
    mean = jnp.mean(values, axis=-1, keepdims=True)
    centred = values - mean
    spread = jnp.mean(centred * centred, axis=-1, keepdims=True)
    return centred * lax.rsqrt(spread + 1e-05) * gain + shift


def exact_gelu(values):
    return jax.nn.gelu(values, approximate=False)


def describe(pack_long, item_table, tau_table, delta_table):
    packs = pack_long.shape[0]
    per = LONG // SHORT
    count = packs * LONG
    longer = jnp.broadcast_to(pack_long[:, None] == 1, (packs, LONG)).reshape(count)
    lead_row = jnp.broadcast_to(item_table.reshape(packs, per)[:, :1], (packs, LONG)).reshape(count)
    each_row = jnp.broadcast_to(item_table[:, None], (packs * per, SHORT)).reshape(count)
    table_row = jnp.where(longer, lead_row, each_row)
    places = jnp.arange(count, dtype=jnp.int32)
    position = jnp.where(longer, places % LONG, places % SHORT)
    segment = jnp.where(longer, places // LONG * per, places // SHORT)
    picker = (table_row[:, None] == jnp.arange(TABLE, dtype=jnp.int32)[None, :]).astype(jnp.float32)
    tau_row = jnp.sum(picker * tau_table[None, :], axis=1)
    picked = jnp.dot(
        picker, delta_table, precision=lax.Precision.HIGHEST, preferred_element_type=jnp.float32
    )
    placed = position[:, None] == jnp.arange(LONG, dtype=jnp.int32)[None, :]
    delta_row = jnp.sum(jnp.where(placed, picked, 0.0), axis=1)
    return (tau_row, delta_row, segment)


def project(rows_all, project_weight, project_bias):
    query = (
        jnp.dot(rows_all, project_weight[0], preferred_element_type=jnp.float32) + project_bias[0]
    ).astype(jnp.bfloat16)
    keys = jnp.dot(rows_all, project_weight[1], preferred_element_type=jnp.float32).astype(
        jnp.bfloat16
    )
    values = (
        jnp.dot(rows_all, project_weight[2], preferred_element_type=jnp.float32) + project_bias[1]
    ).astype(jnp.bfloat16)
    return (query, keys, values)


def split_blocks(arrays):
    width = 2 * LONG
    return tuple((a.reshape((a.shape[0] // width, width) + a.shape[1:]) for a in arrays))


def block_scores(block_q, block_k, block_tau, block_delta, block_seg):
    raw = jnp.einsum("qhd,khd->hqk", block_q, block_k, preferred_element_type=jnp.float32)
    scores = (block_tau[None, :, None] * raw + block_delta[None, None, :]) * HEAD ** (-0.5)
    same = block_seg[:, None] == block_seg[None, :]
    return jnp.where(same[None], scores, -1e30)


def attend_forward(query, keys, values, tau_row, delta_row, segment):
    heads = query.shape[1] // HEAD
    shaped = tuple((a.reshape(a.shape[0], heads, HEAD) for a in (query, keys, values)))

    def one_block(parts):
        block_q, block_k, block_v, block_tau, block_delta, block_seg = parts
        scores = block_scores(block_q, block_k, block_tau, block_delta, block_seg)
        top = jnp.max(scores, axis=-1, keepdims=True)
        expo = jnp.exp(scores - top)
        totals = jnp.sum(expo, axis=-1, keepdims=True)
        weights = (expo / totals).astype(jnp.bfloat16)
        mixed = jnp.einsum("hqk,khd->qhd", weights, block_v, preferred_element_type=jnp.float32)
        return (
            mixed.reshape(mixed.shape[0], heads * HEAD).astype(jnp.bfloat16),
            top + jnp.log(totals),
        )

    attended, logsum = lax.map(one_block, split_blocks(shaped + (tau_row, delta_row, segment)))
    return (attended.reshape(query.shape), logsum)


def attend_backward(query, keys, values, grad_att, logsum, tau_row, delta_row, segment):
    heads = query.shape[1] // HEAD
    shaped = tuple((a.reshape(a.shape[0], heads, HEAD) for a in (query, keys, values, grad_att)))
    blocked = split_blocks(shaped + (tau_row, delta_row, segment))

    def one_block(parts):
        block_q, block_k, block_v, block_g, block_lse, block_tau, block_delta, block_seg = parts
        scores = block_scores(block_q, block_k, block_tau, block_delta, block_seg)
        probs = jnp.exp(scores - block_lse)
        dprob = jnp.einsum("qhd,khd->hqk", block_g, block_v, preferred_element_type=jnp.float32)
        dscore = probs * (dprob - jnp.sum(dprob * probs, axis=-1, keepdims=True))
        lowered = (dscore * HEAD ** (-0.5) * block_tau[None, :, None]).astype(jnp.bfloat16)
        grad_q = jnp.einsum("hqk,khd->qhd", lowered, block_k, preferred_element_type=jnp.float32)
        grad_k = jnp.einsum("hqk,qhd->khd", lowered, block_q, preferred_element_type=jnp.float32)
        grad_v = jnp.einsum(
            "hqk,qhd->khd", probs.astype(jnp.bfloat16), block_g, preferred_element_type=jnp.float32
        )
        width = block_q.shape[0]
        return tuple(
            (g.reshape(width, heads * HEAD).astype(jnp.bfloat16) for g in (grad_q, grad_k, grad_v))
        )

    grads = lax.map(one_block, blocked[:4] + (logsum,) + blocked[4:])
    return tuple((g.reshape(query.shape) for g in grads))


def row_term(left, right, form):
    return jnp.einsum(form, left, right, preferred_element_type=jnp.float32)


def feed_backward(feed_rows, preact_rows, active_rows, grad_fed, reduce_matrix):
    grad_reduce_weight = jnp.einsum(
        "tf,td->fd", active_rows, grad_fed, preferred_element_type=jnp.float32
    )
    grad_active = jnp.einsum(
        "td,fd->tf", grad_fed, reduce_matrix, preferred_element_type=jnp.float32
    )
    grad_preact = jax.vjp(exact_gelu, preact_rows)[1](grad_active)[0].astype(jnp.bfloat16)
    grad_expand_bias = jnp.sum(grad_preact.astype(jnp.float32), axis=0)
    grad_expand_weight = jnp.einsum(
        "td,tf->df", feed_rows, grad_preact, preferred_element_type=jnp.float32
    )
    return (grad_reduce_weight, grad_preact, grad_expand_bias, grad_expand_weight)


def split_layer(
    inputs,
    pack_long,
    item_table,
    tau_table,
    delta_table,
    project_weight,
    project_bias,
    merge_weight,
    merge_bias,
    first_gain,
    first_shift,
    expand_weight,
    expand_bias,
    reduce_weight,
    reduce_bias,
    second_gain,
    second_shift,
    grad_output,
):
    tau_row, delta_row, segment = describe(pack_long, item_table, tau_table, delta_table)
    rows_all = lax.all_gather(inputs, "tensor", axis=0, tiled=True)
    query, keys, values = project(rows_all, project_weight, project_bias)
    attended, logsum = attend_forward(query, keys, values, tau_row, delta_row, segment)
    mixed_part = lax.psum_scatter(
        row_term(attended, merge_weight, "tc,cd->td"), "tensor", scatter_dimension=0, tiled=True
    )
    first_sum = inputs.astype(jnp.float32) + (mixed_part + merge_bias)
    normed, first_back = jax.vjp(layer_norm, first_sum, first_gain, first_shift)
    normed_low = normed.astype(jnp.bfloat16)
    feed_all = lax.all_gather(normed_low, "tensor", axis=0, tiled=True)
    preact = jnp.dot(feed_all, expand_weight, preferred_element_type=jnp.float32) + expand_bias
    active = exact_gelu(preact).astype(jnp.bfloat16)
    fed_part = lax.psum_scatter(
        row_term(active, reduce_weight, "tf,fd->td"), "tensor", scatter_dimension=0, tiled=True
    )
    second_sum = normed + (fed_part + reduce_bias)
    block_output, second_back = jax.vjp(layer_norm, second_sum, second_gain, second_shift)
    grad_second, grad_gain_b, grad_shift_b = second_back(grad_output.astype(jnp.float32))
    grad_reduce_bias = jnp.sum(grad_second, axis=0)
    grad_fed = lax.all_gather(grad_second.astype(jnp.bfloat16), "tensor", axis=0, tiled=True)
    feed_again = lax.all_gather(normed_low, "tensor", axis=0, tiled=True)
    preact_again = (
        jnp.dot(feed_again, expand_weight, preferred_element_type=jnp.float32) + expand_bias
    )
    active_again = exact_gelu(preact_again).astype(jnp.bfloat16)
    grad_reduce_weight, grad_preact, grad_expand_bias, grad_expand_weight = feed_backward(
        feed_again, preact_again, active_again, grad_fed, reduce_weight
    )
    grad_normed = grad_second + lax.psum_scatter(
        row_term(grad_preact, expand_weight, "tf,df->td"), "tensor", scatter_dimension=0, tiled=True
    )
    grad_first, grad_gain_a, grad_shift_a = first_back(grad_normed)
    grad_merge_bias = jnp.sum(grad_first, axis=0)
    grad_att = lax.all_gather(grad_first.astype(jnp.bfloat16), "tensor", axis=0, tiled=True)
    grad_merge_weight = jnp.einsum(
        "tc,td->cd", attended, grad_att, preferred_element_type=jnp.float32
    )
    grad_attended = jnp.einsum(
        "td,cd->tc", grad_att, merge_weight, preferred_element_type=jnp.float32
    ).astype(jnp.bfloat16)
    rows_again = lax.all_gather(inputs, "tensor", axis=0, tiled=True)
    query_again, keys_again, values_again = project(rows_again, project_weight, project_bias)
    grad_q, grad_k, grad_v = attend_backward(
        query_again, keys_again, values_again, grad_attended, logsum, tau_row, delta_row, segment
    )
    grad_stack = jnp.stack((grad_q, grad_k, grad_v), axis=1)
    grad_project_weight = jnp.einsum(
        "td,tjc->jdc", rows_again, grad_stack, preferred_element_type=jnp.float32
    )
    grad_project_bias = jnp.stack(
        (jnp.sum(grad_q.astype(jnp.float32), axis=0), jnp.sum(grad_v.astype(jnp.float32), axis=0))
    )
    input_grad = grad_first + lax.psum_scatter(
        row_term(grad_stack, project_weight, "tjc,jdc->td").astype(jnp.bfloat16),
        "tensor",
        scatter_dimension=0,
        tiled=True,
    ).astype(jnp.float32)
    summed_all = (
        lax.psum(grad_project_weight.astype(jnp.bfloat16), "dp").astype(jnp.float32),
        lax.psum(grad_project_bias.astype(jnp.bfloat16), "dp").astype(jnp.float32),
        lax.psum(grad_merge_weight.astype(jnp.bfloat16), "dp").astype(jnp.float32),
        lax.psum(grad_expand_weight.astype(jnp.bfloat16), "dp").astype(jnp.float32),
        lax.psum(grad_expand_bias.astype(jnp.bfloat16), "dp").astype(jnp.float32),
        lax.psum(grad_reduce_weight.astype(jnp.bfloat16), "dp").astype(jnp.float32),
    )
    summed_attention = summed_all[:3]
    summed_feed = summed_all[3:]
    small = lax.psum(
        (grad_merge_bias, grad_gain_a, grad_shift_a, grad_reduce_bias, grad_gain_b, grad_shift_b),
        ("dp", "tensor"),
    )
    return (
        block_output,
        input_grad,
        summed_attention[0],
        summed_attention[1],
        summed_attention[2],
        small[0],
        small[1],
        small[2],
        summed_feed[0],
        summed_feed[1],
        summed_feed[2],
        small[3],
        small[4],
        small[5],
    )


def mm(a, b):
    return lax.dot_general(a, b, (((1,), (0,)), ((), ())), preferred_element_type=F32)


def mm_nt(a, b):
    return lax.dot_general(a, b, (((1,), (1,)), ((), ())), preferred_element_type=F32)


def mm_tn(a, b):
    return lax.dot_general(a, b, (((0,), (0,)), ((), ())), preferred_element_type=F32)


def col_sum(v):
    return jnp.sum(v, axis=0, keepdims=True)


def row_mean(v):
    return jnp.mean(v, axis=1, keepdims=True)


def pack_rows(pack, long_ref, item_ref):
    per = LONG // SHORT
    longer = long_ref[pack] == 1
    rows = [jnp.where(longer, item_ref[pack * per], item_ref[pack * per + k]) for k in range(per)]
    return longer, rows


def pack_tau(rows, tau_ref):
    slot = lax.broadcasted_iota(jnp.int32, (LONG, 1), 0) // SHORT
    tau = jnp.full((LONG, 1), tau_ref[rows[0]], F32)
    for k in range(1, LONG // SHORT):
        tau = jnp.where(slot == k, tau_ref[rows[k]], tau)
    return tau


def pack_bias(longer, rows, delta_ref):
    slot_r = lax.broadcasted_iota(jnp.int32, (LONG, 1), 0) // SHORT
    slot_c = lax.broadcasted_iota(jnp.int32, (1, LONG), 1) // SHORT
    shift = delta_ref[pl.ds(rows[0], 1), :]
    for k in range(1, LONG // SHORT):
        piece = jnp.broadcast_to(delta_ref[pl.ds(rows[k], 1), :], (8, LONG))
        piece = pltpu.roll(piece, SHORT * k, 1)[0:1]
        shift = jnp.where(jnp.logical_and(jnp.logical_not(longer), slot_c == k), piece, shift)
    mask = jnp.logical_or(longer, slot_r == slot_c)
    return jnp.where(mask, shift * (HEAD**-0.5 * LOG2E), -1e30)


def forward_kernel(
    place, long_ref, item_ref, tau_ref, delta_ref, x_ref, wa_ref, wb_ref, ba_ref, bb_ref, *refs, own,
):
    step = pl.program_id(0)
    if own:
        q_ref, k_ref, v_ref, o_ref, r_ref, p_ref, w_ref, bias_ref = refs
    else:
        o0_ref, mk_ref, ms_ref, bm_ref = refs[:4]
        q_ref, k_ref, v_ref, o_ref, r_ref, p_ref, xh_ref, rs_ref, w_ref, bias_ref, wm_ref = refs[4:]

    @pl.when(step == 0)
    def _():
        if not own:
            merge_rows(wm_ref, mk_ref, ms_ref, wa_ref.at[3 * x_ref.shape[1]:], wb_ref.at[3 * x_ref.shape[1]:])
        for k, ref in enumerate((wa_ref, wb_ref)):
            for j in range(3):
                w_ref[j, :, k * PAIR:(k + 1) * PAIR] = projection(ref, j, x_ref.shape[1])

    longer, rows = pack_rows(step + place[1], long_ref, item_ref)
    bias_ref[...] = pack_bias(longer, rows, delta_ref)
    tau = pack_tau(rows, tau_ref) * (HEAD**-0.5 * LOG2E)
    x = x_ref[...]
    if own:
        q_bias, v_bias = [jnp.concatenate([ba_ref[j:j + 1], bb_ref[j:j + 1]], axis=1) for j in range(2)]
    else:
        b = joined_rows(ba_ref[...])
        q_bias, v_bias = [
            jnp.where(
                place[0] == 0,
                jnp.concatenate([b[k:k + 1], b[k + 1:k + 2]], axis=1),
                jnp.concatenate([b[k + 1:k + 2], b[k:k + 1]], axis=1),
            )
            for k in (0, 2)
        ]
    q = (mm(x, w_ref[0]) + q_bias).astype(BF16)
    k = mm(x, w_ref[1]).astype(BF16)
    v = (mm(x, w_ref[2]) + v_bias).astype(BF16)
    q_ref[...] = q
    k_ref[...] = k
    v_ref[...] = v
    scaled = (q.astype(F32) * tau).astype(BF16)
    vf = v.astype(F32)
    first = lax.broadcasted_iota(jnp.int32, (1, PAIR), 1) < HEAD
    heads = q.shape[1] // HEAD

    def score(h):
        at = slice(h * HEAD, (h + 1) * HEAD)
        return mm_nt(scaled[:, at], k[:, at])

    def soften(s):
        s = s + bias_ref[...]
        return jnp.exp2(s - jnp.max(s, axis=1, keepdims=True)).astype(BF16)

    mixed = []

    def mix(h, w):
        p_ref[0, h] = w
        at = slice(h // 2 * PAIR, (h // 2 + 1) * PAIR)
        own = first if h % 2 == 0 else jnp.logical_not(first)
        mixed.append(mm(w, jnp.where(own, vf[:, at], 1.0).astype(BF16)))
        if h % 2 == 1:
            a, b = mixed[-2:]
            r = 1.0 / pltpu.roll(jnp.where(first, b, a), HEAD, 1)
            r_ref[:, at] = r.astype(BF16)
            o_ref[:, at] = (jnp.where(first, a, b) * r).astype(BF16)

    s = score(0)
    held = None
    for h in range(heads):
        later = score(h + 1) if h + 1 < heads else None
        w = soften(s)
        if held is not None:
            mix(h - 1, held)
        held, s = w, later
    mix(heads - 1, held)
    if not own:
        half = wm_ref.shape[0] // 2
        mixed = mm(o0_ref[...], wm_ref[:half]) + mm(o_ref[...], wm_ref[half:])
        h1 = x.astype(F32) + (mixed + bm_ref[...])
        c = h1 - row_mean(h1)
        rs = lax.rsqrt(row_mean(c * c) + 1e-05)
        xh_ref[...] = c * rs
        rs_ref[...] = jnp.broadcast_to(rs, rs_ref.shape)


def merge_rows(out_ref, keep_ref, other_ref, near_ref, far_ref):
    rows = keep_ref.shape[0]
    out_ref[0:rows] = keep_ref[...]
    out_ref[rows:2 * rows] = other_ref[...]
    for m, ref in ((2, near_ref), (3, far_ref)):
        for k in range(out_ref.shape[1] // PAIR):
            out_ref[m * rows:(m + 1) * rows, k * PAIR:(k + 1) * PAIR] = ref[k * rows:(k + 1) * rows]


def whole(shape):
    return pl.BlockSpec(shape, lambda *_: (0,) * len(shape), pipeline_mode=pl.Buffered(1))


def smem():
    return pl.BlockSpec(memory_space=pltpu.SMEM)


def kernel_params(mib):
    return pltpu.CompilerParams(vmem_limit_bytes=mib * 2**20)


def cost(us):
    return pl.CostEstimate(flops=int(us * 1.0e6), bytes_accessed=0, transcendentals=0)


def projection(ref, j, d):
    return ref[j] if len(ref.shape) == 3 else ref[j * d:(j + 1) * d]


def bias_block(d):
    return pl.BlockSpec((BIAS_ROWS, PAIR), lambda *_: (4 * d // BIAS_ROWS, 0), pipeline_mode=pl.Buffered(1))


def attend(place, long_, item, tau, delta, x, wa, wb, bias, own, o0=None, merge=None, merge_bias=None):
    n, d = x.shape
    packs = n // LONG
    cols = 2 * PAIR
    row = lambda c: pl.BlockSpec((LONG, c), lambda i, *_: (i, 0))
    if own:
        weights = [
            pl.BlockSpec((3, d, PAIR), lambda i, place, *_, h=h: (0, 0, place[0] ^ h), pipeline_mode=pl.Buffered(1))
            for h in (0, 1)
        ]
        biases = [pl.BlockSpec((2, PAIR), lambda i, place, *_, h=h: (0, place[0] ^ h)) for h in (0, 1)]
    else:
        weights, biases = [whole(wa.shape), whole(wb.shape)], [bias_block(d)] * 2
    out = jax.ShapeDtypeStruct((n, cols), BF16)
    heads = cols // HEAD
    more_in, more_out, more_shapes, more_scratch, more = [], [], [], [], []
    if not own:
        mrows = merge.shape[0] // 2
        more_in = [row(cols)]
        more_in += [
            pl.BlockSpec((mrows, d), lambda i, place, *_, h=h: (place[0] ^ h, 0), pipeline_mode=pl.Buffered(1))
            for h in (0, 1)
        ]
        more_in += [whole((1, d))]
        more_out = [row(d), row(PAIR)]
        more_shapes = [jax.ShapeDtypeStruct((n, d), F32), jax.ShapeDtypeStruct((n, PAIR), F32)]
        more_scratch = [pltpu.VMEM((4 * mrows, d), BF16)]
        more = [o0, merge, merge, merge_bias]
    return pl.pallas_call(
        functools.partial(forward_kernel, own=own),
        grid_spec=pltpu.PrefetchScalarGridSpec(
            num_scalar_prefetch=3,
            grid=(packs,),
            in_specs=[smem(), whole(delta.shape), row(d)]
            + weights
            + biases
            + more_in,
            out_specs=[row(cols)] * 5
            + [pl.BlockSpec((1, heads, LONG, LONG), lambda i, *_: (i, 0, 0, 0))]
            + more_out,
            scratch_shapes=[pltpu.VMEM((3, d, cols), BF16), pltpu.VMEM((LONG, LONG), F32)] + more_scratch,
        ),
        out_shape=[out] * 4
        + [
            jax.ShapeDtypeStruct((n, cols), BF16),
            jax.ShapeDtypeStruct((packs, heads, LONG, LONG), BF16),
        ]
        + more_shapes,
        compiler_params=kernel_params(63),
        cost_estimate=cost(1 if own else 4000),
        name="attend_own" if own else "attend_other",
    )(place, long_, item, tau, delta, x, wa, wb, bias, bias, *more)


def gelu_parts(u):
    phi = 0.5 + 0.5 * lax.erf(u * 0.7071067811865476)
    return phi, jnp.exp2(u * u * (-0.5 * LOG2E))


def feed_kernel(
    place, o0_ref, o1_ref, xh_ref, rs1_ref, gy_ref, mk_ref, ms_ref, mnear_ref, mfar_ref,
    ek_ref, es_ref, rk_ref, rs_ref,
    near_ref, far_ref, b0_ref, b1_ref, b2_ref, g1_ref, h1_ref, br_ref, g2_ref, h2_ref,
    out_ref, do_ref, act_ref, du_ref, n1_ref, dh2_ref, dh1b_ref, sum_ref, sbe_ref, send_ref,
    wm_ref, act_all, du_all, gp_ref, n1_all, dh2_all, dh1b_all, o_all, *, tiles, tile,
):
    step = pl.program_id(0)
    d = xh_ref.shape[1]
    hid = ek_ref.shape[1]
    mrows = mk_ref.shape[0]
    expand = (ek_ref, es_ref, near_ref.at[0:d], far_ref.at[0:d])
    reduce_ = (rk_ref, rs_ref, near_ref.at[d:d + hid], far_ref.at[d:d + hid])

    @pl.when(step == 0)
    def _():
        merge_rows(wm_ref, mk_ref, ms_ref, mnear_ref, mfar_ref)

    @pl.when(step < tiles)
    def _():
        here = pl.ds(pl.multiple_of(step * tile, tile), tile)
        g1, b1, br, g2, b2 = [ref[...] for ref in (g1_ref, h1_ref, br_ref, g2_ref, h2_ref)]
        b = joined_rows(b2_ref[...])
        wide = hid // PAIR
        parts = [
            jnp.concatenate([b[4 + wide * k + m:5 + wide * k + m] for m in range(wide)], axis=1) for k in range(2)
        ]
        first = place[0] == 0
        be = [b0_ref[...], b1_ref[...], jnp.where(first, *parts), jnp.where(first, *parts[::-1])]
        o_all[here, :mrows] = o0_ref[...]
        o_all[here, mrows:] = o1_ref[...]
        xh, rs = xh_ref[...], rs1_ref[:, 0:1]
        n1 = xh * g1 + b1
        low = n1.astype(BF16)
        n1_ref[...] = low
        n1_all[here] = low
        u = mm(low, expand[0][...])
        fed = n1 + br
        for k in range(4):
            later = mm(low, expand[k + 1][...]) if k < 3 else None
            at = slice(k * hid, (k + 1) * hid)
            u = u + be[k]
            phi, e = gelu_parts(u)
            act = (u * phi).astype(BF16)
            mine = slice(k // 2 * hid, (k // 2 + 1) * hid)
            if k % 2 == 0:
                act_ref[:, mine] = act
            else:
                act_all[here, mine] = act
            gp_ref[:, at] = (phi + u * (e * 0.3989422804014327)).astype(BF16)
            fed = fed + mm(act, reduce_[k][...])
            u = later
        c2 = fed - row_mean(fed)
        rs2 = lax.rsqrt(row_mean(c2 * c2) + 1e-05)
        xh2 = c2 * rs2
        out_ref[...] = xh2 * g2 + b2
        gy = gy_ref[...].astype(F32)
        gg = gy * g2
        dh2 = rs2 * ((gg - row_mean(gg)) - xh2 * row_mean(gg * xh2))
        dh2b = dh2.astype(BF16)
        dh2_ref[...] = dh2b
        dh2_all[here] = dh2b
        dn = dh2
        sbe = []
        da = mm_nt(dh2b, reduce_[0][...])
        for k in range(4):
            later = mm_nt(dh2b, reduce_[k + 1][...]) if k < 3 else None
            at = slice(k * hid, (k + 1) * hid)
            du = (da * gp_ref[:, at].astype(F32)).astype(BF16)
            mine = slice(k // 2 * hid, (k // 2 + 1) * hid)
            if k % 2 == 0:
                du_ref[:, mine] = du
            else:
                du_all[here, mine] = du
            sbe.append(col_sum(du.astype(F32)))
            dn = dn + mm_nt(du, expand[k][...])
            da = later
        gg1 = dn * g1
        dh1 = rs * ((gg1 - row_mean(gg1)) - xh * row_mean(gg1 * xh))
        dh1b = dh1.astype(BF16)
        dh1b_ref[...] = dh1b
        dh1b_all[here] = dh1b
        do_ref[...] = mm_nt(dh1b, wm_ref[...]).astype(BF16)
        sums = [col_sum(dh1), col_sum(dn * xh), col_sum(dn), col_sum(dh2), col_sum(gy * xh2), col_sum(gy)]
        sums = jnp.concatenate(sums + [jnp.zeros((2, d), F32)], axis=0)
        sbe = jnp.broadcast_to(jnp.concatenate(sbe, axis=1), sbe_ref.shape)

        @pl.when(step == 0)
        def _():
            sum_ref[...] = sums
            sbe_ref[...] = sbe

        @pl.when(step > 0)
        def _():
            sum_ref[...] += sums
            sbe_ref[...] += sbe

    for slot in range(2):

        @pl.when(step == tiles + slot)
        def _(slot=slot):
            at = slice(slot * hid, (slot + 1) * hid)
            om = slice(slot * mrows, (slot + 1) * mrows)
            send_ref[0, 0:hid] = mm_tn(act_all[:, at], dh2_all[...]).astype(BF16)
            send_ref[0, hid:hid + d] = mm_tn(n1_all[...], du_all[:, at]).astype(BF16)
            rows = hid + d + mrows
            send_ref[0, hid + d:rows] = mm_tn(o_all[:, om], dh1b_all[...]).astype(BF16)
            send_ref[0, rows:] = small_rows(place[0] ^ 1, sum_ref[...], sbe_ref[...], slot, 1, hid)


def small_rows(which, sums, sbe, slot, h, hid):
    lo = (2 * slot + h) * hid
    part = jnp.where(which == 0, sums[0:3], sums[3:6])
    fill = jnp.zeros((SMALL - 4, sums.shape[1]), F32)
    return jnp.concatenate([sbe[0:1, lo:lo + hid], part, fill], axis=0).astype(BF16)


def feed(place, o0, o1, xh, rs1, gy, merge, mnear, mfar, expand, reduce_, near, far, be0, be1, vecs):
    n, d = xh.shape
    tile = 2 * LONG
    tiles = n // tile
    mrows, hid = merge.shape[0] // 2, expand.shape[1] // 2
    full_hid = 4 * hid
    at = lambda i: jnp.minimum(i, tiles - 1)
    row = lambda c: pl.BlockSpec((tile, c), lambda i, *_: (at(i), 0))
    once = pl.Buffered(1)
    by_row = lambda shape, h: pl.BlockSpec(shape, lambda i, place: (place[0] ^ h, 0), pipeline_mode=once)
    by_col = lambda shape, h: pl.BlockSpec(shape, lambda i, place: (0, place[0] ^ h), pipeline_mode=once)
    S = jax.ShapeDtypeStruct
    grows = hid + d + mrows + SMALL
    bias = lambda h: pl.BlockSpec((1, hid), lambda i, place: (0, place[0] ^ h), pipeline_mode=once)
    return pl.pallas_call(
        functools.partial(feed_kernel, tiles=tiles, tile=tile),
        grid_spec=pltpu.PrefetchScalarGridSpec(
            num_scalar_prefetch=1,
            grid=(tiles + 2,),
            in_specs=[pl.BlockSpec((tile, mrows), lambda i, *_: (at(i), 1))] * 2
            + [row(d), row(rs1.shape[1]), row(d)]
            + [by_row((mrows, d), h) for h in (0, 1)]
            + [pl.BlockSpec((d, PAIR), lambda *_: (3, 0), pipeline_mode=once)] * 2
            + [by_col((d, hid), h) for h in (0, 1)]
            + [by_row((hid, d), h) for h in (0, 1)]
            + [whole(near.shape), whole(far.shape)]
            + [bias(0), bias(1), bias_block(d)]
            + [whole((1, d))] * 5,
            out_specs=[row(d), row(d), row(2 * hid), row(2 * hid), row(d), row(d), row(d)]
            + [
                pl.BlockSpec((8, d), lambda i, *_: (0, 0)),
                pl.BlockSpec((8, full_hid), lambda i, *_: (0, 0)),
                pl.BlockSpec((1, grows, d), lambda i, *_: (jnp.maximum(i - tiles, 0), 0, 0)),
            ],
            scratch_shapes=[
                pltpu.VMEM((4 * mrows, d), BF16),
                pltpu.VMEM((n, 2 * hid), BF16),
                pltpu.VMEM((n, 2 * hid), BF16),
                pltpu.VMEM((tile, full_hid), BF16),
                pltpu.VMEM((n, d), BF16),
                pltpu.VMEM((n, d), BF16),
                pltpu.VMEM((n, d), BF16),
                pltpu.VMEM((n, 2 * mrows), BF16),
            ],
        ),
        out_shape=[S((n, d), F32), S((n, d), BF16)]
        + [S((n, 2 * hid), BF16)] * 2
        + [S((n, d), BF16)] * 3
        + [S((8, d), F32), S((8, full_hid), F32), S((2, grows, d), BF16)],
        compiler_params=kernel_params(63),
        cost_estimate=cost(60),
        name="feed",
    )(
        place, o0, o1, xh, rs1, gy, merge, merge, mnear, mfar, expand, expand, reduce_, reduce_,
        near, far, be0, be0, be1, *vecs,
    )


def feed_grad_kernel(
    place, act_hbm, du_hbm, n1_hbm, dh2_hbm, dh1b_hbm, o0_hbm, o1_hbm, sum_ref, sbe_ref, keep_hbm,
    act, du, n1, dh2, dh1b, o, keep, sems, out_sems,
):
    hid, d, mrows = act.shape[2], n1.shape[1], o.shape[2]

    def fetch(src, dst, k):
        copy = pltpu.make_async_copy(src, dst, sems.at[k])
        copy.start()
        return copy

    cols = lambda s: (slice(None), pl.ds(s * hid, hid))
    heads = lambda ref: ref.at[:, pl.ds(0, mrows)]
    third = n1.shape[0] // 3
    parts = [pl.ds(k * third, third) for k in range(3)]
    order = tuple(
        pair
        for p in parts
        for pair in ((act_hbm.at[p, pl.ds(hid, hid)], act.at[1, p]), (dh2_hbm.at[p], dh2.at[p]))
    ) + (
        (n1_hbm, n1), (du_hbm.at[cols(1)], du.at[1]),
        (heads(o1_hbm), o.at[1]), (dh1b_hbm, dh1b),
        (act_hbm.at[cols(0)], act.at[0]), (du_hbm.at[cols(0)], du.at[0]), (heads(o0_hbm), o.at[0]),
    )
    copies = [fetch(src, dst, k) for k, (src, dst) in enumerate(order)]
    flush = []
    rows = hid + d + mrows
    for slot, waits in ((1, (0, 6, 8, 10)), (0, (10, 11, 12, 13))):
        if slot == 1:
            total = None
            for k, p in enumerate(parts):
                copies[2 * k].wait()
                copies[2 * k + 1].wait()
                term = mm_tn(act[slot, p], dh2[p])
                total = term if total is None else total + term
        else:
            copies[10].wait()
            total = mm_tn(act[slot], dh2[...])
        keep[slot, 0:hid] = total.astype(BF16)
        for k in range(waits[1], waits[2]):
            copies[k].wait()
        keep[slot, hid:hid + d] = mm_tn(n1[...], du[slot]).astype(BF16)
        for k in range(waits[2], waits[3]):
            copies[k].wait()
        keep[slot, hid + d:rows] = mm_tn(o[slot], dh1b[...]).astype(BF16)
        keep[slot, rows:] = small_rows(place[0], sum_ref[...], sbe_ref[...], slot, 0, hid)
        out = pltpu.make_async_copy(keep.at[slot], keep_hbm.at[slot], out_sems.at[slot])
        out.start()
        flush.append(out)
    for out in flush:
        out.wait()


def feed_grad(place, act, du, n1, dh2, dh1b, o0, o1, sums, sbe):
    n, d = n1.shape
    hid, mrows = act.shape[1] // 2, o0.shape[1] // 2
    grows = hid + d + mrows + SMALL
    hbm = pl.BlockSpec(memory_space=pl.ANY)
    return pl.pallas_call(
        feed_grad_kernel,
        in_specs=[smem()] + [hbm] * 7 + [whole(sums.shape), whole(sbe.shape)],
        out_specs=hbm,
        out_shape=jax.ShapeDtypeStruct((2, grows, d), BF16),
        scratch_shapes=[
            pltpu.VMEM((2, n, hid), BF16),
            pltpu.VMEM((2, n, hid), BF16),
            pltpu.VMEM((n, d), BF16),
            pltpu.VMEM((n, d), BF16),
            pltpu.VMEM((n, d), BF16),
            pltpu.VMEM((2, n, mrows), BF16),
            pltpu.VMEM((2, grows, d), BF16),
            pltpu.SemaphoreType.DMA((13,)),
            pltpu.SemaphoreType.DMA((2,)),
        ],
        compiler_params=kernel_params(58),
        cost_estimate=cost(9),
        name="feed_grad",
    )(place, act, du, n1, dh2, dh1b, o0, o1, sums, sbe)


def backward_kernel(place, long_ref, item_ref, tau_ref, *refs, sets, steps, group):
    step = pl.program_id(0)
    width = group * LONG
    per = [refs[7 * s:7 * s + 7] for s in range(sets)]
    x_hbm = refs[7 * sets]
    outs = refs[7 * sets + 1:7 * sets + 1 + 2 * sets]
    x_all, d_all, sem = refs[-3:]
    fetch = pltpu.make_async_copy(x_hbm, x_all, sem)

    @pl.when(step == 0)
    def _():
        fetch.start()

    lane = lax.broadcasted_iota(jnp.int32, (1, PAIR), 1)
    first = lane < HEAD
    ready = []
    for m in range(group):
        _, rows = pack_rows(step * group + m + place[1], long_ref, item_ref)
        tau = pack_tau(rows, tau_ref) * HEAD**-0.5
        here = slice(m * LONG, (m + 1) * LONG)
        for s in range(sets):
            _, _, v_ref, g_ref, o_ref, r_ref, _ = per[s]
            g = g_ref[here].astype(F32) * r_ref[here].astype(F32)
            low = g.astype(BF16)
            scaled = (g * tau).astype(BF16).astype(F32)
            d = scaled * o_ref[here].astype(F32)
            v = v_ref[here].astype(F32)
            for j in range(2):
                own = first if j == 0 else jnp.logical_not(first)
                spare = HEAD if j == 0 else 0
                dd = jnp.sum(jnp.where(own, d, 0.0), axis=1, keepdims=True)
                high = dd.astype(BF16).astype(F32)
                left = jnp.where(lane == spare, -high, jnp.where(lane == spare + 1, high - dd, 0.0))
                left = jnp.where(own, scaled, left).astype(BF16)
                ones = jnp.where(jnp.logical_or(lane == spare, lane == spare + 1), 1.0, 0.0)
                right = jnp.where(own, v, ones).astype(BF16)
                ready.append((left, right, low[:, j * HEAD:(j + 1) * HEAD], m, s, j))
    res = []
    t = mm_nt(*ready[0][:2])
    for n, (_, _, low, m, s, j) in enumerate(ready):
        later = mm_nt(*ready[n + 1][:2]) if n + 1 < len(ready) else None
        q_ref, k_ref, _, _, _, _, p_ref = per[s]
        here = slice(m * LONG, (m + 1) * LONG)
        at = slice(j * HEAD, (j + 1) * HEAD)
        w = p_ref[m, j]
        r = (w.astype(F32) * t).astype(BF16)
        res.append((mm(r, k_ref[here, at]), mm_tn(q_ref[here, at], r), mm_tn(low, w)))
        t = later
        if j == 1:
            a, b = res[-2:]
            out = [jnp.concatenate([a[0], b[0]], axis=1).astype(BF16)]
            out += [jnp.concatenate([a[k], b[k]], axis=0).astype(BF16).T for k in (1, 2)]
            spot = pl.ds(pl.multiple_of(step * width + m * LONG, LONG), LONG)
            for k in range(3):
                outs[2 * s][here, k * PAIR:(k + 1) * PAIR] = out[k]
                d_all[spot, (3 * s + k) * PAIR:(3 * s + k + 1) * PAIR] = out[k]

    @pl.when(step == steps - 1)
    def _():
        fetch.wait()
        depth = x_all.shape[1]
        res = mm_tn(x_all[...], d_all[...]).astype(BF16)
        for s in range(sets):
            grad_ref = outs[2 * s + 1]
            for k in range(3):
                grad_ref[k * depth:(k + 1) * depth] = res[:, (3 * s + k) * PAIR:(3 * s + k + 1) * PAIR]
            cols = [slice((3 * s + k) * PAIR, (3 * s + k + 1) * PAIR) for k in (0, 2)]
            dq, dv = [col_sum(d_all[:, at].astype(F32)) for at in cols]
            small = jnp.concatenate([dq, dv, jnp.zeros((SMALL_PAIR - 2, PAIR), F32)], axis=0)
            grad_ref[3 * depth:] = small.astype(BF16)


def attend_back(place, long_, item, tau, saved, x, quarters):
    n, d = x.shape
    sets = len(quarters)
    group = 2 // sets
    width = group * LONG
    steps = n // width
    col = lambda c: pl.BlockSpec((width, PAIR), lambda i, *_: (i, c))
    S = jax.ShapeDtypeStruct
    rows = 3 * d + SMALL_PAIR
    specs, operands = [], []
    for slot, h in quarters:
        p = saved[slot][-1]
        specs += [col(h)] * 3 + [col(2 * slot + h)] + [col(h)] * 2
        specs += [pl.BlockSpec((group, 2) + p.shape[2:], lambda i, *_, h=h: (i, h, 0, 0))]
        operands += list(saved[slot])
    return pl.pallas_call(
        functools.partial(backward_kernel, sets=sets, steps=steps, group=group),
        grid_spec=pltpu.PrefetchScalarGridSpec(
            num_scalar_prefetch=3,
            grid=(steps,),
            in_specs=[smem()] + specs + [pl.BlockSpec(memory_space=pl.ANY)],
            out_specs=[
                pl.BlockSpec((width, 3 * PAIR), lambda i, *_: (i, 0)),
                pl.BlockSpec((rows, PAIR), lambda i, *_: (0, 0)),
            ]
            * sets,
            scratch_shapes=[
                pltpu.VMEM((n, d), BF16), pltpu.VMEM((n, sets * 3 * PAIR), BF16), pltpu.SemaphoreType.DMA,
            ],
        ),
        out_shape=[S((n, 3 * PAIR), BF16), S((rows, PAIR), BF16)] * sets,
        compiler_params=kernel_params(58),
        cost_estimate=cost(8),
        name="attend_back_" + "_".join("%d%d" % q for q in quarters),
    )(place, long_, item, tau, *operands, x)


def input_grad_kernel(place, dh1_ref, ka_ref, sa_ref, near_ref, far_ref, *refs):
    d_refs, (out_ref, w_ref) = refs[:4], refs[-2:]

    @pl.when(pl.program_id(0) == 0)
    def _():
        for j in range(3):
            for k, ref in enumerate((ka_ref, sa_ref, near_ref, far_ref)):
                lo = (k * 3 + j) * PAIR
                w_ref[:, lo:lo + PAIR] = projection(ref, j, w_ref.shape[0])

    d = jnp.concatenate([ref[...] for ref in d_refs], axis=1)
    out_ref[...] = dh1_ref[...].astype(F32) + mm_nt(d, w_ref[...])


def input_grad(place, dh1, weight, near, far, grads, part, held=None):
    n, d = dh1.shape
    tile = LONG
    begin, end = [n // tile * k // 3 for k in ((0, 2) if part == 0 else (2, 3))]
    steps = end - begin
    cols = grads[0].shape[1]
    row = lambda c: pl.BlockSpec((tile, c), lambda i, *_: (begin + i, 0))
    pick = lambda h: pl.BlockSpec((3, d, PAIR), lambda i, place: (0, 0, place[0] ^ h), pipeline_mode=pl.Buffered(1))
    extra = [] if held is None else [held]
    return pl.pallas_call(
        input_grad_kernel,
        grid_spec=pltpu.PrefetchScalarGridSpec(
            num_scalar_prefetch=1,
            grid=(steps,),
            in_specs=[row(d), pick(0), pick(1), whole(near.shape), whole(far.shape)]
            + [row(cols)] * 4
            + [pl.BlockSpec(memory_space=pl.ANY)] * len(extra),
            out_specs=row(d),
            scratch_shapes=[pltpu.VMEM((d, 4 * cols), BF16)],
        ),
        out_shape=jax.ShapeDtypeStruct((n, d), F32),
        input_output_aliases={10: 0} if extra else {},
        compiler_params=kernel_params(58),
        cost_estimate=cost(8000),
        name="input_grad%d" % part,
    )(place, dh1, weight, weight, near, far, *grads, *extra)


def flip(v, axis, mask=1):
    size = lax.axis_size(axis)
    return lax.ppermute(v, axis, [(i, i ^ mask) for i in range(size)])


def add_low(*parts):
    return functools.reduce(lambda a, b: a + b, [p.astype(F32) for p in parts]).astype(BF16)


def piece(v, which, rows):
    return lax.dynamic_slice_in_dim(v, which * rows, rows, v.ndim - 2)


def split_rows(v):
    high = v.astype(BF16)
    left = v - high.astype(F32)
    mid = left.astype(BF16)
    low = (left - mid.astype(F32)).astype(BF16)
    return jnp.concatenate([high, mid, low, jnp.zeros_like(high)], axis=0)


def joined_rows(v):
    rows = v.shape[0] // 4
    v = v.astype(F32)
    return v[:rows] + v[rows:2 * rows] + v[2 * rows:3 * rows]


def pull(copies, sems):
    copies = [pltpu.make_async_copy(src, dst, sems.at[k]) for k, (src, dst) in enumerate(copies)]
    for copy in copies:
        copy.start()
    return copies


def prepare_kernel(project_hbm, merge_hbm, pb_ref, eb_ref, out_ref, place_ref, sems, *, packs):
    core, side, outer = lax.axis_index("core"), lax.axis_index("tensor"), lax.axis_index("outer")
    d, mrows = project_hbm.shape[1], merge_hbm.shape[0] // 2
    half = lambda n: pl.ds(pl.multiple_of(core * n, n), n)
    copies = pull(
        [(project_hbm.at[j, :, half(PAIR)], out_ref.at[pl.ds(j * d, d)]) for j in range(3)]
        + [
            (merge_hbm.at[half(mrows), pl.ds(k * PAIR, PAIR)], out_ref.at[pl.ds(3 * d + k * mrows, mrows)])
            for k in range(d // PAIR)
        ],
        sems,
    )
    at = lambda k: slice(k * PAIR, (k + 1) * PAIR)
    rows = [pb_ref[j:j + 1, at(k)] for j in range(2) for k in range(2)]
    rows += [eb_ref[:, at(k)] for k in range(eb_ref.shape[1] // PAIR)]
    fill = jnp.zeros((BIAS_ROWS // 4 - len(rows), PAIR), F32)
    out_ref[4 * d:] = split_rows(jnp.concatenate(rows + [fill], axis=0))
    place_ref[0] = core
    place_ref[1] = side * packs
    place_ref[2] = outer % 2
    for copy in copies:
        copy.wait()


def prepare_rest_kernel(place, expand_hbm, reduce_hbm, out_ref, sems):
    hid, d = expand_hbm.shape[1] // 2, expand_hbm.shape[0]
    half = pl.ds(pl.multiple_of(place[0] * hid, hid), hid)
    pairs = [(expand_hbm.at[:, half], out_ref.at[pl.ds(0, d)]), (reduce_hbm.at[half], out_ref.at[pl.ds(d, hid)])]
    for copy in pull(pairs, sems):
        copy.wait()


def prepare(project, merge, project_bias, expand_bias, packs):
    d, hidden = merge.shape[1], expand_bias.shape[0]
    S = jax.ShapeDtypeStruct
    hbm = pl.BlockSpec(memory_space=pl.ANY)
    return pl.pallas_call(
        functools.partial(prepare_kernel, packs=packs),
        in_specs=[hbm] * 2 + [whole(project_bias.shape), whole((1, hidden))],
        out_specs=[whole((4 * d + BIAS_ROWS, PAIR)), smem()],
        out_shape=[S((4 * d + BIAS_ROWS, PAIR), BF16), S((3,), jnp.int32)],
        scratch_shapes=[pltpu.SemaphoreType.DMA((3 + d // PAIR,))],
        compiler_params=kernel_params(63),
        cost_estimate=cost(3),
        name="prepare",
    )(project, merge, project_bias, expand_bias[None])


def prepare_rest(place, expand, reduce_):
    d, hid = expand.shape[0], expand.shape[1] // 2
    hbm = pl.BlockSpec(memory_space=pl.ANY)
    return pl.pallas_call(
        prepare_rest_kernel,
        in_specs=[smem(), hbm, hbm],
        out_specs=whole((d + hid, d)),
        out_shape=jax.ShapeDtypeStruct((d + hid, d), BF16),
        scratch_shapes=[pltpu.SemaphoreType.DMA((2,))],
        compiler_params=kernel_params(63),
        cost_estimate=cost(3),
        name="prepare_rest",
    )(place, expand, reduce_)


def combine_kernel(place, keep_ref, got_ref, ax_ref, a0_ref, send_ref, keep_out_ref):
    step = pl.program_id(0)
    total = (keep_ref[...].astype(F32) + got_ref[...].astype(F32)).astype(BF16)

    @pl.when(step < 2)
    def _():
        a0_ref[...] = total[0]
        ax_ref[...] = total[1]

    @pl.when(step == 2)
    def _():
        send_ref[...] = total

    @pl.when(step == 3)
    def _():
        keep_out_ref[...] = total


def combine(place, keep, got):
    _, rows, d = keep.shape
    half = rows // 4
    S = jax.ShapeDtypeStruct
    pick = lambda i, place: (0, jnp.where(i < 2, i, jnp.where(i == 2, 3 - place[2], 2 + place[2])), 0)
    first = pl.BlockSpec((half, d), lambda i, *_: (jnp.minimum(i, 1), 0))
    both = pl.BlockSpec((2, half, d), lambda i, *_: (0, 0, 0))
    return pl.pallas_call(
        combine_kernel,
        grid_spec=pltpu.PrefetchScalarGridSpec(
            num_scalar_prefetch=1,
            grid=(4,),
            in_specs=[pl.BlockSpec((2, half, d), pick)] * 2,
            out_specs=[first, first, both, both],
        ),
        out_shape=[S((2 * half, d), BF16)] * 2 + [S((2, half, d), BF16)] * 2,
        compiler_params=kernel_params(20),
        cost_estimate=cost(3),
        name="combine",
    )(place, keep, got)


def unpack_kernel(place, from_ref, part_ref, *refs, small_at):
    if small_at is None:
        reduce_ref, expand_ref, merge_ref, project_ref, bias_ref = refs
    else:
        own_ref, refs = refs[0], refs[6:]
        reduce_ref, expand_ref, merge_ref, project_ref, bias_ref, hidden_ref = refs[:6]
        own, other = own_ref[0:8].astype(F32), from_ref[small_at:small_at + 8].astype(F32)
        low, high = [jnp.where(place[0] == k, own, other) for k in range(2)]
        hidden_ref[...] = jnp.concatenate([low[0:1], high[0:1]], axis=1).reshape(hidden_ref.shape)
        for k, ref in enumerate(refs[6:]):
            half = low if k < 3 else high
            ref[...] = half[k % 3 + 1:k % 3 + 2].reshape(ref.shape)
    hid, d, mrows = reduce_ref.shape[0], expand_ref.shape[0], merge_ref.shape[0]
    reduce_ref[...] = from_ref[0:hid].astype(F32)
    expand_ref[...] = from_ref[hid:hid + d].astype(F32)
    merge_ref[...] = from_ref[hid + d:hid + d + mrows].astype(F32)
    for j in range(3):
        project_ref[j] = part_ref[j * d:(j + 1) * d].astype(F32)
    bias_ref[...] = part_ref[3 * d:3 * d + 8].astype(F32)[0:2]


def unpack(place, own, other, own_part, other_part, hid, mrows):
    d = own.shape[1]
    small_at = hid + d + mrows
    S = jax.ShapeDtypeStruct
    shapes = [S((2 * hid, d), F32), S((d, 2 * hid), F32), S((2 * mrows, d), F32)]
    shapes += [S((3, d, 2 * PAIR), F32), S((2, 2 * PAIR), F32)]

    def call(which, operands, in_specs, out_shape, out_specs, **more):
        rows = lambda r: pl.BlockSpec((r, d), lambda i, place: (place[0] ^ which, 0))
        blocks = [rows(hid), pl.BlockSpec((d, hid), lambda i, place: (0, place[0] ^ which)), rows(mrows)]
        blocks += [
            pl.BlockSpec((3, d, PAIR), lambda i, place: (0, 0, place[0] ^ which)),
            pl.BlockSpec((2, PAIR), lambda i, place: (0, place[0] ^ which)),
        ]
        return pl.pallas_call(
            functools.partial(unpack_kernel, small_at=small_at if which else None),
            grid_spec=pltpu.PrefetchScalarGridSpec(
                num_scalar_prefetch=1, grid=(1,), in_specs=in_specs, out_specs=blocks + out_specs,
            ),
            out_shape=out_shape,
            compiler_params=kernel_params(24),
            cost_estimate=cost(3),
            name="unpack%d" % which,
            **more,
        )(place, *operands)

    held = call(0, [own, own_part], [whole(own.shape), whole(own_part.shape)], shapes, [])
    one = lambda size: pl.BlockSpec((size,), lambda *_: (0,))
    hbm = pl.BlockSpec(memory_space=pl.ANY)
    return call(
        1,
        [other, other_part, own] + list(held),
        [whole(other.shape), whole(other_part.shape)]
        + [pl.BlockSpec((SMALL, d), lambda *_: (small_at // SMALL, 0))]
        + [hbm] * 5,
        shapes + [S((2 * hid,), F32)] + [S((d,), F32)] * 6,
        [one(2 * hid)] + [one(d)] * 6,
        input_output_aliases={4: 0, 5: 1, 6: 2, 7: 3, 8: 4},
    )


def by_bits(bits, pieces):
    v = jnp.stack(pieces)
    v = jnp.where(bits % 2 == 0, v, jnp.stack([v[1], v[0], v[3], v[2]]))
    v = jnp.where(bits // 2 == 0, v, jnp.stack([v[2], v[3], v[0], v[1]]))
    return v.reshape((-1,) + v.shape[2:])


def row_layer(
    inputs,
    pack_long,
    item_table,
    tau_table,
    delta_table,
    project_weight,
    project_bias,
    merge_weight,
    merge_bias,
    first_gain,
    first_shift,
    expand_weight,
    expand_bias,
    reduce_weight,
    reduce_bias,
    second_gain,
    second_shift,
    grad_output,
):
    n, d = inputs.shape
    hid = expand_weight.shape[1] // 2
    mrows = merge_weight.shape[0] // 2
    outer = lax.axis_size("outer")
    y_bit, z_bit = lax.axis_index("outer") % 2, lax.axis_index("outer") // 2 % 2
    project_half, place = prepare(project_weight, merge_weight, project_bias, expand_bias, n // LONG)
    project_near = flip(project_half, "tensor")
    rest_half = prepare_rest(place, expand_weight, reduce_weight)
    rest_near = flip(rest_half, "tensor")

    table = (place, pack_long, item_table, tau_table)
    q0, k0, v0, o0, r0, p0 = attend(
        *table, delta_table, inputs, project_weight, project_weight, project_bias, True
    )
    project_near, o0 = lax.optimization_barrier((project_near, o0))
    project_far = flip(project_near, "core")
    q1, k1, v1, o1, r1, p1, xh, rs = attend(
        *table, delta_table, inputs, project_near, project_far, project_near, False,
        o0, merge_weight, merge_bias[None],
    )
    rest_near, o1 = lax.optimization_barrier((rest_near, o1))
    rest_far = flip(rest_near, "core")
    block_output, grad_att, act, du, n1, dh2, dh1b, sums, sbe, send = feed(
        place, o0, o1, xh, rs, grad_output, merge_weight, project_near, project_far, expand_weight, reduce_weight,
        rest_near, rest_far, expand_bias[None], project_near,
        [v[None] for v in (first_gain, first_shift, reduce_bias, second_gain, second_shift)],
    )
    saved = ((q0, k0, v0, grad_att, o0, r0, p0), (q1, k1, v1, grad_att, o1, r1, p1))
    back = lambda x, *quarters: attend_back(*table, saved, x, quarters)

    got = flip(send, "core")
    keep = feed_grad(place, act, du, n1, dh2, dh1b, o0, o1, sums, sbe)
    got, keep = lax.optimization_barrier((got, keep))
    half = keep.shape[1] // 4
    a_x, a, b_y, b = combine(place, keep, got)
    x, a_x, b_y = lax.optimization_barrier((inputs, a_x, b_y))
    a_x, b_y = flip(a_x, "tensor"), flip(b_y, "outer", 1)
    d01, g01, d11, g11 = back(x, (0, 1), (1, 1))
    got01, got11 = flip(g01, "core"), flip(g11, "core")
    a_x, b_y, d11 = lax.optimization_barrier((a_x, b_y, d11))
    a, b = add_low(a, a_x), add_low(b, b_y)
    a_y, b_x = piece(a, 1 - y_bit, half), b[1]
    x, a_y, b_x = lax.optimization_barrier((x, a_y, b_x))
    a_y, b_x = flip(a_y, "outer", 1), flip(b_x, "tensor")
    d10, g10 = back(x, (1, 0))
    a_y, b_x, d10 = lax.optimization_barrier((a_y, b_x, d10))
    far = add_low(g10, got11)
    total = jnp.concatenate([add_low(piece(a, y_bit, half), a_y), add_low(b[0], b_x)])
    to_z = piece(total, 1 - z_bit, half)
    x, far, to_z = lax.optimization_barrier((x, far, to_z))
    far, to_z = flip(far, "tensor"), flip(to_z, "outer", 2)
    d00, g00 = back(x, (0, 0))
    far, to_z, d00 = lax.optimization_barrier((far, to_z, d00))
    feed_part = add_low(piece(total, z_bit, half), to_z)
    feed_part, g00 = lax.optimization_barrier((feed_part, g00))

    mine = add_low(g00, got01, far)
    rows = mine.shape[0] // 4
    to_y = flip(piece(mine, 1 - y_bit, 2 * rows), "outer", 1)
    came = flip(feed_part, "outer", 4)
    dx = functools.partial(input_grad, place, dh1b, project_weight, project_near, project_far)
    mine = add_low(piece(mine, y_bit, 2 * rows), to_y)
    to_z = piece(mine, 1 - z_bit, rows)
    d00, to_z, mine = lax.optimization_barrier((d00, to_z, mine))
    to_z = flip(to_z, "outer", 2)
    dx0 = dx((d00, d01, d10, d11), 0)
    to_z, came, dx0 = lax.optimization_barrier((to_z, came, dx0))
    project_part = add_low(piece(mine, z_bit, rows), to_z)
    feed_part = add_low(feed_part, came)
    project_part, feed_part, d00 = lax.optimization_barrier((project_part, feed_part, d00))
    came = flip(project_part, "outer", 4) if outer > 4 else jnp.zeros_like(project_part)
    by_y, by_z = flip(feed_part, "outer", 1), flip(feed_part, "outer", 2)
    dx1 = dx((d00, d01, d10, d11), 1, dx0)
    came, dx1, by_y, by_z = lax.optimization_barrier((came, dx1, by_y, by_z))
    mid = feed_part.shape[0] // 2
    cross = flip(by_z[:mid], "outer", 1), flip(by_y[mid:], "outer", 2)
    project_part = add_low(project_part, came)
    others = [flip(project_part, "outer", mask) for mask in (2, 1, 3)]
    cross, others = lax.optimization_barrier((cross, others))
    feed_pieces = [feed_part, by_y, by_z, jnp.concatenate(cross)]
    project_pieces = [project_part] + others
    total = by_bits(z_bit * 2 + y_bit, feed_pieces)
    project_total = by_bits(y_bit * 2 + z_bit, project_pieces)
    reduce_grad, expand_grad, merge_grad, project_grad, bias_grad, hidden, *small = unpack(
        place, total, flip(total, "core"), project_total, flip(project_total, "core"), hid, mrows
    )
    return (
        block_output,
        dx1,
        project_grad,
        bias_grad,
        merge_grad,
        *small[:3],
        expand_grad,
        hidden,
        reduce_grad,
        *small[3:],
    )


def rows_fit(mesh):
    size = mesh.shape["dp"]
    return mesh.shape["tensor"] == 2 and size in (8, 16)


def solution(mesh):
    if rows_fit(mesh):
        mesh = Mesh(mesh.devices.reshape(-1, 2, 2), ("outer", "core", "tensor"))
        body, dp = row_layer, ("outer", "core")
    else:
        body, dp = split_layer, ("dp",)
    all_ = P(dp + ("tensor",), None)
    placed = (
        all_,
        P(dp),
        P(dp),
        P(),
        P(),
        P(None, None, "tensor"),
        P(None, "tensor"),
        P("tensor", None),
        P(),
        P(),
        P(),
        P(None, "tensor"),
        P("tensor"),
        P("tensor", None),
        P(),
        P(),
        P(),
        all_,
    )
    return jax.shard_map(
        body,
        mesh=mesh,
        in_specs=placed,
        out_specs=(
            all_,
            all_,
            P(None, None, "tensor"),
            P(None, "tensor"),
            P("tensor", None),
            P(),
            P(),
            P(),
            P(None, "tensor"),
            P("tensor"),
            P("tensor", None),
            P(),
            P(),
            P(),
        ),
        check_vma=False,
    )
```
